128 devices in a mesh: section: 2 (over y_lo), dp: 16 (over z, x), seq: 4 (over y_hi, core).
Axes of the slice: x: 4, y: 4 (y_hi: 2, y_lo: 2; y = y_hi * 2 + y_lo), z: 4, core: 2. Of those that a mesh axis runs over, the one named last changes fastest.
Arguments:
- states: bfloat16 [2, 16, 1024, 1024], P('section', 'dp', 'seq'), may hold values from -6 to 6
- mirror: bfloat16 [2, 16, 1024, 1024], P('section', 'dp', 'seq'), may hold values from -6 to 6
- w_skip: bfloat16 [2048, 1024], replicated, may hold values from -0.125 to 0.125
- norm1_gain: bfloat16 [1024], replicated, may hold values from 0.099609375 to 1.8984375
- norm1_bias: bfloat16 [1024], replicated, may hold values from -1.5 to 1.5
- w_query: bfloat16 [1024, 1024], replicated, may hold values from -0.1875 to 0.1875
- w_key: bfloat16 [1024, 1024], replicated, may hold values from -0.1875 to 0.1875
- w_value: bfloat16 [1024, 1024], replicated, may hold values from -0.1875 to 0.1875
- w_out: bfloat16 [1024, 1024], replicated, may hold values from -0.75 to 0.75
- norm2_gain: bfloat16 [1024], replicated, may hold values from 0.099609375 to 1.8984375
- norm2_bias: bfloat16 [1024], replicated, may hold values from -1.5 to 1.5
- w_up: bfloat16 [1024, 4096], replicated, may hold values from -0.1875 to 0.1875
- w_down: bfloat16 [4096, 1024], replicated, may hold values from -0.09375 to 0.09375
- out_grad: bfloat16 [2, 16, 1024, 1024], P('section', 'dp', 'seq'), may hold values from -6 to 6
- lengths: int32 [2, 16, 4], P('section', 'dp'), may hold values from 1 to 896, as said below
- infill_spans: int32 [2, 16, 4, 2], P('section', 'dp'), may hold values from 0 to 896, as said below
Outputs:
- output: bfloat16 [2, 16, 1024, 1024], P('section', 'dp', 'seq')
- grad_states: bfloat16 [2, 16, 1024, 1024], P('section', 'dp', 'seq')
- grad_mirror: bfloat16 [2, 16, 1024, 1024], P('section', 'dp', 'seq')
- grad_w_skip: float32 [2, 2048, 1024], P('section', ('dp', 'seq'))
- grad_norm1_gain: float32 [2, 1024], P('section', ('dp', 'seq'))
- grad_norm1_bias: float32 [2, 1024], P('section', ('dp', 'seq'))
- grad_w_query: float32 [2, 1024, 1024], P('section', ('dp', 'seq'))
- grad_w_key: float32 [2, 1024, 1024], P('section', ('dp', 'seq'))
- grad_w_value: float32 [2, 1024, 1024], P('section', ('dp', 'seq'))
- grad_w_out: float32 [2, 1024, 1024], P('section', ('dp', 'seq'))
- grad_norm2_gain: float32 [2, 1024], P('section', ('dp', 'seq'))
- grad_norm2_bias: float32 [2, 1024], P('section', ('dp', 'seq'))
- grad_w_up: float32 [2, 1024, 4096], P('section', ('dp', 'seq'))
- grad_w_down: float32 [2, 4096, 1024], P('section', ('dp', 'seq'))
The draws below stay inside these ranges and needn't reach their ends.
Inputs may be any that keep to these rules, and one draw needn't show every extreme that they name: Per packed row, 4 utterance lengths that sum to 1024; one of them is exactly 896. `infill_spans`: per utterance, offsets start < end within it whose span covers up to 100 percent of its frames (at least one frame).
All inputs are finite; a program needn't handle non-finite values.
Results may differ from the reference program's by a relative error of at most 0.019.
Values may be sent and summed in bfloat16 or wider, within the bound.
A program may use at most 256 MiB of HBM per device.

```python
import jax
import jax.numpy as jnp
from jax import lax

D = 1024
HEADS = 16
FF = 4096
HEAD_DIM = 64
NUTT = 4
ROW = 1024
MOST = 896
ROWS = 16
MICRO = 2


def shared_lengths(key):
    total_rows = MICRO * ROWS
    long_slot = jax.random.randint(jax.random.fold_in(key, 11), (total_rows,), 0, NUTT)
    weights = jax.random.randint(jax.random.fold_in(key, 12), (total_rows, NUTT), 1, 5)
    short_total = ROW - MOST
    spare = short_total - (NUTT - 1)
    is_long = jnp.arange(NUTT)[None, :] == long_slot[:, None]
    weights = jnp.where(is_long, 0, weights)
    share = 1 + spare * weights // jnp.sum(weights, axis=1, keepdims=True)
    share = jnp.where(is_long, 0, share)
    leftover = short_total - jnp.sum(share, axis=1, keepdims=True)
    first_short = jnp.where(long_slot == 0, 1, 0)
    add_here = jnp.arange(NUTT)[None, :] == first_short[:, None]
    share = share + jnp.where(add_here, leftover, 0)
    lengths = jnp.where(is_long, MOST, share)
    return lengths.reshape(MICRO, ROWS, NUTT).astype(jnp.int32)


def draw_lengths(key, part):
    return shared_lengths(key)


def draw_infill_spans(key, part):
    lengths = shared_lengths(key)
    key = jax.random.fold_in(key, 5)
    percent = jax.random.randint(jax.random.fold_in(key, 1), lengths.shape, 70, 101)
    span_size = jnp.maximum(1, lengths * percent // 100)
    room = lengths - span_size + 1
    offset = jax.random.randint(jax.random.fold_in(key, 2), lengths.shape, 0, 1 << 20) % room
    is_long = lengths == MOST
    offset = jnp.where(is_long, lengths - span_size, offset)
    return jnp.stack([offset, offset + span_size], axis=-1).astype(jnp.int32)


def block_scale(key, extent, pieces, least, largest):
    loudness, own = 1.0, jax.random.fold_in(key, 6)
    for position, shards_of in pieces:
        heights = jnp.exp(jax.random.uniform(jax.random.fold_in(own, position), (shards_of,), jnp.float32, least / len(pieces), largest / len(pieces)))
        loudness = loudness * jnp.repeat(heights, extent[position] // shards_of).reshape([-1 if axis == position else 1 for axis in range(len(extent))])
    return loudness


def scatter_about(key, shape, scale, bound, cuts=(), kind=jnp.bfloat16):
    loudness = block_scale(key, shape, cuts, -0.22, 0.18) if cuts else 1.0
    drawn = jax.random.normal(key, shape, jnp.float32) * scale * loudness
    return jnp.minimum(jnp.maximum(drawn, -bound), bound).astype(kind)


def setup_inputs(seed: int = 0) -> dict:
    arg_keys = jax.random.split(jax.random.key(seed), 17)
    states = scatter_about(arg_keys[0], (MICRO, ROWS, ROW, D), 1.0, 6.0, ((0, 2), (1, 16), (2, 4)))
    mirror = scatter_about(arg_keys[1], (MICRO, ROWS, ROW, D), 1.0, 6.0, ((0, 2), (1, 16), (2, 4)))
    w_skip = scatter_about(arg_keys[2], (2 * D, D), (2 * D) ** -0.5, 0.125)
    norm1_gain = jnp.clip(1.0 + 0.18 * jax.random.normal(arg_keys[3], (D,), jnp.float32), 0.099609375, 1.8984375).astype(jnp.bfloat16)
    norm1_bias = scatter_about(arg_keys[4], (D,), 0.3, 1.5)
    w_query = scatter_about(arg_keys[5], (D, D), D ** -0.5, 0.1875)
    w_key = scatter_about(arg_keys[6], (D, D), D ** -0.5, 0.1875)
    w_value = scatter_about(arg_keys[7], (D, D), D ** -0.5, 0.1875)
    w_out = scatter_about(arg_keys[8], (D, D), (D // 16) ** -0.5, 0.75)
    norm2_gain = jnp.clip(1.0 + 0.18 * jax.random.normal(arg_keys[9], (D,), jnp.float32), 0.099609375, 1.8984375).astype(jnp.bfloat16)
    norm2_bias = scatter_about(arg_keys[10], (D,), 0.3, 1.5)
    w_up = scatter_about(arg_keys[11], (D, FF), D ** -0.5, 0.1875)
    w_down = scatter_about(arg_keys[12], (FF, D), FF ** -0.5, 0.09375)
    out_grad = scatter_about(arg_keys[13], (MICRO, ROWS, ROW, D), 1.0, 6.0, ((0, 2), (1, 16), (2, 4)))
    lengths = draw_lengths(jax.random.fold_in(arg_keys[16], 71), 0)
    infill_spans = draw_infill_spans(jax.random.fold_in(arg_keys[16], 71), 0)
    return {"states": states, "mirror": mirror, "w_skip": w_skip, "norm1_gain": norm1_gain, "norm1_bias": norm1_bias, "w_query": w_query, "w_key": w_key, "w_value": w_value, "w_out": w_out, "norm2_gain": norm2_gain, "norm2_bias": norm2_bias, "w_up": w_up, "w_down": w_down, "out_grad": out_grad, "lengths": lengths, "infill_spans": infill_spans}


@jax.custom_vjp
def low(v):
    return lax.optimization_barrier(v.astype(jnp.bfloat16)).astype(jnp.float32)

@jax.custom_vjp
def low_back(v):
    return v

def low_keep(v):
    return (low(v), None)

def low_pass(kept, grad):
    return (grad,)

def back_keep(v):
    return (v, None)

def back_low(kept, grad):
    return (low(grad),)
low.defvjp(low_keep, low_pass)
low_back.defvjp(back_keep, back_low)
EPS = 1e-05
HIGHEST = lax.Precision.HIGHEST

def matmul_high(left, right):
    return jnp.dot(left, right, precision=HIGHEST, preferred_element_type=jnp.float32)

def layer_norm(hidden, gain, bias):
    center = hidden - lax.optimization_barrier(jnp.mean(hidden, axis=-1, keepdims=True))
    variance = lax.optimization_barrier(jnp.mean(center * center, axis=-1, keepdims=True))
    return center * lax.rsqrt(variance + EPS) * gain + bias

def row_tables(lengths_row, spans_row):
    ends = jnp.cumsum(lengths_row, dtype=jnp.int32)
    starts = ends - lengths_row
    places = jnp.arange(ROW, dtype=jnp.int32)
    segment = lax.optimization_barrier(jnp.sum((places[:, None] >= ends[None, :]).astype(jnp.int32), axis=1))
    lower = starts + spans_row[:, 0]
    upper = starts + spans_row[:, 1]
    inside = jnp.any((places[:, None] >= lower[None, :]) & (places[:, None] < upper[None, :]), axis=1)
    return (places, segment, inside)

def forward(params, states_row, skip_row, places, segment):
    w_skip, gain_one, bias_one, w_query, w_key, w_value, w_out, gain_two, bias_two, w_up, w_down = params
    joined = low_back(jnp.concatenate([states_row, skip_row], axis=1))
    hidden = low_back(matmul_high(joined, w_skip))
    normed = low(layer_norm(hidden, gain_one, bias_one))
    query = low_back(low(matmul_high(normed, w_query))).reshape(ROW, HEADS, HEAD_DIM)
    keys = low_back(low(matmul_high(normed, w_key))).reshape(ROW, HEADS, HEAD_DIM)
    values = low_back(low(matmul_high(normed, w_value))).reshape(ROW, HEADS, HEAD_DIM)
    slopes = 2.0 ** (-8.0 * (jnp.arange(HEADS, dtype=jnp.float32) + 1.0) / HEADS)
    distance = jnp.abs(places[:, None] - places[None, :]).astype(jnp.float32)
    same_utt = segment[:, None] == segment[None, :]
    raw = jnp.einsum('qhd,khd->hqk', query, keys, precision=HIGHEST)
    scores = raw * HEAD_DIM ** (-0.5) - slopes[:, None, None] * distance[None]
    scores = low_back(jnp.where(same_utt[None], scores, -1e+30))
    attention = low(jax.nn.softmax(scores, axis=-1))
    mixed_rows = jnp.einsum('hqk,khd->qhd', attention, values, precision=HIGHEST).reshape(ROW, D)
    mixed_rows = low_back(low(mixed_rows))
    residual = hidden + low_back(matmul_high(mixed_rows, w_out))
    normed_two = low(layer_norm(residual, gain_two, bias_two))
    upward = low_back(matmul_high(normed_two, w_up))
    activated = low(jax.nn.gelu(upward, approximate=False))
    return residual + low_back(matmul_high(activated, w_down))

def reference(states, mirror, w_skip, norm1_gain, norm1_bias, w_query, w_key, w_value, w_out, norm2_gain, norm2_bias, w_up, w_down, out_grad, lengths, infill_spans):
    params = tuple((weight.astype(jnp.float32) for weight in (w_skip, norm1_gain, norm1_bias, w_query, w_key, w_value, w_out, norm2_gain, norm2_bias, w_up, w_down)))

    def one_row(sums_so_far, row_data):
        states_row, skip_row, grad_row, lengths_row, spans_row = row_data
        places, segment, inside = row_tables(lengths_row, spans_row)

        def closed(param_set, first_input, second_input):
            return forward(param_set, first_input, second_input, places, segment)
        layer_out, pullback = jax.vjp(closed, params, states_row.astype(jnp.float32), skip_row.astype(jnp.float32))
        masked = grad_row.astype(jnp.float32) * inside[:, None].astype(jnp.float32)
        grads, grad_states_row, grad_skip_row = pullback(masked)
        sums_so_far = jax.tree.map(jnp.add, sums_so_far, grads)
        return (sums_so_far, (layer_out.astype(jnp.bfloat16), grad_states_row.astype(jnp.bfloat16), grad_skip_row.astype(jnp.bfloat16)))
    outputs, input_grads, skip_grads, param_grads = ([], [], [], [])
    for section_index in range(MICRO):
        partner_index = MICRO - 1 - section_index
        zero_sums = jax.tree.map(jnp.zeros_like, params)
        param_sums, stacked = lax.scan(one_row, zero_sums, (states[section_index], mirror[partner_index], out_grad[section_index], lengths[section_index], infill_spans[section_index]))
        outputs.append(stacked[0])
        input_grads.append(stacked[1])
        skip_grads.append(stacked[2])
        param_grads.append(param_sums)
    grad_mirror = jnp.stack(skip_grads[::-1])
    gathered = [jnp.stack([grads[index] for grads in param_grads]) for index in range(11)]
    return (jnp.stack(outputs), jnp.stack(input_grads), grad_mirror, gathered[0], gathered[1], gathered[2], gathered[3], gathered[4], gathered[5], gathered[6], gathered[7], gathered[8], gathered[9], gathered[10])
```

```python
import jax
import jax.numpy as jnp
import numpy as np
from jax import lax
from jax.sharding import PartitionSpec as P

HEADS = 16


EPS = 1e-05


def from_partner(value, axis, stride):
    mask = 2**stride
    pairs = [(source, source ^ mask) for source in range(lax.axis_size(axis))]
    return lax.ppermute(value, axis, pairs)


def project(left, right):
    return jnp.dot(left, right, preferred_element_type=jnp.float32)


def rows_product(left, right):
    return lax.dot_general(
        left, right, (((0,), (0,)), ((), ())), preferred_element_type=jnp.float32
    )


def back_product(left, right):
    return lax.dot_general(
        left, right, (((1,), (1,)), ((), ())), preferred_element_type=jnp.float32
    )


def gelu_exact(values):
    return jax.nn.gelu(values, approximate=False)


def norm_forward(hidden, gain, bias):
    center = hidden - jnp.mean(hidden, axis=-1, keepdims=True)
    variance = jnp.mean(center * center, axis=-1, keepdims=True)
    inverse = lax.rsqrt(variance + EPS)
    unit = center * inverse
    return (unit * gain + bias, unit, inverse)


def norm_backward(grad, unit, inverse, gain):
    scaled = grad * gain
    mean_one = jnp.mean(scaled, axis=-1, keepdims=True)
    mean_two = jnp.mean(scaled * unit, axis=-1, keepdims=True)
    grad_input = inverse * (scaled - mean_one - unit * mean_two)
    return (grad_input, jnp.sum(grad * unit, axis=0), jnp.sum(grad, axis=0))


def segment_tables(lengths_row, spans_row, places):
    ends = jnp.cumsum(lengths_row, dtype=jnp.int32)
    starts = ends - lengths_row
    segment = jnp.sum((places[:, None] >= ends[None, :]).astype(jnp.int32), axis=1)
    lower = starts + spans_row[:, 0]
    upper = starts + spans_row[:, 1]
    inside = jnp.any(
        (places[:, None] >= lower[None, :]) & (places[:, None] < upper[None, :]), axis=1
    )
    return (segment, inside)


ORDER_NEAR = (0, 3, 1, 2)
ORDER_WRAP = (0, 1, 3, 2)
QUARTERS = (("x", ORDER_NEAR), ("x", ORDER_WRAP), ("z", ORDER_NEAR), ("z", ORDER_WRAP))


def partner_of(value, axis, mask):
    pairs = [(source, source ^ mask) for source in range(lax.axis_size(axis))]
    return lax.ppermute(value, axis, pairs)


def quarter_masks(quarter):
    first, order = QUARTERS[quarter]
    ring = (1, 3) if order == ORDER_NEAR else (3, 1)
    x_masks = [("dp", mask) for mask in ring]
    z_masks = [("dp", mask * 4) for mask in ring]
    return x_masks + z_masks if first == "x" else z_masks + x_masks


def relative_blocks():
    shards, quarters = [], []
    for core in range(2):
        for quarter, (first, order) in enumerate(QUARTERS):
            for outer in order:
                for inner in order:
                    for high in range(2):
                        x, z = (outer, inner) if first == "x" else (inner, outer)
                        shards.append(z * 16 + x * 4 + high * 2 + core)
                        quarters.append(quarter)
    return np.asarray(shards, np.int32), np.asarray(quarters, np.int32)


def relative_rows(shard, rows):
    shards, quarters = relative_blocks()
    piece = rows // 256
    inner = np.arange(piece, dtype=np.int32)
    fixed = quarters[:, None] * piece + inner[None, :]
    return (((jnp.asarray(shards) ^ shard)[:, None] * (4 * piece)) + fixed).reshape(-1)


def selector(shard, rows):
    source = relative_rows(shard, rows)
    return (source[:, None] == jnp.arange(rows, dtype=jnp.int32)[None, :]).astype(jnp.bfloat16)


def reduce_rows(value):
    rows = value.shape[0] // 4
    kept = []
    for quarter in range(4):
        piece = value[quarter * rows : (quarter + 1) * rows]
        for axis, mask in quarter_masks(quarter):
            half = piece.shape[0] // 2
            other = partner_of(piece[half:], axis, mask)
            piece = (piece[:half].astype(jnp.float32) + other.astype(jnp.float32)).astype(
                jnp.bfloat16
            )
        kept.append(piece)
    half = kept[0].shape[0] // 2
    other = partner_of(jnp.concatenate([piece[half:] for piece in kept], axis=0), "seq", 2)
    mine = jnp.concatenate([piece[:half] for piece in kept], axis=0)
    return mine.astype(jnp.float32) + other.astype(jnp.float32)


def swap_core(value):
    return partner_of(value, "seq", 1)


def low(value):
    return value.astype(jnp.bfloat16)


def pair_product(kept, swapped, grad, grad_swapped):
    left = jnp.concatenate([kept, swapped], axis=1)
    right = jnp.concatenate([grad, grad_swapped], axis=0)
    return low(project(left, right))


def on_device(
    states,
    mirror,
    w_skip,
    norm1_gain,
    norm1_bias,
    w_query,
    w_key,
    w_value,
    w_out,
    norm2_gain,
    norm2_bias,
    w_up,
    w_down,
    out_grad,
    lengths,
    infill_spans,
):
    rows_here = states.shape[2]
    model_width = states.shape[3]
    head_count = HEADS
    head_dim = model_width // head_count
    score_scale = head_dim ** (-0.5)
    seq = lax.axis_index("seq")
    shard = lax.axis_index("dp") * 4 + seq
    own_rows = states.reshape(rows_here, model_width)
    stored = mirror.reshape(rows_here, model_width)
    partner = from_partner(stored, "section", 0)
    lengths_row = lengths.reshape(-1)
    spans_row = infill_spans.reshape(-1, 2)
    row_length = rows_here * lax.axis_size("seq")
    local = jnp.arange(rows_here, dtype=jnp.int32)
    query_place = seq * rows_here + local
    key_place = jnp.concatenate([(seq ^ step) * rows_here + local for step in range(4)])
    query_segment, inside = segment_tables(lengths_row, spans_row, query_place)
    key_segment = segment_tables(lengths_row, spans_row, key_place)[0]
    allowed = query_segment[:, None] == key_segment[None, :]
    distance = jnp.abs(query_place[:, None] - key_place[None, :]).astype(jnp.float32)
    slopes = 2.0 ** (-8.0 * (jnp.arange(head_count, dtype=jnp.float32) + 1.0) / head_count)
    gain_one = norm1_gain.astype(jnp.float32)
    bias_one = norm1_bias.astype(jnp.float32)
    gain_two = norm2_gain.astype(jnp.float32)
    bias_two = norm2_bias.astype(jnp.float32)
    w_first = w_skip[:model_width]
    w_second = w_skip[model_width:]
    select = selector(shard, model_width)
    half = model_width // 2

    grad_rows = (
        out_grad.reshape(rows_here, model_width).astype(jnp.float32)
        * inside.astype(jnp.float32)[:, None]
    )
    grad_low = low(grad_rows)
    grad_low_other = swap_core(grad_low)
    hidden = project(own_rows, w_first) + project(partner, w_second)
    normed_one, unit_one, inverse_one = norm_forward(hidden, gain_one, bias_one)
    normed_one = low(normed_one)
    far = partner_of(normed_one, "seq", 2)
    near = swap_core(normed_one)
    far_near = swap_core(far)
    normed_all = jnp.concatenate([normed_one, near, far, far_near], axis=0)
    query = low(project(normed_one, w_query))
    keys_all = low(project(normed_all, w_key))
    values_all = low(project(normed_all, w_value))
    query3 = query.reshape(rows_here, head_count, head_dim)
    keys3 = keys_all.reshape(row_length, head_count, head_dim)
    values3 = values_all.reshape(row_length, head_count, head_dim)

    def scores_of():
        raw = jnp.einsum("qhd,khd->hqk", query3, keys3, preferred_element_type=jnp.float32)
        scores = raw * score_scale - slopes[:, None, None] * distance[None]
        return jnp.where(allowed[None], scores, -1e30)

    scores = scores_of()
    row_top = jnp.max(scores, axis=-1, keepdims=True)
    exponent = jnp.exp(scores - row_top)
    row_total = jnp.sum(exponent, axis=-1, keepdims=True)
    log_total = row_top + jnp.log(row_total)
    softmax_low = (exponent / row_total).astype(jnp.bfloat16)
    mixed_rows = jnp.einsum(
        "hqk,khd->qhd", softmax_low, values3, preferred_element_type=jnp.float32
    )
    mixed_rows = low(mixed_rows.reshape(rows_here, model_width))
    residual = hidden + project(mixed_rows, w_out)
    normed_two, unit_two, inverse_two = norm_forward(residual, gain_two, bias_two)
    normed_two = low(normed_two)
    upward = project(normed_two, w_up)
    activated, gelu_pull = jax.vjp(gelu_exact, upward)
    act_low = low(activated)
    result = residual + project(act_low, w_down)
    output = low(result).reshape(states.shape)
    grad_act = back_product(grad_low, w_down)
    grad_upward = low(gelu_pull(grad_act)[0])
    grad_upward_other = swap_core(grad_upward)

    hidden_width = act_low.shape[1]
    piece = hidden_width // 256
    shards, quarters = relative_blocks()
    act_rows = act_low.T.reshape(256, piece, rows_here)
    act_rows = act_rows[(jnp.asarray(shards) ^ shard) * 4 + jnp.asarray(quarters)]
    act_rows = act_rows.reshape(2, hidden_width // 2, rows_here)
    act_other = swap_core(act_rows[1])
    down_sum = reduce_rows(pair_product(act_rows[0], act_other, grad_low, grad_low_other))

    two_rows = low(back_product(select, normed_two))
    two_other = swap_core(two_rows[half:])
    up_sum = reduce_rows(pair_product(two_rows[:half], two_other, grad_upward, grad_upward_other))

    grad_normed_two = back_product(grad_upward, w_up)
    grad_resid_norm, grad_gain_two, grad_bias_two = norm_backward(
        grad_normed_two, unit_two, inverse_two, gain_two
    )
    grad_residual = grad_rows + grad_resid_norm
    grad_attn = low(grad_residual)
    grad_attn_other = swap_core(grad_attn)
    mixed_cut = low(back_product(select, mixed_rows))
    mixed_other = swap_core(mixed_cut[half:])
    out_sum = reduce_rows(pair_product(mixed_cut[:half], mixed_other, grad_attn, grad_attn_other))

    grad_mixed = low(back_product(grad_attn, w_out))
    grad_mixed3 = grad_mixed.reshape(rows_here, head_count, head_dim)
    softmax_again = jnp.exp(scores_of() - log_total)
    grad_softmax = jnp.einsum(
        "qhd,khd->hqk", grad_mixed3, values3, preferred_element_type=jnp.float32
    )
    centre = jnp.sum(softmax_again * grad_softmax, axis=-1, keepdims=True)
    grad_scores = (softmax_again * (grad_softmax - centre)).astype(jnp.bfloat16)
    grad_query = (
        jnp.einsum("hqk,khd->qhd", grad_scores, keys3, preferred_element_type=jnp.float32)
        * score_scale
    )
    grad_query = low(grad_query.reshape(rows_here, model_width))
    key_part = (
        jnp.einsum("hqk,qhd->khd", grad_scores, query3, preferred_element_type=jnp.float32)
        * score_scale
    )
    value_part = jnp.einsum(
        "hqk,qhd->khd",
        softmax_again.astype(jnp.bfloat16),
        grad_mixed3,
        preferred_element_type=jnp.float32,
    )
    both_part = low(
        jnp.concatenate(
            [
                key_part.reshape(row_length, model_width),
                value_part.reshape(row_length, model_width),
            ],
            axis=1,
        )
    ).reshape(4, rows_here, 2 * model_width)
    both_other = swap_core(jnp.concatenate([both_part[1], both_part[3]], axis=0))
    both_mine = low(
        jnp.concatenate([both_part[0], both_part[2]], axis=0).astype(jnp.float32)
        + both_other.astype(jnp.float32)
    )
    both_far = swap_core(both_mine)
    grad_query_other = swap_core(grad_query)
    w_both = jnp.concatenate([w_key, w_value], axis=1)
    normed_part = back_product(both_mine, w_both)
    normed_far = partner_of(low(normed_part[rows_here:]), "seq", 2)
    grad_normed_one = (
        back_product(grad_query, w_query)
        + normed_part[:rows_here]
        + normed_far.astype(jnp.float32)
    )
    one_rows = low(back_product(select[:half], normed_all))
    query_share = low(
        project(one_rows[:, : 2 * rows_here], jnp.concatenate([grad_query, grad_query_other], axis=0))
    )
    both_rows = jnp.concatenate(
        [both_mine[:rows_here], both_far[:rows_here], both_mine[rows_here:], both_far[rows_here:]],
        axis=0,
    )
    both_share = low(project(one_rows, both_rows))
    query_sum = reduce_rows(query_share)
    both_sum = reduce_rows(both_share)

    grad_hidden_norm, grad_gain_one, grad_bias_one = norm_backward(
        grad_normed_one, unit_one, inverse_one, gain_one
    )
    grad_hidden = low(grad_residual + grad_hidden_norm)
    grad_hidden_other = swap_core(grad_hidden)
    grad_partner = low(back_product(grad_hidden, w_second))
    grad_stored = from_partner(grad_partner, "section", 0)
    grad_own = low(back_product(grad_hidden, w_first))
    select_joined = selector(shard, 2 * model_width)
    joined = jnp.concatenate([own_rows, partner], axis=1)
    joined_rows = low(back_product(select_joined, joined))
    joined_other = swap_core(joined_rows[model_width:])
    skip_sum = reduce_rows(
        pair_product(joined_rows[:model_width], joined_other, grad_hidden, grad_hidden_other)
    )

    sums = jnp.stack([grad_gain_one, grad_bias_one, grad_gain_two, grad_bias_two])
    for axis, mask in (("seq", 1), ("dp", 1), ("dp", 3), ("dp", 4), ("dp", 12), ("seq", 2)):
        sums = sums + partner_of(sums, axis, mask)
    sums = lax.dynamic_slice_in_dim(sums, shard * (model_width // 64), model_width // 64, axis=1)
    return (
        output,
        grad_own.reshape(states.shape),
        grad_stored.reshape(states.shape),
        skip_sum[None],
        sums[0][None],
        sums[1][None],
        query_sum[None],
        both_sum[None, :, :model_width],
        both_sum[None, :, model_width:],
        out_sum[None],
        sums[2][None],
        sums[3][None],
        up_sum[None],
        down_sum[None],
    )


def solution(mesh):
    in_specs = (
        P("section", "dp", "seq", None),
        P("section", "dp", "seq", None),
        P(),
        P(),
        P(),
        P(),
        P(),
        P(),
        P(),
        P(),
        P(),
        P(),
        P(),
        P("section", "dp", "seq", None),
        P("section", "dp", None),
        P("section", "dp", None, None),
    )
    out_specs = (
        P("section", "dp", "seq", None),
        P("section", "dp", "seq", None),
        P("section", "dp", "seq", None),
        P("section", ("dp", "seq"), None),
        P("section", ("dp", "seq")),
        P("section", ("dp", "seq")),
        P("section", ("dp", "seq"), None),
        P("section", ("dp", "seq"), None),
        P("section", ("dp", "seq"), None),
        P("section", ("dp", "seq"), None),
        P("section", ("dp", "seq")),
        P("section", ("dp", "seq")),
        P("section", ("dp", "seq"), None),
        P("section", ("dp", "seq"), None),
    )
    return jax.shard_map(
        on_device, mesh=mesh, in_specs=in_specs, out_specs=out_specs, check_vma=False
    )
```

```python
import functools

import jax
import jax.numpy as jnp
from jax.experimental import pallas as pl
from jax.experimental.pallas import tpu as pltpu
from jax import lax
from jax.sharding import PartitionSpec as P

HEADS = 16


EPS = 1e-05


def from_partner(value, axis, stride):
    mask = 2**stride
    pairs = [(source, source ^ mask) for source in range(lax.axis_size(axis))]
    return lax.ppermute(value, axis, pairs)


def project(left, right):
    return jnp.dot(left, right, preferred_element_type=jnp.float32)


def rows_product(left, right):
    return lax.dot_general(
        left, right, (((0,), (0,)), ((), ())), preferred_element_type=jnp.float32
    )


def back_product(left, right):
    return lax.dot_general(
        left, right, (((1,), (1,)), ((), ())), preferred_element_type=jnp.float32
    )


def gelu_exact(values):
    return jax.nn.gelu(values, approximate=False)


def norm_forward(hidden, gain, bias):
    center = hidden - jnp.mean(hidden, axis=-1, keepdims=True)
    variance = jnp.mean(center * center, axis=-1, keepdims=True)
    inverse = lax.rsqrt(variance + EPS)
    unit = center * inverse
    return (unit * gain + bias, unit, inverse)


def norm_backward(grad, unit, inverse, gain):
    scaled = grad * gain
    mean_one = jnp.mean(scaled, axis=-1, keepdims=True)
    mean_two = jnp.mean(scaled * unit, axis=-1, keepdims=True)
    grad_input = inverse * (scaled - mean_one - unit * mean_two)
    return (grad_input, jnp.sum(grad * unit, axis=0), jnp.sum(grad, axis=0))


def segment_tables(lengths_row, spans_row, places):
    ends = jnp.cumsum(lengths_row, dtype=jnp.int32)
    starts = ends - lengths_row
    segment = jnp.sum((places[:, None] >= ends[None, :]).astype(jnp.int32), axis=1)
    lower = starts + spans_row[:, 0]
    upper = starts + spans_row[:, 1]
    inside = jnp.any(
        (places[:, None] >= lower[None, :]) & (places[:, None] < upper[None, :]), axis=1
    )
    return (segment, inside)


def partner_of(value, axis, mask):
    pairs = [(source, source ^ mask) for source in range(lax.axis_size(axis))]
    return lax.ppermute(value, axis, pairs)


def core_selector(core, rows):
    piece = rows // 64
    target = jnp.arange(rows // 2, dtype=jnp.int32)
    source = (target // piece) * (2 * piece) + core * piece + target % piece
    return (source[:, None] == jnp.arange(rows, dtype=jnp.int32)[None, :]).astype(jnp.bfloat16)


def swap_core(value):
    return partner_of(value, "seq", 1)


def low(value):
    return value.astype(jnp.bfloat16)


def pair_product(kept, swapped, grad, grad_swapped):
    left = jnp.concatenate([kept, swapped], axis=1)
    right = jnp.concatenate([grad, grad_swapped], axis=0)
    return by_dp(low(project(left, right)))


def by_dp(value):
    return value.reshape(16, value.shape[0] // 16, value.shape[1])


MESH = pl.DeviceIdType.MESH
NEAR, WRAP = (0, 3, 1, 2), (0, 1, 3, 2)
QUARTERS = (("x", NEAR), ("x", WRAP), ("z", NEAR), ("z", WRAP))


def flip(value, mask):
    if mask == 1:
        return value + 1 - 2 * lax.rem(value, 2)
    if mask == 2:
        return lax.rem(value + 2, 4)
    if mask == 3:
        return 3 - value
    return value


def block_place(quarter, outer, inner, x, z):
    first, order = QUARTERS[quarter]
    if first == "x":
        return flip(z, order[inner]) * 4 + flip(x, order[outer])
    return flip(z, order[outer]) * 4 + flip(x, order[inner])


def stage_partner(quarter, stage, x, z, seq):
    if stage == 4:
        return {"seq": lax.rem(seq + 2, 4)}
    first, order = QUARTERS[quarter]
    mask = order[2] if stage % 2 == 0 else order[1]
    if (first == "x") == (stage < 2):
        return {"dp": z * 4 + flip(x, mask)}
    return {"dp": flip(z, mask) * 4 + x}


def remote(source, target, send, recv, device):
    return pltpu.make_async_remote_copy(
        src_ref=source,
        dst_ref=target,
        send_sem=send,
        recv_sem=recv,
        device_id=device,
        device_id_type=MESH,
    )


def enter(devices):
    barrier = pltpu.get_barrier_semaphore()
    for device in devices:
        pl.semaphore_signal(barrier, inc=1, device_id=device, device_id_type=MESH)
    pl.semaphore_wait(barrier, len(devices))


def add_blocks(count, total, other):
    def one(index, carry):
        total[index] = (
            total[index].astype(jnp.float32) + other[index].astype(jnp.float32)
        ).astype(jnp.bfloat16)
        return carry

    lax.fori_loop(0, count, one, 0)


def reduce_kernel(shapes, with_vectors, *refs):
    count = len(shapes)
    refs = list(refs)
    take = lambda n: [refs.pop(0) for _ in range(n)]
    sources = take(count)
    vector = take(1)[0] if with_vectors else None
    results = take(count)
    vector_result = take(1)[0] if with_vectors else None
    totals = take(count)
    landings = [take(5) for _ in range(count)]
    local_sem, send_sem, recv_sem = take(3)
    if with_vectors:
        vector_total, vector_landing, vector_send, vector_recv = take(4)

    dp, seq = lax.axis_index("dp"), lax.axis_index("seq")
    z, x = lax.div(dp, 4), lax.rem(dp, 4)
    y = lax.div(seq, 2)
    partners = [stage_partner(0, 0, x, z, seq), stage_partner(0, 1, x, z, seq)]
    partners += [stage_partner(2, 0, x, z, seq), stage_partner(2, 1, x, z, seq)]
    partners += [stage_partner(0, 4, x, z, seq)]
    core = {"seq": flip(seq, 1)}
    if with_vectors:
        partners += [core]
    enter(partners)

    vector_stages = [(core, 0, 0, 16)]
    if with_vectors:
        vector_stages += [(stage_partner(0, 0, x, z, seq), 8, 16, 8)]
        vector_stages += [(stage_partner(0, 1, x, z, seq), 4, 24, 4)]
        vector_stages += [(stage_partner(0, 2, x, z, seq), 2, 28, 2)]
        vector_stages += [(stage_partner(0, 3, x, z, seq), 1, 30, 1)]
        vector_stages += [(stage_partner(0, 4, x, z, seq), 0, 31, 1)]

    def vector_copy(step):
        device, first, landing, size = vector_stages[step]
        return remote(
            vector_total.at[pl.ds(first, size)],
            vector_landing.at[pl.ds(landing, size)],
            vector_send.at[step],
            vector_recv.at[step],
            device,
        )

    def vector_finish(step):
        _, _, landing, size = vector_stages[step]
        copy = vector_copy(step)
        copy.wait()
        vector_total[pl.ds(0, size)] += vector_landing[pl.ds(landing, size)]

    if with_vectors:
        for index in range(16):
            outer, inner = index // 4, index % 4
            vector_total[index] = vector[block_place(0, outer, inner, x, z)]
        vector_copy(0).start()

    def first_blocks(job, quarter):
        rows, width = shapes[job]
        columns = pl.ds(quarter * (width // 4), width // 4)
        for index in range(8):
            outer, inner = index // 4, index % 4
            there = block_place(quarter, outer + 2, inner, x, z)
            here = block_place(quarter, outer, inner, x, z)
            remote(
                sources[job].at[there, :, columns],
                landings[job][0].at[quarter, index],
                send_sem.at[job, quarter, 0],
                recv_sem.at[job, quarter, 0],
                stage_partner(quarter, 0, x, z, seq),
            ).start()
            pltpu.make_async_copy(
                sources[job].at[here, :, columns],
                totals[job].at[quarter, index],
                local_sem.at[job, quarter],
            ).start()

    def stage_copy(job, quarter, stage):
        rows, width = shapes[job]
        if stage == 0:
            source = landings[job][0].at[quarter]
            target = landings[job][0].at[quarter]
        elif stage < 4:
            size = 8 >> stage
            source = totals[job].at[quarter, pl.ds(size, size)]
            target = landings[job][stage].at[quarter]
        else:
            away = pl.multiple_of((1 - y) * rows, 16)
            source = totals[job].at[quarter, 0, pl.ds(away, rows)]
            target = landings[job][4].at[quarter]
        return remote(
            source,
            target,
            send_sem.at[job, quarter, stage],
            recv_sem.at[job, quarter, stage],
            stage_partner(quarter, stage, x, z, seq),
        )

    def finish(job, quarter, stage):
        rows, width = shapes[job]
        stage_copy(job, quarter, stage).wait_recv()
        if stage == 0:
            pltpu.make_async_copy(
                totals[job].at[quarter], totals[job].at[quarter], local_sem.at[job, quarter]
            ).wait()
        if stage < 4:
            add_blocks(8 >> stage, totals[job].at[quarter], landings[job][stage].at[quarter])
            stage_copy(job, quarter, stage + 1).start()
        else:
            mine = pl.multiple_of(y * rows, 16)
            columns = pl.ds(quarter * (width // 4), width // 4)
            results[job][:, columns] = totals[job][quarter, 0, pl.ds(mine, rows)].astype(
                jnp.float32
            ) + landings[job][4][quarter].astype(jnp.float32)

    for job in range(count):
        for quarter in range(4):
            first_blocks(job, quarter)
    for stage in range(5):
        for job in range(count):
            for quarter in range(4):
                finish(job, quarter, stage)
        if with_vectors:
            vector_finish(stage)
            vector_copy(stage + 1).start()
    if with_vectors:
        vector_finish(5)
        vector_result[...] = vector_total[0]
    for job in range(count):
        for quarter in range(4):
            for stage in range(5):
                stage_copy(job, quarter, stage).wait_send()


def reduce_shares(shares, vectors, collective_id):
    shapes = [(share.shape[1] // 2, share.shape[2]) for share in shares]
    count = len(shares)
    scratch = [
        pltpu.VMEM((4, 8, 2 * rows, width // 4), jnp.bfloat16) for rows, width in shapes
    ]
    for rows, width in shapes:
        for blocks in (8, 4, 2, 1):
            scratch.append(pltpu.VMEM((4, blocks, 2 * rows, width // 4), jnp.bfloat16))
        scratch.append(pltpu.VMEM((4, rows, width // 4), jnp.bfloat16))
    scratch += [
        pltpu.SemaphoreType.DMA((count, 4)),
        pltpu.SemaphoreType.DMA((count, 4, 5)),
        pltpu.SemaphoreType.DMA((count, 4, 5)),
    ]
    in_specs = [pl.BlockSpec(memory_space=pl.ANY)] * count
    out_specs = [pl.BlockSpec(memory_space=pltpu.VMEM)] * count
    out_shape = [jax.ShapeDtypeStruct(shape, jnp.float32) for shape in shapes]
    operands = list(shares)
    if vectors is not None:
        in_specs.append(pl.BlockSpec(memory_space=pltpu.VMEM))
        out_specs.append(pl.BlockSpec(memory_space=pltpu.VMEM))
        out_shape.append(jax.ShapeDtypeStruct(vectors.shape[1:], jnp.float32))
        operands.append(vectors)
        scratch += [
            pltpu.VMEM(vectors.shape, jnp.float32),
            pltpu.VMEM((32,) + vectors.shape[1:], jnp.float32),
            pltpu.SemaphoreType.DMA((6,)),
            pltpu.SemaphoreType.DMA((6,)),
        ]
    return pl.pallas_call(
        functools.partial(reduce_kernel, shapes, vectors is not None),
        out_shape=out_shape,
        in_specs=in_specs,
        out_specs=out_specs,
        scratch_shapes=scratch,
        compiler_params=pltpu.CompilerParams(
            collective_id=collective_id,
            has_side_effects=True,
            vmem_limit_bytes=56 * 2**20,
        ),
    )(*operands)


def on_device(
    states,
    mirror,
    w_skip,
    norm1_gain,
    norm1_bias,
    w_query,
    w_key,
    w_value,
    w_out,
    norm2_gain,
    norm2_bias,
    w_up,
    w_down,
    out_grad,
    lengths,
    infill_spans,
):
    rows_here = states.shape[2]
    model_width = states.shape[3]
    head_count = HEADS
    head_dim = model_width // head_count
    score_scale = head_dim ** (-0.5)
    seq = lax.axis_index("seq")
    own_rows = states.reshape(rows_here, model_width)
    stored = mirror.reshape(rows_here, model_width)
    partner = from_partner(stored, "section", 0)
    lengths_row = lengths.reshape(-1)
    spans_row = infill_spans.reshape(-1, 2)
    row_length = rows_here * lax.axis_size("seq")
    local = jnp.arange(rows_here, dtype=jnp.int32)
    query_place = seq * rows_here + local
    key_place = jnp.concatenate([(seq ^ step) * rows_here + local for step in range(4)])
    query_segment, inside = segment_tables(lengths_row, spans_row, query_place)
    key_segment = segment_tables(lengths_row, spans_row, key_place)[0]
    allowed = query_segment[:, None] == key_segment[None, :]
    distance = jnp.abs(query_place[:, None] - key_place[None, :]).astype(jnp.float32)
    slopes = 2.0 ** (-8.0 * (jnp.arange(head_count, dtype=jnp.float32) + 1.0) / head_count)
    gain_one = norm1_gain.astype(jnp.float32)
    bias_one = norm1_bias.astype(jnp.float32)
    gain_two = norm2_gain.astype(jnp.float32)
    bias_two = norm2_bias.astype(jnp.float32)
    w_first = w_skip[:model_width]
    w_second = w_skip[model_width:]
    core = seq % 2
    select_mine = core_selector(core, model_width)
    select_other = core_selector(1 - core, model_width)

    grad_rows = (
        out_grad.reshape(rows_here, model_width).astype(jnp.float32)
        * inside.astype(jnp.float32)[:, None]
    )
    grad_low = low(grad_rows)
    grad_low_other = swap_core(grad_low)
    hidden = project(own_rows, w_first) + project(partner, w_second)
    normed_one, unit_one, inverse_one = norm_forward(hidden, gain_one, bias_one)
    normed_one = low(normed_one)
    far = partner_of(normed_one, "seq", 2)
    near = swap_core(normed_one)
    far_near = swap_core(far)
    normed_all = jnp.concatenate([normed_one, near, far, far_near], axis=0)
    query = low(project(normed_one, w_query))
    keys_all = low(project(normed_all, w_key))
    values_all = low(project(normed_all, w_value))
    query3 = query.reshape(rows_here, head_count, head_dim)
    keys3 = keys_all.reshape(row_length, head_count, head_dim)
    values3 = values_all.reshape(row_length, head_count, head_dim)

    def scores_of():
        raw = jnp.einsum("qhd,khd->hqk", query3, keys3, preferred_element_type=jnp.float32)
        scores = raw * score_scale - slopes[:, None, None] * distance[None]
        return jnp.where(allowed[None], scores, -1e30)

    scores = scores_of()
    row_top = jnp.max(scores, axis=-1, keepdims=True)
    exponent = jnp.exp(scores - row_top)
    row_total = jnp.sum(exponent, axis=-1, keepdims=True)
    log_total = row_top + jnp.log(row_total)
    softmax_low = (exponent / row_total).astype(jnp.bfloat16)
    mixed_rows = jnp.einsum(
        "hqk,khd->qhd", softmax_low, values3, preferred_element_type=jnp.float32
    )
    mixed_rows = low(mixed_rows.reshape(rows_here, model_width))
    residual = hidden + project(mixed_rows, w_out)
    normed_two, unit_two, inverse_two = norm_forward(residual, gain_two, bias_two)
    normed_two = low(normed_two)
    upward = project(normed_two, w_up)
    activated, gelu_pull = jax.vjp(gelu_exact, upward)
    act_low = low(activated)
    result = residual + project(act_low, w_down)
    output = low(result).reshape(states.shape)
    grad_act = back_product(grad_low, w_down)
    grad_upward = low(gelu_pull(grad_act)[0])
    grad_upward_other = swap_core(grad_upward)

    hidden_width = act_low.shape[1]
    act_rows = act_low.T.reshape(32, 2, hidden_width // 64, rows_here)
    act_mine = lax.dynamic_index_in_dim(act_rows, core, 1, False).reshape(-1, rows_here)
    act_send = lax.dynamic_index_in_dim(act_rows, 1 - core, 1, False).reshape(-1, rows_here)
    act_other = swap_core(act_send)
    down_share = pair_product(act_mine, act_other, grad_low, grad_low_other)

    two_mine = low(back_product(select_mine, normed_two))
    two_other = swap_core(low(back_product(select_other, normed_two)))
    up_share = pair_product(two_mine, two_other, grad_upward, grad_upward_other)

    grad_normed_two = back_product(grad_upward, w_up)
    grad_resid_norm, grad_gain_two, grad_bias_two = norm_backward(
        grad_normed_two, unit_two, inverse_two, gain_two
    )
    grad_residual = grad_rows + grad_resid_norm
    grad_attn = low(grad_residual)
    grad_attn_other = swap_core(grad_attn)
    mixed_mine = low(back_product(select_mine, mixed_rows))
    mixed_other = swap_core(low(back_product(select_other, mixed_rows)))
    out_share = pair_product(mixed_mine, mixed_other, grad_attn, grad_attn_other)
    up_sum, down_sum, out_sum = reduce_shares([up_share, down_share, out_share], None, 1)

    grad_mixed = low(back_product(grad_attn, w_out))
    grad_mixed3 = grad_mixed.reshape(rows_here, head_count, head_dim)
    softmax_again = jnp.exp(scores_of() - log_total)
    grad_softmax = jnp.einsum(
        "qhd,khd->hqk", grad_mixed3, values3, preferred_element_type=jnp.float32
    )
    centre = jnp.sum(softmax_again * grad_softmax, axis=-1, keepdims=True)
    grad_scores = (softmax_again * (grad_softmax - centre)).astype(jnp.bfloat16)
    grad_query = (
        jnp.einsum("hqk,khd->qhd", grad_scores, keys3, preferred_element_type=jnp.float32)
        * score_scale
    )
    grad_query = low(grad_query.reshape(rows_here, model_width))
    key_part = (
        jnp.einsum("hqk,qhd->khd", grad_scores, query3, preferred_element_type=jnp.float32)
        * score_scale
    )
    value_part = jnp.einsum(
        "hqk,qhd->khd",
        softmax_again.astype(jnp.bfloat16),
        grad_mixed3,
        preferred_element_type=jnp.float32,
    )
    both_part = low(
        jnp.concatenate(
            [
                key_part.reshape(row_length, model_width),
                value_part.reshape(row_length, model_width),
            ],
            axis=1,
        )
    ).reshape(4, rows_here, 2 * model_width)
    both_other = swap_core(jnp.concatenate([both_part[1], both_part[3]], axis=0))
    both_mine = low(
        jnp.concatenate([both_part[0], both_part[2]], axis=0).astype(jnp.float32)
        + both_other.astype(jnp.float32)
    )
    both_far = swap_core(both_mine)
    grad_query_other = swap_core(grad_query)
    w_both = jnp.concatenate([w_key, w_value], axis=1)
    normed_part = back_product(both_mine, w_both)
    normed_far = partner_of(low(normed_part[rows_here:]), "seq", 2)
    grad_normed_one = (
        back_product(grad_query, w_query)
        + normed_part[:rows_here]
        + normed_far.astype(jnp.float32)
    )
    one_rows = low(back_product(select_mine, normed_all))
    query_share = low(
        project(one_rows[:, : 2 * rows_here], jnp.concatenate([grad_query, grad_query_other], axis=0))
    )
    both_rows = jnp.concatenate(
        [both_mine[:rows_here], both_far[:rows_here], both_mine[rows_here:], both_far[rows_here:]],
        axis=0,
    )
    both_share = low(project(one_rows, both_rows))

    grad_hidden_norm, grad_gain_one, grad_bias_one = norm_backward(
        grad_normed_one, unit_one, inverse_one, gain_one
    )
    grad_hidden = low(grad_residual + grad_hidden_norm)
    grad_hidden_other = swap_core(grad_hidden)
    grad_partner = low(back_product(grad_hidden, w_second))
    grad_stored = from_partner(grad_partner, "section", 0)
    grad_own = low(back_product(grad_hidden, w_first))
    joined = jnp.concatenate([own_rows, partner], axis=1)
    joined_mine = low(back_product(core_selector(core, 2 * model_width), joined))
    joined_other = swap_core(low(back_product(core_selector(1 - core, 2 * model_width), joined)))
    skip_share = pair_product(joined_mine, joined_other, grad_hidden, grad_hidden_other)
    vectors = jnp.stack([grad_gain_one, grad_bias_one, grad_gain_two, grad_bias_two])
    vectors = vectors.reshape(4, 16, 4, 16).transpose(1, 2, 0, 3).reshape(16, 4, 64)
    vectors = jnp.pad(vectors, ((0, 0), (0, 4), (0, 64)))
    query_sum, both_sum, skip_sum, sums = reduce_shares(
        [by_dp(query_share), by_dp(both_share), skip_share], vectors, 2
    )
    sums = lax.dynamic_index_in_dim(sums, seq, 0, False)[:64].reshape(4, 16)
    return (
        output,
        grad_own.reshape(states.shape),
        grad_stored.reshape(states.shape),
        skip_sum[None],
        sums[0][None],
        sums[1][None],
        query_sum[None],
        both_sum[None, :, :model_width],
        both_sum[None, :, model_width:],
        out_sum[None],
        sums[2][None],
        sums[3][None],
        up_sum[None],
        down_sum[None],
    )


def solution(mesh):
    in_specs = (
        P("section", "dp", "seq", None),
        P("section", "dp", "seq", None),
        P(),
        P(),
        P(),
        P(),
        P(),
        P(),
        P(),
        P(),
        P(),
        P(),
        P(),
        P("section", "dp", "seq", None),
        P("section", "dp", None),
        P("section", "dp", None, None),
    )
    out_specs = (
        P("section", "dp", "seq", None),
        P("section", "dp", "seq", None),
        P("section", "dp", "seq", None),
        P("section", ("dp", "seq"), None),
        P("section", ("dp", "seq")),
        P("section", ("dp", "seq")),
        P("section", ("dp", "seq"), None),
        P("section", ("dp", "seq"), None),
        P("section", ("dp", "seq"), None),
        P("section", ("dp", "seq"), None),
        P("section", ("dp", "seq")),
        P("section", ("dp", "seq")),
        P("section", ("dp", "seq"), None),
        P("section", ("dp", "seq"), None),
    )
    return jax.shard_map(
        on_device, mesh=mesh, in_specs=in_specs, out_specs=out_specs, check_vma=False
    )
```

```python
import functools

import jax
import jax.numpy as jnp
from jax.experimental import pallas as pl
from jax.experimental.pallas import tpu as pltpu
from jax import lax
from jax.sharding import PartitionSpec as P

HEADS = 16
LOG2E = 1.4426950408889634


EPS = 1e-05


def from_partner(value, axis, stride):
    mask = 2**stride
    pairs = [(source, source ^ mask) for source in range(lax.axis_size(axis))]
    return lax.ppermute(value, axis, pairs)


def project(left, right):
    return jnp.dot(left, right, preferred_element_type=jnp.float32)


def rows_product(left, right):
    return lax.dot_general(
        left, right, (((0,), (0,)), ((), ())), preferred_element_type=jnp.float32
    )


def back_product(left, right):
    return lax.dot_general(
        left, right, (((1,), (1,)), ((), ())), preferred_element_type=jnp.float32
    )


def norm_forward(hidden, gain, bias):
    center = hidden - jnp.mean(hidden, axis=-1, keepdims=True)
    variance = jnp.mean(center * center, axis=-1, keepdims=True)
    inverse = lax.rsqrt(variance + EPS)
    unit = center * inverse
    return (unit * gain + bias, unit, inverse)


def norm_backward(grad, unit, inverse, gain):
    scaled = grad * gain
    mean_one = jnp.mean(scaled, axis=-1, keepdims=True)
    mean_two = jnp.mean(scaled * unit, axis=-1, keepdims=True)
    grad_input = inverse * (scaled - mean_one - unit * mean_two)
    return (grad_input, jnp.sum(grad * unit, axis=0), jnp.sum(grad, axis=0))


def segment_tables(lengths_row, spans_row, places):
    ends = jnp.cumsum(lengths_row, dtype=jnp.int32)
    starts = ends - lengths_row
    segment = jnp.sum((places[:, None] >= ends[None, :]).astype(jnp.int32), axis=1)
    lower = starts + spans_row[:, 0]
    upper = starts + spans_row[:, 1]
    inside = jnp.any(
        (places[:, None] >= lower[None, :]) & (places[:, None] < upper[None, :]), axis=1
    )
    return (segment, inside)


def partner_of(value, axis, mask):
    pairs = [(source, source ^ mask) for source in range(lax.axis_size(axis))]
    return lax.ppermute(value, axis, pairs)


def core_selector(core, rows):
    piece = rows // 64
    target = jnp.arange(rows // 2, dtype=jnp.int32)
    source = (target // piece) * (2 * piece) + core * piece + target % piece
    return (source[:, None] == jnp.arange(rows, dtype=jnp.int32)[None, :]).astype(jnp.bfloat16)


def swap_core(value):
    return partner_of(value, "seq", 1)


def low(value):
    return value.astype(jnp.bfloat16)


def pair_product(kept, swapped, grad, grad_swapped):
    left = jnp.concatenate([kept, swapped], axis=1)
    right = jnp.concatenate([grad, grad_swapped], axis=0)
    return by_dp(low(project(left, right)))


def by_dp(value):
    return value.reshape(16, value.shape[0] // 16, value.shape[1])


MESH = pl.DeviceIdType.MESH
NEAR, WRAP = (0, 3, 1, 2), (0, 1, 3, 2)
QUARTERS = (("x", NEAR), ("x", WRAP), ("z", NEAR), ("z", WRAP))


def flip(value, mask):
    if mask == 1:
        return value + 1 - 2 * lax.rem(value, 2)
    if mask == 2:
        return lax.rem(value + 2, 4)
    if mask == 3:
        return 3 - value
    return value


def block_place(quarter, outer, inner, x, z):
    first, order = QUARTERS[quarter]
    if first == "x":
        return flip(z, order[inner]) * 4 + flip(x, order[outer])
    return flip(z, order[outer]) * 4 + flip(x, order[inner])


def stage_partner(quarter, stage, x, z, seq):
    if stage == 4:
        return {"seq": lax.rem(seq + 2, 4)}
    first, order = QUARTERS[quarter]
    mask = order[2] if stage % 2 == 0 else order[1]
    if (first == "x") == (stage < 2):
        return {"dp": z * 4 + flip(x, mask)}
    return {"dp": flip(z, mask) * 4 + x}


def remote(source, target, send, recv, device):
    return pltpu.make_async_remote_copy(
        src_ref=source,
        dst_ref=target,
        send_sem=send,
        recv_sem=recv,
        device_id=device,
        device_id_type=MESH,
    )


def enter(devices):
    barrier = pltpu.get_barrier_semaphore()
    for device in devices:
        pl.semaphore_signal(barrier, inc=1, device_id=device, device_id_type=MESH)
    pl.semaphore_wait(barrier, len(devices))


def add_blocks(count, total, other):
    def one(index, carry):
        total[index] = (
            total[index].astype(jnp.float32) + other[index].astype(jnp.float32)
        ).astype(jnp.bfloat16)
        return carry

    lax.fori_loop(0, count, one, 0)


def reduce_kernel(shapes, with_vectors, *refs):
    count = len(shapes)
    refs = list(refs)
    take = lambda n: [refs.pop(0) for _ in range(n)]
    sources = take(count)
    vector = take(1)[0] if with_vectors else None
    results = take(count)
    vector_result = take(1)[0] if with_vectors else None
    totals = take(count)
    landings = [take(5) for _ in range(count)]
    local_sem, send_sem, recv_sem = take(3)
    if with_vectors:
        vector_total, vector_landing, vector_send, vector_recv = take(4)

    dp, seq = lax.axis_index("dp"), lax.axis_index("seq")
    z, x = lax.div(dp, 4), lax.rem(dp, 4)
    y = lax.div(seq, 2)
    partners = [stage_partner(0, 0, x, z, seq), stage_partner(0, 1, x, z, seq)]
    partners += [stage_partner(2, 0, x, z, seq), stage_partner(2, 1, x, z, seq)]
    partners += [stage_partner(0, 4, x, z, seq)]
    core = {"seq": flip(seq, 1)}
    if with_vectors:
        partners += [core]
    enter(partners)

    vector_stages = [(core, 0, 0, 16)]
    if with_vectors:
        vector_stages += [(stage_partner(0, 0, x, z, seq), 8, 16, 8)]
        vector_stages += [(stage_partner(0, 1, x, z, seq), 4, 24, 4)]
        vector_stages += [(stage_partner(0, 2, x, z, seq), 2, 28, 2)]
        vector_stages += [(stage_partner(0, 3, x, z, seq), 1, 30, 1)]
        vector_stages += [(stage_partner(0, 4, x, z, seq), 0, 31, 1)]

    def vector_copy(step):
        device, first, landing, size = vector_stages[step]
        return remote(
            vector_total.at[pl.ds(first, size)],
            vector_landing.at[pl.ds(landing, size)],
            vector_send.at[step],
            vector_recv.at[step],
            device,
        )

    def vector_finish(step):
        _, _, landing, size = vector_stages[step]
        copy = vector_copy(step)
        copy.wait()
        vector_total[pl.ds(0, size)] += vector_landing[pl.ds(landing, size)]

    if with_vectors:
        for index in range(16):
            outer, inner = index // 4, index % 4
            vector_total[index] = vector[block_place(0, outer, inner, x, z)]
        vector_copy(0).start()

    def first_blocks(job, quarter):
        rows, width = shapes[job]
        columns = pl.ds(quarter * (width // 4), width // 4)
        for index in range(8):
            outer, inner = index // 4, index % 4
            there = block_place(quarter, outer + 2, inner, x, z)
            here = block_place(quarter, outer, inner, x, z)
            remote(
                sources[job].at[there, :, columns],
                landings[job][0].at[quarter, index],
                send_sem.at[job, quarter, 0],
                recv_sem.at[job, quarter, 0],
                stage_partner(quarter, 0, x, z, seq),
            ).start()
            pltpu.make_async_copy(
                sources[job].at[here, :, columns],
                totals[job].at[quarter, index],
                local_sem.at[job, quarter],
            ).start()

    def stage_copy(job, quarter, stage):
        rows, width = shapes[job]
        if stage == 0:
            source = landings[job][0].at[quarter]
            target = landings[job][0].at[quarter]
        elif stage < 4:
            size = 8 >> stage
            source = totals[job].at[quarter, pl.ds(size, size)]
            target = landings[job][stage].at[quarter]
        else:
            away = pl.multiple_of((1 - y) * rows, 16)
            source = totals[job].at[quarter, 0, pl.ds(away, rows)]
            target = landings[job][4].at[quarter]
        return remote(
            source,
            target,
            send_sem.at[job, quarter, stage],
            recv_sem.at[job, quarter, stage],
            stage_partner(quarter, stage, x, z, seq),
        )

    def finish(job, quarter, stage):
        rows, width = shapes[job]
        stage_copy(job, quarter, stage).wait_recv()
        if stage == 0:
            pltpu.make_async_copy(
                totals[job].at[quarter], totals[job].at[quarter], local_sem.at[job, quarter]
            ).wait()
        if stage < 4:
            add_blocks(8 >> stage, totals[job].at[quarter], landings[job][stage].at[quarter])
            stage_copy(job, quarter, stage + 1).start()
        else:
            mine = pl.multiple_of(y * rows, 16)
            columns = pl.ds(quarter * (width // 4), width // 4)
            results[job][:, columns] = totals[job][quarter, 0, pl.ds(mine, rows)].astype(
                jnp.float32
            ) + landings[job][4][quarter].astype(jnp.float32)

    for job in range(count):
        for quarter in range(4):
            first_blocks(job, quarter)
    for stage in range(5):
        for job in range(count):
            for quarter in range(4):
                finish(job, quarter, stage)
        if with_vectors:
            vector_finish(stage)
            vector_copy(stage + 1).start()
    if with_vectors:
        vector_finish(5)
        vector_result[...] = vector_total[0]
    for job in range(count):
        for quarter in range(4):
            for stage in range(5):
                stage_copy(job, quarter, stage).wait_send()


def reduce_shares(shares, vectors, collective_id):
    shapes = [(share.shape[1] // 2, share.shape[2]) for share in shares]
    count = len(shares)
    scratch = [
        pltpu.VMEM((4, 8, 2 * rows, width // 4), jnp.bfloat16) for rows, width in shapes
    ]
    for rows, width in shapes:
        for blocks in (8, 4, 2, 1):
            scratch.append(pltpu.VMEM((4, blocks, 2 * rows, width // 4), jnp.bfloat16))
        scratch.append(pltpu.VMEM((4, rows, width // 4), jnp.bfloat16))
    scratch += [
        pltpu.SemaphoreType.DMA((count, 4)),
        pltpu.SemaphoreType.DMA((count, 4, 5)),
        pltpu.SemaphoreType.DMA((count, 4, 5)),
    ]
    in_specs = [pl.BlockSpec(memory_space=pl.ANY)] * count
    out_specs = [pl.BlockSpec(memory_space=pltpu.VMEM)] * count
    out_shape = [jax.ShapeDtypeStruct(shape, jnp.float32) for shape in shapes]
    operands = list(shares)
    if vectors is not None:
        in_specs.append(pl.BlockSpec(memory_space=pltpu.VMEM))
        out_specs.append(pl.BlockSpec(memory_space=pltpu.VMEM))
        out_shape.append(jax.ShapeDtypeStruct(vectors.shape[1:], jnp.float32))
        operands.append(vectors)
        scratch += [
            pltpu.VMEM(vectors.shape, jnp.float32),
            pltpu.VMEM((32,) + vectors.shape[1:], jnp.float32),
            pltpu.SemaphoreType.DMA((6,)),
            pltpu.SemaphoreType.DMA((6,)),
        ]
    return pl.pallas_call(
        functools.partial(reduce_kernel, shapes, vectors is not None),
        out_shape=out_shape,
        in_specs=in_specs,
        out_specs=out_specs,
        scratch_shapes=scratch,
        compiler_params=pltpu.CompilerParams(
            collective_id=collective_id,
            has_side_effects=True,
            vmem_limit_bytes=56 * 2**20,
        ),
    )(*operands)


def attention_forward_kernel(
    query, keys, values, key_places, key_segments, query_places, query_segments, slopes,
    shares, mixed, inverses, distance, scores,
):
    span = keys.shape[0]
    chunk = 128
    here = query.shape[0]

    @pl.when(pl.program_id(0) == 0)
    def _():
        gap = jnp.abs(query_places[...] - key_places[...]).astype(jnp.float32)
        same = query_segments[...] == key_segments[...]
        distance[...] = jnp.where(same, gap, 1e30)

    lane = lax.broadcasted_iota(jnp.int32, query.shape, 1)
    zero = jnp.zeros(query.shape, query.dtype)
    both = jnp.concatenate(
        [jnp.where(lane < 64, query[...], zero), jnp.where(lane >= 64, query[...], zero)], axis=0
    )
    slope = slopes[0]

    def raw(index, top):
        rows = pl.ds(pl.multiple_of(index * chunk, chunk), chunk)
        part = back_product(keys[rows], both)
        gap = distance[rows]
        part = part - slope * jnp.concatenate([gap, gap], axis=1)
        scores[rows] = part
        return jnp.maximum(top, jnp.max(part.reshape(chunk // 8, 8, 2 * here), axis=0))

    top = lax.fori_loop(
        0, span // chunk, raw, jnp.full((8, 2 * here), -jnp.inf, jnp.float32), unroll=True
    )
    top = jnp.max(top, axis=0, keepdims=True)

    def exponent(index, carry):
        rows = pl.ds(pl.multiple_of(index * chunk, chunk), chunk)
        shares[0, rows] = jnp.exp2(scores[rows] - top).astype(jnp.bfloat16)
        return carry

    lax.fori_loop(0, span // chunk, exponent, 0, unroll=True)
    turned = jnp.concatenate([values[...].T, jnp.ones((16, span), jnp.bfloat16)], axis=0)
    out = project(turned, shares[0])
    inverse = 1.0 / out[128:129]
    inverses[0] = inverse
    out = out[:128] * inverse
    out = jnp.concatenate([out[:64, :here], out[64:, here:]], axis=0)
    mixed[...] = out.T.astype(jnp.bfloat16)


def attention_forward(query, keys, values, tables, slopes):
    here, width = query.shape
    span = keys.shape[0]
    pairs = width // 128
    whole = lambda a: pl.BlockSpec(a.shape, lambda i: (0,) * a.ndim)
    return pl.pallas_call(
        attention_forward_kernel,
        grid=(pairs,),
        in_specs=[
            pl.BlockSpec((here, 128), lambda i: (0, i)),
            pl.BlockSpec((span, 128), lambda i: (0, i)),
            pl.BlockSpec((span, 128), lambda i: (0, i)),
            *[whole(table) for table in tables],
            pl.BlockSpec((1, 1, 2 * here), lambda i: (i, 0, 0)),
        ],
        out_specs=[
            pl.BlockSpec((1, span, 2 * here), lambda i: (i, 0, 0)),
            pl.BlockSpec((here, 128), lambda i: (0, i)),
            pl.BlockSpec((1, 1, 2 * here), lambda i: (i, 0, 0)),
        ],
        out_shape=[
            jax.ShapeDtypeStruct((pairs, span, 2 * here), jnp.bfloat16),
            jax.ShapeDtypeStruct((here, width), jnp.bfloat16),
            jax.ShapeDtypeStruct((pairs, 1, 2 * here), jnp.float32),
        ],
        scratch_shapes=[
            pltpu.VMEM((span, here), jnp.float32),
            pltpu.VMEM((span, 2 * here), jnp.float32),
        ],
        compiler_params=pltpu.CompilerParams(vmem_limit_bytes=40 * 2**20),
    )(query, keys, values, *tables, slopes)


def attention_backward_kernel(
    query, keys, values, shares, inverses, grad, mixed, grad_query, grad_keys, grad_values, lows
):
    span = keys.shape[0]
    chunk = 128
    here = query.shape[0]
    lane = lax.broadcasted_iota(jnp.int32, query.shape, 1)
    zero = jnp.zeros(query.shape, query.dtype)

    def stacked(value):
        return jnp.concatenate(
            [jnp.where(lane < 64, value, zero), jnp.where(lane >= 64, value, zero)], axis=0
        )

    queries = stacked(query[...])
    inverse = inverses[0]
    turned = grad[...].astype(jnp.float32).T
    product = turned * mixed[...].astype(jnp.float32).T
    top = turned[:64] * inverse[:, :here]
    low_half = turned[64:] * inverse[:, here:]
    none = jnp.zeros_like(top)
    grads = jnp.concatenate(
        [jnp.concatenate([top, none], axis=1), jnp.concatenate([none, low_half], axis=1)], axis=0
    ).astype(jnp.bfloat16)
    grads_back = grads.T
    centre = inverse * jnp.concatenate(
        [
            jnp.sum(product[:64], axis=0, keepdims=True),
            jnp.sum(product[64:], axis=0, keepdims=True),
        ],
        axis=1,
    )

    def part(index, carry):
        rows = pl.ds(pl.multiple_of(index * chunk, chunk), chunk)
        grad_share = project(values[rows], grads)
        share = shares[0, rows]
        grad_score = (share.astype(jnp.float32) * (grad_share - centre)).astype(jnp.bfloat16)
        lows[rows] = grad_score
        grad_keys[rows] = (project(grad_score, queries) * 0.6931471805599453).astype(jnp.bfloat16)
        grad_values[rows] = project(share, grads_back).astype(jnp.bfloat16)
        return carry

    lax.fori_loop(0, span // chunk, part, 0, unroll=True)
    out = rows_product(keys[...], lows[...])
    out = jnp.concatenate([out[:64, :here], out[64:, here:]], axis=0)
    grad_query[...] = (out.T * 0.125).astype(jnp.bfloat16)


def attention_backward(query, keys, values, shares, inverses, grad, mixed):
    here, width = query.shape
    span = keys.shape[0]
    pairs = width // 128
    column = lambda rows: pl.BlockSpec((rows, 128), lambda i: (0, i))
    return pl.pallas_call(
        attention_backward_kernel,
        grid=(pairs,),
        in_specs=[
            column(here),
            column(span),
            column(span),
            pl.BlockSpec((1, span, 2 * here), lambda i: (i, 0, 0)),
            pl.BlockSpec((1, 1, 2 * here), lambda i: (i, 0, 0)),
            column(here),
            column(here),
        ],
        out_specs=[column(here), column(span), column(span)],
        out_shape=[
            jax.ShapeDtypeStruct((here, width), jnp.bfloat16),
            jax.ShapeDtypeStruct((span, width), jnp.bfloat16),
            jax.ShapeDtypeStruct((span, width), jnp.bfloat16),
        ],
        scratch_shapes=[pltpu.VMEM((span, 2 * here), jnp.bfloat16)],
        compiler_params=pltpu.CompilerParams(vmem_limit_bytes=40 * 2**20),
    )(query, keys, values, shares, inverses, grad, mixed)


def mean_rows(value):
    return jnp.mean(value, axis=-1, keepdims=True)


def ffn_kernel(
    core, hidden, mixed, grad_low, w_out, gain, bias, w_up, w_down,
    output, act_kept, act_sent, two_kept, two_sent, grad_up, grad_attn, grad_mixed, gain_sum, bias_sum,
    residual, unit, inverse, normed, total, grad_normed, turned,
):
    step = pl.program_id(0)
    last = pl.num_programs(0) - 1
    here = hidden.shape[0]
    mine = core[0]
    root = 0.7071067811865476

    @pl.when(step == 0)
    def _():
        value = hidden[...] + project(mixed[...], w_out[...])
        center = value - mean_rows(value)
        scale = lax.rsqrt(mean_rows(center * center) + EPS)
        residual[...] = value
        unit[...] = center * scale
        inverse[...] = scale
        two = (unit[...] * gain[...] + bias[...]).astype(jnp.bfloat16)
        normed[...] = two
        total[...] = jnp.zeros_like(total)
        grad_normed[...] = jnp.zeros_like(grad_normed)
        turned[...] = two.T

        def split(index, carry):
            place = pl.ds(pl.multiple_of(index * 16, 16), 16)
            two_kept[place] = turned[pl.ds(pl.multiple_of(index * 32 + mine * 16, 16), 16)]
            two_sent[place] = turned[pl.ds(pl.multiple_of(index * 32 + (1 - mine) * 16, 16), 16)]
            return carry

        lax.fori_loop(0, two_kept.shape[0] // 16, split, 0)

    upward = project(normed[...], w_up[...])
    cdf = 0.5 * (1.0 + lax.erf(upward * root))
    act = (upward * cdf).astype(jnp.bfloat16)
    density = jnp.exp(upward * upward * -0.5) * 0.3989422804014327
    slope = cdf + upward * density
    back = back_product(grad_low[...], w_down[...])
    grad = (back * slope).astype(jnp.bfloat16)
    grad_up[...] = grad
    total[...] += project(act, w_down[...])
    grad_normed[...] += back_product(grad, w_up[...])
    width = act.shape[1]
    turned[pl.ds(0, width)] = act.T
    for index in range(width // 128):
        place = pl.ds(index * 64, 64)
        act_kept[place] = turned[pl.ds(pl.multiple_of(index * 128 + mine * 64, 64), 64)]
        act_sent[place] = turned[pl.ds(pl.multiple_of(index * 128 + (1 - mine) * 64, 64), 64)]

    @pl.when(step == last)
    def _():
        output[...] = (residual[...] + total[...]).astype(jnp.bfloat16)
        grads = grad_normed[...]
        scaled = grads * gain[...]
        units = unit[...]
        step_one = scaled - mean_rows(scaled) - units * mean_rows(scaled * units)
        value = grad_low[...].astype(jnp.float32) + inverse[...] * step_one
        gain_sum[...] = jnp.sum(grads * units, axis=0, keepdims=True)
        bias_sum[...] = jnp.sum(grads, axis=0, keepdims=True)
        grad_attn[...] = value
        grad_mixed[...] = back_product(value.astype(jnp.bfloat16), w_out[...]).astype(jnp.bfloat16)


def feed_forward(core, hidden, mixed, grad_low, w_out, gain, bias, w_up, w_down):
    here, width = hidden.shape
    full = w_up.shape[1]
    block = 512
    whole = lambda shape: pl.BlockSpec(shape, lambda i: (0,) * len(shape))
    return pl.pallas_call(
        ffn_kernel,
        grid=(full // block,),
        in_specs=[
            pl.BlockSpec(memory_space=pltpu.SMEM),
            whole((here, width)),
            whole((here, width)),
            whole((here, width)),
            whole((width, width)),
            whole((1, width)),
            whole((1, width)),
            pl.BlockSpec((width, block), lambda i: (0, i)),
            pl.BlockSpec((block, width), lambda i: (i, 0)),
        ],
        out_specs=[
            whole((here, width)),
            pl.BlockSpec((block // 2, here), lambda i: (i, 0)),
            pl.BlockSpec((block // 2, here), lambda i: (i, 0)),
            whole((width // 2, here)),
            whole((width // 2, here)),
            pl.BlockSpec((here, block), lambda i: (0, i)),
            whole((here, width)),
            whole((here, width)),
            whole((1, width)),
            whole((1, width)),
        ],
        out_shape=[
            jax.ShapeDtypeStruct((here, width), jnp.bfloat16),
            jax.ShapeDtypeStruct((full // 2, here), jnp.bfloat16),
            jax.ShapeDtypeStruct((full // 2, here), jnp.bfloat16),
            jax.ShapeDtypeStruct((width // 2, here), jnp.bfloat16),
            jax.ShapeDtypeStruct((width // 2, here), jnp.bfloat16),
            jax.ShapeDtypeStruct((here, full), jnp.bfloat16),
            jax.ShapeDtypeStruct((here, width), jnp.float32),
            jax.ShapeDtypeStruct((here, width), jnp.bfloat16),
            jax.ShapeDtypeStruct((1, width), jnp.float32),
            jax.ShapeDtypeStruct((1, width), jnp.float32),
        ],
        scratch_shapes=[
            pltpu.VMEM((here, width), jnp.float32),
            pltpu.VMEM((here, width), jnp.float32),
            pltpu.VMEM((here, 1), jnp.float32),
            pltpu.VMEM((here, width), jnp.bfloat16),
            pltpu.VMEM((here, width), jnp.float32),
            pltpu.VMEM((here, width), jnp.float32),
            pltpu.VMEM((width, here), jnp.bfloat16),
        ],
        compiler_params=pltpu.CompilerParams(vmem_limit_bytes=48 * 2**20),
    )(core, hidden, mixed, grad_low, w_out, gain, bias, w_up, w_down)


def on_device(
    states,
    mirror,
    w_skip,
    norm1_gain,
    norm1_bias,
    w_query,
    w_key,
    w_value,
    w_out,
    norm2_gain,
    norm2_bias,
    w_up,
    w_down,
    out_grad,
    lengths,
    infill_spans,
):
    rows_here = states.shape[2]
    model_width = states.shape[3]
    head_count = HEADS
    head_dim = model_width // head_count
    query_scale = head_dim ** (-0.5) * LOG2E
    seq = lax.axis_index("seq")
    own_rows = states.reshape(rows_here, model_width)
    stored = mirror.reshape(rows_here, model_width)
    partner = from_partner(stored, "section", 0)
    lengths_row = lengths.reshape(-1)
    spans_row = infill_spans.reshape(-1, 2)
    row_length = rows_here * lax.axis_size("seq")
    local = jnp.arange(rows_here, dtype=jnp.int32)
    query_place = seq * rows_here + local
    key_place = jnp.concatenate([(seq ^ step) * rows_here + local for step in range(4)])
    query_segment, inside = segment_tables(lengths_row, spans_row, query_place)
    key_segment = segment_tables(lengths_row, spans_row, key_place)[0]
    tables = (key_place[:, None], key_segment[:, None], query_place[None], query_segment[None])
    slopes = 2.0 ** (-8.0 * (jnp.arange(head_count, dtype=jnp.float32) + 1.0) / head_count)
    slopes = jnp.repeat(LOG2E * slopes.reshape(-1, 2), rows_here, axis=1)[:, None, :]
    gain_one = norm1_gain.astype(jnp.float32)
    bias_one = norm1_bias.astype(jnp.float32)
    w_first = w_skip[:model_width]
    w_second = w_skip[model_width:]
    core = seq % 2
    select_mine = core_selector(core, model_width)
    select_other = core_selector(1 - core, model_width)

    grad_low = jnp.where(
        inside[:, None], out_grad.reshape(rows_here, model_width), jnp.bfloat16(0)
    )
    grad_low_other = swap_core(grad_low)
    hidden = project(own_rows, w_first) + project(partner, w_second)
    normed_one, unit_one, inverse_one = norm_forward(hidden, gain_one, bias_one)
    normed_one = low(normed_one)
    far = partner_of(normed_one, "seq", 2)
    near = swap_core(normed_one)
    far_near = swap_core(far)
    normed_all = jnp.concatenate([normed_one, near, far, far_near], axis=0)
    query = low(project(normed_one, w_query) * query_scale)
    keys_all = low(project(normed_all, w_key))
    values_all = low(project(normed_all, w_value))
    shares, mixed_rows, inverses = attention_forward(query, keys_all, values_all, tables, slopes)
    (
        output,
        act_mine,
        act_send,
        two_mine,
        two_send,
        grad_upward,
        grad_residual,
        grad_mixed,
        grad_gain_two,
        grad_bias_two,
    ) = feed_forward(
        core.reshape(1),
        hidden,
        mixed_rows,
        grad_low,
        w_out,
        norm2_gain.astype(jnp.float32)[None],
        norm2_bias.astype(jnp.float32)[None],
        w_up,
        w_down,
    )
    output = output.reshape(states.shape)
    grad_upward_other = swap_core(grad_upward)

    act_other = swap_core(act_send)
    down_share = pair_product(act_mine, act_other, grad_low, grad_low_other)
    two_other = swap_core(two_send)
    up_share = pair_product(two_mine, two_other, grad_upward, grad_upward_other)
    grad_attn = low(grad_residual)
    grad_attn_other = swap_core(grad_attn)
    mixed_mine = low(back_product(select_mine, mixed_rows))
    mixed_other = swap_core(low(back_product(select_other, mixed_rows)))
    out_share = pair_product(mixed_mine, mixed_other, grad_attn, grad_attn_other)
    up_sum, down_sum, out_sum = reduce_shares([up_share, down_share, out_share], None, 1)

    grad_query, key_part, value_part = attention_backward(
        query, keys_all, values_all, shares, inverses, grad_mixed, mixed_rows
    )
    both_part = jnp.concatenate([key_part, value_part], axis=1).reshape(4, rows_here, -1)
    both_other = swap_core(jnp.concatenate([both_part[1], both_part[3]], axis=0))
    both_mine = low(
        jnp.concatenate([both_part[0], both_part[2]], axis=0).astype(jnp.float32)
        + both_other.astype(jnp.float32)
    )
    both_far = swap_core(both_mine)
    grad_query_other = swap_core(grad_query)
    w_both = jnp.concatenate([w_key, w_value], axis=1)
    normed_part = back_product(both_mine, w_both)
    normed_far = partner_of(low(normed_part[rows_here:]), "seq", 2)
    grad_normed_one = (
        back_product(grad_query, w_query)
        + normed_part[:rows_here]
        + normed_far.astype(jnp.float32)
    )
    one_rows = low(back_product(select_mine, normed_all))
    query_share = low(
        project(one_rows[:, : 2 * rows_here], jnp.concatenate([grad_query, grad_query_other], axis=0))
    )
    both_rows = jnp.concatenate(
        [both_mine[:rows_here], both_far[:rows_here], both_mine[rows_here:], both_far[rows_here:]],
        axis=0,
    )
    both_share = low(project(one_rows, both_rows))

    grad_hidden_norm, grad_gain_one, grad_bias_one = norm_backward(
        grad_normed_one, unit_one, inverse_one, gain_one
    )
    grad_hidden = low(grad_residual + grad_hidden_norm)
    grad_hidden_other = swap_core(grad_hidden)
    grad_partner = low(back_product(grad_hidden, w_second))
    grad_stored = from_partner(grad_partner, "section", 0)
    grad_own = low(back_product(grad_hidden, w_first))
    joined = jnp.concatenate([own_rows, partner], axis=1)
    joined_mine = low(back_product(core_selector(core, 2 * model_width), joined))
    joined_other = swap_core(low(back_product(core_selector(1 - core, 2 * model_width), joined)))
    skip_share = pair_product(joined_mine, joined_other, grad_hidden, grad_hidden_other)
    vectors = jnp.stack(
        [grad_gain_one, grad_bias_one, grad_gain_two[0], grad_bias_two[0]]
    )
    vectors = vectors.reshape(4, 16, 4, 16).transpose(1, 2, 0, 3).reshape(16, 4, 64)
    vectors = jnp.pad(vectors, ((0, 0), (0, 4), (0, 64)))
    query_sum, both_sum, skip_sum, sums = reduce_shares(
        [by_dp(query_share), by_dp(both_share), skip_share], vectors, 2
    )
    sums = lax.dynamic_index_in_dim(sums, seq, 0, False)[:64].reshape(4, 16)
    return (
        output,
        grad_own.reshape(states.shape),
        grad_stored.reshape(states.shape),
        skip_sum[None],
        sums[0][None],
        sums[1][None],
        query_sum[None],
        both_sum[None, :, :model_width],
        both_sum[None, :, model_width:],
        out_sum[None],
        sums[2][None],
        sums[3][None],
        up_sum[None],
        down_sum[None],
    )


def solution(mesh):
    in_specs = (
        P("section", "dp", "seq", None),
        P("section", "dp", "seq", None),
        P(),
        P(),
        P(),
        P(),
        P(),
        P(),
        P(),
        P(),
        P(),
        P(),
        P(),
        P("section", "dp", "seq", None),
        P("section", "dp", None),
        P("section", "dp", None, None),
    )
    out_specs = (
        P("section", "dp", "seq", None),
        P("section", "dp", "seq", None),
        P("section", "dp", "seq", None),
        P("section", ("dp", "seq"), None),
        P("section", ("dp", "seq")),
        P("section", ("dp", "seq")),
        P("section", ("dp", "seq"), None),
        P("section", ("dp", "seq"), None),
        P("section", ("dp", "seq"), None),
        P("section", ("dp", "seq"), None),
        P("section", ("dp", "seq")),
        P("section", ("dp", "seq")),
        P("section", ("dp", "seq"), None),
        P("section", ("dp", "seq"), None),
    )
    return jax.shard_map(
        on_device, mesh=mesh, in_specs=in_specs, out_specs=out_specs, check_vma=False
    )
```

```python
import functools

import jax
import jax.numpy as jnp
from jax.experimental import pallas as pl
from jax.experimental.pallas import tpu as pltpu
from jax import lax
from jax.sharding import PartitionSpec as P

HEADS = 16
LOG2E = 1.4426950408889634
LN2 = 0.6931471805599453


EPS = 1e-05


def from_partner(value, axis, stride):
    mask = 2**stride
    pairs = [(source, source ^ mask) for source in range(lax.axis_size(axis))]
    return lax.ppermute(value, axis, pairs)


def project(left, right):
    return jnp.dot(left, right, preferred_element_type=jnp.float32)


def rows_product(left, right):
    return lax.dot_general(
        left, right, (((0,), (0,)), ((), ())), preferred_element_type=jnp.float32
    )


def back_product(left, right):
    return lax.dot_general(
        left, right, (((1,), (1,)), ((), ())), preferred_element_type=jnp.float32
    )


def norm_forward(hidden, gain, bias):
    center = hidden - jnp.mean(hidden, axis=-1, keepdims=True)
    variance = jnp.mean(center * center, axis=-1, keepdims=True)
    inverse = lax.rsqrt(variance + EPS)
    unit = center * inverse
    return (unit * gain + bias, unit, inverse)


def norm_backward(grad, unit, inverse, gain):
    scaled = grad * gain
    mean_one = jnp.mean(scaled, axis=-1, keepdims=True)
    mean_two = jnp.mean(scaled * unit, axis=-1, keepdims=True)
    grad_input = inverse * (scaled - mean_one - unit * mean_two)
    return (grad_input, jnp.sum(grad * unit, axis=0), jnp.sum(grad, axis=0))


def segment_tables(lengths_row, spans_row, places):
    ends = jnp.cumsum(lengths_row, dtype=jnp.int32)
    starts = ends - lengths_row
    segment = jnp.sum((places[:, None] >= ends[None, :]).astype(jnp.int32), axis=1)
    lower = starts + spans_row[:, 0]
    upper = starts + spans_row[:, 1]
    inside = jnp.any(
        (places[:, None] >= lower[None, :]) & (places[:, None] < upper[None, :]), axis=1
    )
    return (segment, inside)


def partner_of(value, axis, mask):
    pairs = [(source, source ^ mask) for source in range(lax.axis_size(axis))]
    return lax.ppermute(value, axis, pairs)


def core_selector(core, rows):
    piece = rows // 64
    target = jnp.arange(rows // 2, dtype=jnp.int32)
    source = (target // piece) * (2 * piece) + core * piece + target % piece
    return (source[:, None] == jnp.arange(rows, dtype=jnp.int32)[None, :]).astype(jnp.bfloat16)


def swap_core(value):
    return partner_of(value, "seq", 1)


def low(value):
    return value.astype(jnp.bfloat16)


def pair_product(kept, swapped, grad, grad_swapped):
    left = jnp.concatenate([kept, swapped], axis=1)
    right = jnp.concatenate([grad, grad_swapped], axis=0)
    return by_dp(low(project(left, right)))


def by_dp(value):
    return value.reshape(16, value.shape[0] // 16, value.shape[1])


MESH = pl.DeviceIdType.MESH
NEAR, WRAP = (0, 3, 1, 2), (0, 1, 3, 2)
QUARTERS = (("x", NEAR), ("x", WRAP), ("z", NEAR), ("z", WRAP))


def flip(value, mask):
    if mask == 1:
        return value + 1 - 2 * lax.rem(value, 2)
    if mask == 2:
        return lax.rem(value + 2, 4)
    if mask == 3:
        return 3 - value
    return value


def block_place(quarter, outer, inner, x, z):
    first, order = QUARTERS[quarter]
    if first == "x":
        return flip(z, order[inner]) * 4 + flip(x, order[outer])
    return flip(z, order[outer]) * 4 + flip(x, order[inner])


def stage_partner(quarter, stage, x, z, seq):
    if stage == 4:
        return {"seq": lax.rem(seq + 2, 4)}
    first, order = QUARTERS[quarter]
    mask = order[2] if stage % 2 == 0 else order[1]
    if (first == "x") == (stage < 2):
        return {"dp": z * 4 + flip(x, mask)}
    return {"dp": flip(z, mask) * 4 + x}


def remote(source, target, send, recv, device):
    return pltpu.make_async_remote_copy(
        src_ref=source,
        dst_ref=target,
        send_sem=send,
        recv_sem=recv,
        device_id=device,
        device_id_type=MESH,
    )


def enter(devices):
    barrier = pltpu.get_barrier_semaphore()
    for device in devices:
        pl.semaphore_signal(barrier, inc=1, device_id=device, device_id_type=MESH)
    pl.semaphore_wait(barrier, len(devices))


def add_blocks(count, total, other):
    def one(index, carry):
        total[index] = (
            total[index].astype(jnp.float32) + other[index].astype(jnp.float32)
        ).astype(jnp.bfloat16)
        return carry

    lax.fori_loop(0, count, one, 0)


def place_here():
    dp, seq = lax.axis_index("dp"), lax.axis_index("seq")
    return lax.div(dp, 4), lax.rem(dp, 4), seq


def ring_partners(z, x, seq):
    pairs = ((0, 0), (0, 1), (2, 0), (2, 1), (0, 4))
    return [stage_partner(quarter, stage, x, z, seq) for quarter, stage in pairs]


class Halving:
    def __init__(self, shapes, sources, results, scratch):
        self.shapes, self.sources, self.results = shapes, sources, results
        scratch = list(scratch)
        count = len(shapes)
        self.totals = scratch[:count]
        self.landings = [scratch[count + 5 * job : count + 5 * job + 5] for job in range(count)]
        self.local_sem, self.send_sem, self.recv_sem = scratch[6 * count :]
        self.z, self.x, self.seq = place_here()
        self.y = lax.div(self.seq, 2)

    @staticmethod
    def scratch(shapes):
        count = len(shapes)
        shapes_of = [(4, 8, 2 * rows, width // 4) for rows, width in shapes]
        for rows, width in shapes:
            shapes_of += [(4, blocks, 2 * rows, width // 4) for blocks in (8, 4, 2, 1)]
            shapes_of.append((4, rows, width // 4))
        return [pltpu.VMEM(shape, jnp.bfloat16) for shape in shapes_of] + [
            pltpu.SemaphoreType.DMA((count, 4)),
            pltpu.SemaphoreType.DMA((count, 4, 5)),
            pltpu.SemaphoreType.DMA((count, 4, 5)),
        ]

    def columns(self, job, quarter):
        width = self.shapes[job][1] // 4
        return pl.ds(quarter * width, width)

    def start(self, job):
        for quarter in range(4):
            columns = self.columns(job, quarter)
            for index in range(8):
                outer, inner = index // 4, index % 4
                there = block_place(quarter, outer + 2, inner, self.x, self.z)
                here = block_place(quarter, outer, inner, self.x, self.z)
                remote(
                    self.sources[job].at[there, :, columns],
                    self.landings[job][0].at[quarter, index],
                    self.send_sem.at[job, quarter, 0],
                    self.recv_sem.at[job, quarter, 0],
                    stage_partner(quarter, 0, self.x, self.z, self.seq),
                ).start()
                pltpu.make_async_copy(
                    self.sources[job].at[here, :, columns],
                    self.totals[job].at[quarter, index],
                    self.local_sem.at[job, quarter],
                ).start()

    def copy(self, job, quarter, stage):
        rows = self.shapes[job][0]
        target = self.landings[job][stage].at[quarter]
        if stage == 0:
            source = target
        elif stage < 4:
            size = 8 >> stage
            source = self.totals[job].at[quarter, pl.ds(size, size)]
        else:
            away = pl.multiple_of((1 - self.y) * rows, 16)
            source = self.totals[job].at[quarter, 0, pl.ds(away, rows)]
        return remote(
            source,
            target,
            self.send_sem.at[job, quarter, stage],
            self.recv_sem.at[job, quarter, stage],
            stage_partner(quarter, stage, self.x, self.z, self.seq),
        )

    def finish(self, job, stage):
        rows = self.shapes[job][0]
        for quarter in range(4):
            total = self.totals[job].at[quarter]
            landing = self.landings[job][stage].at[quarter]
            self.copy(job, quarter, stage).wait_recv()
            if stage == 0:
                pltpu.make_async_copy(total, total, self.local_sem.at[job, quarter]).wait()
            if stage < 4:
                add_blocks(8 >> stage, total, landing)
                self.copy(job, quarter, stage + 1).start()
            else:
                mine = pl.multiple_of(self.y * rows, 16)
                self.results[job][:, self.columns(job, quarter)] = total[
                    0, pl.ds(mine, rows)
                ].astype(jnp.float32) + landing[...].astype(jnp.float32)

    def drain(self):
        for job in range(len(self.shapes)):
            for quarter in range(4):
                for stage in range(5):
                    self.copy(job, quarter, stage).wait_send()


def reduce_kernel(shapes, *refs):
    count = len(shapes)
    refs = list(refs)
    take = lambda n: [refs.pop(0) for _ in range(n)]
    sources, vector = take(count), take(1)[0]
    results, vector_result = take(count), take(1)[0]
    vector_total, vector_landing, vector_send, vector_recv = take(4)
    halving = Halving(shapes, sources, results, refs)
    z, x, seq = place_here()
    core = {"seq": flip(seq, 1)}
    enter(ring_partners(z, x, seq) + [core])

    devices = [core] + [stage_partner(0, stage, x, z, seq) for stage in range(5)]
    vector_stages = list(zip(devices, (0, 8, 4, 2, 1, 0), (0, 16, 24, 28, 30, 31), (16, 8, 4, 2, 1, 1)))

    def vector_copy(step):
        device, first, landing, size = vector_stages[step]
        return remote(
            vector_total.at[pl.ds(first, size)],
            vector_landing.at[pl.ds(landing, size)],
            vector_send.at[step],
            vector_recv.at[step],
            device,
        )

    def vector_finish(step):
        _, _, landing, size = vector_stages[step]
        vector_copy(step).wait()
        vector_total[pl.ds(0, size)] += vector_landing[pl.ds(landing, size)]

    for index in range(16):
        vector_total[index] = vector[block_place(0, index // 4, index % 4, x, z)]
    vector_copy(0).start()
    for job in range(count):
        halving.start(job)
    for stage in range(5):
        for job in range(count):
            halving.finish(job, stage)
        vector_finish(stage)
        vector_copy(stage + 1).start()
    vector_finish(5)
    vector_result[...] = vector_total[0]
    halving.drain()


def reduce_shares(shares, vectors, collective_id):
    shapes = [(share.shape[1] // 2, share.shape[2]) for share in shares]
    count = len(shares)
    return pl.pallas_call(
        functools.partial(reduce_kernel, shapes),
        out_shape=[jax.ShapeDtypeStruct(shape, jnp.float32) for shape in shapes]
        + [jax.ShapeDtypeStruct(vectors.shape[1:], jnp.float32)],
        in_specs=[pl.BlockSpec(memory_space=pl.ANY)] * count
        + [pl.BlockSpec(memory_space=pltpu.VMEM)],
        out_specs=[pl.BlockSpec(memory_space=pltpu.VMEM)] * (count + 1),
        scratch_shapes=[
            pltpu.VMEM(vectors.shape, jnp.float32),
            pltpu.VMEM((32,) + vectors.shape[1:], jnp.float32),
            pltpu.SemaphoreType.DMA((6,)),
            pltpu.SemaphoreType.DMA((6,)),
        ]
        + Halving.scratch(shapes),
        compiler_params=pltpu.CompilerParams(
            collective_id=collective_id,
            has_side_effects=True,
            vmem_limit_bytes=56 * 2**20,
        ),
    )(*shares, vectors)


def attention_backward_pair(query, keys, values, share, inverse, grad, mixed, lows):
    span = keys.shape[0]
    here = query.shape[0]
    chunk = 128
    lane = lax.broadcasted_iota(jnp.int32, query.shape, 1)
    zero = jnp.zeros(query.shape, query.dtype)
    queries = jnp.concatenate(
        [jnp.where(lane < 64, query, zero), jnp.where(lane >= 64, query, zero)], axis=0
    )
    turned = grad.astype(jnp.float32).T
    product = turned * mixed.astype(jnp.float32).T
    first = turned[:64] * inverse[:, :here]
    second = turned[64:] * inverse[:, here:]
    none = jnp.zeros_like(first)
    grads = jnp.concatenate(
        [jnp.concatenate([first, none], axis=1), jnp.concatenate([none, second], axis=1)], axis=0
    ).astype(jnp.bfloat16)
    grads_back = grads.T
    centre = inverse * jnp.concatenate(
        [
            jnp.sum(product[:64], axis=0, keepdims=True),
            jnp.sum(product[64:], axis=0, keepdims=True),
        ],
        axis=1,
    )
    grad_keys, grad_values = [], []
    for index in range(span // chunk):
        rows = pl.ds(index * chunk, chunk)
        part = share[rows]
        grad_share = project(values[rows], grads)
        grad_score = (part.astype(jnp.float32) * (grad_share - centre)).astype(jnp.bfloat16)
        lows[rows] = grad_score
        grad_keys.append((project(grad_score, queries) * LN2).astype(jnp.bfloat16))
        grad_values.append(project(part, grads_back).astype(jnp.bfloat16))
    out = rows_product(keys[...], lows[...])
    out = jnp.concatenate([out[:64, :here], out[64:, here:]], axis=0)
    return (out.T * 0.125).astype(jnp.bfloat16), grad_keys, grad_values


def backward_kernel(
    shapes, query, keys, values, shares, inverses, grad, mixed, share_one, share_two, share_three,
    grad_query, both, result_one, result_two, result_three,
    lows, held, held_sem, parts, landing, swap_send, swap_recv, *halving_refs,
):
    halving = Halving(
        shapes,
        (share_one, share_two, share_three),
        (result_one, result_two, result_three),
        halving_refs,
    )
    z, x, seq = place_here()
    core = {"seq": flip(seq, 1)}
    pairs = shares.shape[0]
    here, width = query.shape

    def fetch(pair):
        slot = lax.rem(pair, 2)
        return pltpu.make_async_copy(shares.at[pair], held.at[slot], held_sem.at[slot])

    fetch(0).start()
    enter(ring_partners(z, x, seq) + [core])
    for job in range(3):
        halving.start(job)

    def one_pair(pair, carry):
        @pl.when(pair + 1 < pairs)
        def _():
            fetch(pair + 1).start()

        fetch(pair).wait()
        columns = pl.ds(pl.multiple_of(pair * 128, 128), 128)
        others = pl.ds(pl.multiple_of(width + pair * 128, 128), 128)
        out, grad_keys, grad_values = attention_backward_pair(
            query[:, columns],
            keys.at[:, columns],
            values.at[:, columns],
            held.at[lax.rem(pair, 2)],
            inverses[pair],
            grad[:, columns],
            mixed[:, columns],
            lows,
        )
        grad_query[:, columns] = out
        for index, (one, two) in enumerate(zip(grad_keys, grad_values)):
            part, rows = index * 128 // here, pl.ds(index * 128 % here, 128)
            parts[part, rows, columns] = one
            parts[part, rows, others] = two
        for step in range(2):
            for place in (columns, others):
                remote(
                    parts.at[2 * step + 1, :, place],
                    landing.at[step, :, place],
                    swap_send,
                    swap_recv,
                    core,
                ).start()
        return carry

    lax.fori_loop(0, 5, one_pair, 0)
    halving.finish(0, 0)
    lax.fori_loop(5, pairs, one_pair, 0)
    swapped = remote(landing, landing, swap_send, swap_recv, core)
    swapped.wait_recv()
    for step in range(2):
        both[step] = (
            parts[2 * step].astype(jnp.float32) + landing[step].astype(jnp.float32)
        ).astype(jnp.bfloat16)
    for job in (1, 2):
        halving.finish(job, 0)
    for stage in range(1, 5):
        for job in range(3):
            halving.finish(job, stage)
    halving.drain()
    swapped.wait_send()


def backward(query, keys, values, shares, inverses, grad, mixed, weights, collective_id):
    here, width = query.shape
    span = keys.shape[0]
    shapes = [(share.shape[1] // 2, share.shape[2]) for share in weights]
    inside = pl.BlockSpec(memory_space=pltpu.VMEM)
    outside = pl.BlockSpec(memory_space=pl.ANY)
    return pl.pallas_call(
        functools.partial(backward_kernel, shapes),
        in_specs=[inside, inside, inside, outside, inside, inside, inside] + [outside] * 3,
        out_specs=[inside] * 5,
        out_shape=[
            jax.ShapeDtypeStruct((here, width), jnp.bfloat16),
            jax.ShapeDtypeStruct((2, here, 2 * width), jnp.bfloat16),
        ]
        + [jax.ShapeDtypeStruct(shape, jnp.float32) for shape in shapes],
        scratch_shapes=[
            pltpu.VMEM((span, 2 * here), jnp.bfloat16),
            pltpu.VMEM((2, span, 2 * here), jnp.bfloat16),
            pltpu.SemaphoreType.DMA((2,)),
            pltpu.VMEM((4, here, 2 * width), jnp.bfloat16),
            pltpu.VMEM((2, here, 2 * width), jnp.bfloat16),
            pltpu.SemaphoreType.DMA,
            pltpu.SemaphoreType.DMA,
        ]
        + Halving.scratch(shapes),
        compiler_params=pltpu.CompilerParams(
            collective_id=collective_id,
            has_side_effects=True,
            vmem_limit_bytes=56 * 2**20,
        ),
    )(query, keys, values, shares, inverses, grad, mixed, *weights)


def attention_forward_kernel(
    query, keys, values, key_places, key_segments, query_places, query_segments, slopes,
    shares, mixed, inverses, distance, scores,
):
    span = keys.shape[0]
    chunk = 128
    here = query.shape[0]

    @pl.when(pl.program_id(0) == 0)
    def _():
        gap = jnp.abs(query_places[...] - key_places[...]).astype(jnp.float32)
        same = query_segments[...] == key_segments[...]
        distance[...] = jnp.where(same, gap, 1e30)

    lane = lax.broadcasted_iota(jnp.int32, query.shape, 1)
    zero = jnp.zeros(query.shape, query.dtype)
    both = jnp.concatenate(
        [jnp.where(lane < 64, query[...], zero), jnp.where(lane >= 64, query[...], zero)], axis=0
    )
    slope = slopes[0]

    def raw(index, top):
        rows = pl.ds(pl.multiple_of(index * chunk, chunk), chunk)
        part = back_product(keys[rows], both)
        gap = distance[rows]
        part = part - slope * jnp.concatenate([gap, gap], axis=1)
        scores[rows] = part
        return jnp.maximum(top, jnp.max(part.reshape(chunk // 8, 8, 2 * here), axis=0))

    top = lax.fori_loop(
        0, span // chunk, raw, jnp.full((8, 2 * here), -jnp.inf, jnp.float32), unroll=True
    )
    top = jnp.max(top, axis=0, keepdims=True)

    def exponent(index, carry):
        rows = pl.ds(pl.multiple_of(index * chunk, chunk), chunk)
        shares[0, rows] = jnp.exp2(scores[rows] - top).astype(jnp.bfloat16)
        return carry

    lax.fori_loop(0, span // chunk, exponent, 0, unroll=True)
    turned = jnp.concatenate([values[...].T, jnp.ones((16, span), jnp.bfloat16)], axis=0)
    out = project(turned, shares[0])
    inverse = 1.0 / out[128:129]
    inverses[0] = inverse
    out = out[:128] * inverse
    out = jnp.concatenate([out[:64, :here], out[64:, here:]], axis=0)
    mixed[...] = out.T.astype(jnp.bfloat16)


def attention_forward(query, keys, values, tables, slopes):
    here, width = query.shape
    span = keys.shape[0]
    pairs = width // 128
    whole = lambda a: pl.BlockSpec(a.shape, lambda i: (0,) * a.ndim)
    return pl.pallas_call(
        attention_forward_kernel,
        grid=(pairs,),
        in_specs=[
            pl.BlockSpec((here, 128), lambda i: (0, i)),
            pl.BlockSpec((span, 128), lambda i: (0, i)),
            pl.BlockSpec((span, 128), lambda i: (0, i)),
            *[whole(table) for table in tables],
            pl.BlockSpec((1, 1, 2 * here), lambda i: (i, 0, 0)),
        ],
        out_specs=[
            pl.BlockSpec((1, span, 2 * here), lambda i: (i, 0, 0)),
            pl.BlockSpec((here, 128), lambda i: (0, i)),
            pl.BlockSpec((1, 1, 2 * here), lambda i: (i, 0, 0)),
        ],
        out_shape=[
            jax.ShapeDtypeStruct((pairs, span, 2 * here), jnp.bfloat16),
            jax.ShapeDtypeStruct((here, width), jnp.bfloat16),
            jax.ShapeDtypeStruct((pairs, 1, 2 * here), jnp.float32),
        ],
        scratch_shapes=[
            pltpu.VMEM((span, here), jnp.float32),
            pltpu.VMEM((span, 2 * here), jnp.float32),
        ],
        compiler_params=pltpu.CompilerParams(vmem_limit_bytes=40 * 2**20),
    )(query, keys, values, *tables, slopes)


def mean_rows(value):
    return jnp.mean(value, axis=-1, keepdims=True)


def ffn_kernel(
    core, hidden, mixed, grad_low, w_out, gain, bias, w_up, w_down,
    output, act_kept, act_sent, two_kept, two_sent, grad_up, grad_attn, grad_mixed, gain_sum, bias_sum,
    residual, unit, inverse, normed, total, grad_normed, turned,
):
    step = pl.program_id(0)
    last = pl.num_programs(0) - 1
    here = hidden.shape[0]
    mine = core[0]
    root = 0.7071067811865476

    @pl.when(step == 0)
    def _():
        value = hidden[...] + project(mixed[...], w_out[...])
        center = value - mean_rows(value)
        scale = lax.rsqrt(mean_rows(center * center) + EPS)
        residual[...] = value
        unit[...] = center * scale
        inverse[...] = scale
        two = (unit[...] * gain[...] + bias[...]).astype(jnp.bfloat16)
        normed[...] = two
        total[...] = jnp.zeros_like(total)
        grad_normed[...] = jnp.zeros_like(grad_normed)
        turned[...] = two.T

        def split(index, carry):
            place = pl.ds(pl.multiple_of(index * 16, 16), 16)
            two_kept[place] = turned[pl.ds(pl.multiple_of(index * 32 + mine * 16, 16), 16)]
            two_sent[place] = turned[pl.ds(pl.multiple_of(index * 32 + (1 - mine) * 16, 16), 16)]
            return carry

        lax.fori_loop(0, two_kept.shape[0] // 16, split, 0)

    upward = project(normed[...], w_up[...])
    cdf = 0.5 * (1.0 + lax.erf(upward * root))
    act = (upward * cdf).astype(jnp.bfloat16)
    density = jnp.exp(upward * upward * -0.5) * 0.3989422804014327
    slope = cdf + upward * density
    back = back_product(grad_low[...], w_down[...])
    grad = (back * slope).astype(jnp.bfloat16)
    grad_up[...] = grad
    total[...] += project(act, w_down[...])
    grad_normed[...] += back_product(grad, w_up[...])
    width = act.shape[1]
    turned[pl.ds(0, width)] = act.T
    for index in range(width // 128):
        place = pl.ds(index * 64, 64)
        act_kept[place] = turned[pl.ds(pl.multiple_of(index * 128 + mine * 64, 64), 64)]
        act_sent[place] = turned[pl.ds(pl.multiple_of(index * 128 + (1 - mine) * 64, 64), 64)]

    @pl.when(step == last)
    def _():
        output[...] = (residual[...] + total[...]).astype(jnp.bfloat16)
        grads = grad_normed[...]
        scaled = grads * gain[...]
        units = unit[...]
        step_one = scaled - mean_rows(scaled) - units * mean_rows(scaled * units)
        value = grad_low[...].astype(jnp.float32) + inverse[...] * step_one
        gain_sum[...] = jnp.sum(grads * units, axis=0, keepdims=True)
        bias_sum[...] = jnp.sum(grads, axis=0, keepdims=True)
        grad_attn[...] = value
        grad_mixed[...] = back_product(value.astype(jnp.bfloat16), w_out[...]).astype(jnp.bfloat16)


def feed_forward(core, hidden, mixed, grad_low, w_out, gain, bias, w_up, w_down):
    here, width = hidden.shape
    full = w_up.shape[1]
    block = 512
    whole = lambda shape: pl.BlockSpec(shape, lambda i: (0,) * len(shape))
    return pl.pallas_call(
        ffn_kernel,
        grid=(full // block,),
        in_specs=[
            pl.BlockSpec(memory_space=pltpu.SMEM),
            whole((here, width)),
            whole((here, width)),
            whole((here, width)),
            whole((width, width)),
            whole((1, width)),
            whole((1, width)),
            pl.BlockSpec((width, block), lambda i: (0, i)),
            pl.BlockSpec((block, width), lambda i: (i, 0)),
        ],
        out_specs=[
            whole((here, width)),
            pl.BlockSpec((block // 2, here), lambda i: (i, 0)),
            pl.BlockSpec((block // 2, here), lambda i: (i, 0)),
            whole((width // 2, here)),
            whole((width // 2, here)),
            pl.BlockSpec((here, block), lambda i: (0, i)),
            whole((here, width)),
            whole((here, width)),
            whole((1, width)),
            whole((1, width)),
        ],
        out_shape=[
            jax.ShapeDtypeStruct((here, width), jnp.bfloat16),
            jax.ShapeDtypeStruct((full // 2, here), jnp.bfloat16),
            jax.ShapeDtypeStruct((full // 2, here), jnp.bfloat16),
            jax.ShapeDtypeStruct((width // 2, here), jnp.bfloat16),
            jax.ShapeDtypeStruct((width // 2, here), jnp.bfloat16),
            jax.ShapeDtypeStruct((here, full), jnp.bfloat16),
            jax.ShapeDtypeStruct((here, width), jnp.float32),
            jax.ShapeDtypeStruct((here, width), jnp.bfloat16),
            jax.ShapeDtypeStruct((1, width), jnp.float32),
            jax.ShapeDtypeStruct((1, width), jnp.float32),
        ],
        scratch_shapes=[
            pltpu.VMEM((here, width), jnp.float32),
            pltpu.VMEM((here, width), jnp.float32),
            pltpu.VMEM((here, 1), jnp.float32),
            pltpu.VMEM((here, width), jnp.bfloat16),
            pltpu.VMEM((here, width), jnp.float32),
            pltpu.VMEM((here, width), jnp.float32),
            pltpu.VMEM((width, here), jnp.bfloat16),
        ],
        compiler_params=pltpu.CompilerParams(vmem_limit_bytes=48 * 2**20),
    )(core, hidden, mixed, grad_low, w_out, gain, bias, w_up, w_down)


def on_device(
    states,
    mirror,
    w_skip,
    norm1_gain,
    norm1_bias,
    w_query,
    w_key,
    w_value,
    w_out,
    norm2_gain,
    norm2_bias,
    w_up,
    w_down,
    out_grad,
    lengths,
    infill_spans,
):
    rows_here = states.shape[2]
    model_width = states.shape[3]
    head_count = HEADS
    head_dim = model_width // head_count
    query_scale = head_dim ** (-0.5) * LOG2E
    seq = lax.axis_index("seq")
    own_rows = states.reshape(rows_here, model_width)
    stored = mirror.reshape(rows_here, model_width)
    partner = from_partner(stored, "section", 0)
    lengths_row = lengths.reshape(-1)
    spans_row = infill_spans.reshape(-1, 2)
    row_length = rows_here * lax.axis_size("seq")
    local = jnp.arange(rows_here, dtype=jnp.int32)
    query_place = seq * rows_here + local
    key_place = jnp.concatenate([(seq ^ step) * rows_here + local for step in range(4)])
    query_segment, inside = segment_tables(lengths_row, spans_row, query_place)
    key_segment = segment_tables(lengths_row, spans_row, key_place)[0]
    tables = (key_place[:, None], key_segment[:, None], query_place[None], query_segment[None])
    slopes = 2.0 ** (-8.0 * (jnp.arange(head_count, dtype=jnp.float32) + 1.0) / head_count)
    slopes = jnp.repeat(LOG2E * slopes.reshape(-1, 2), rows_here, axis=1)[:, None, :]
    gain_one = norm1_gain.astype(jnp.float32)
    bias_one = norm1_bias.astype(jnp.float32)
    w_first = w_skip[:model_width]
    w_second = w_skip[model_width:]
    core = seq % 2
    select_mine = core_selector(core, model_width)
    select_other = core_selector(1 - core, model_width)

    grad_low = jnp.where(
        inside[:, None], out_grad.reshape(rows_here, model_width), jnp.bfloat16(0)
    )
    grad_low_other = swap_core(grad_low)
    hidden = project(own_rows, w_first) + project(partner, w_second)
    normed_one, unit_one, inverse_one = norm_forward(hidden, gain_one, bias_one)
    normed_one = low(normed_one)
    far = partner_of(normed_one, "seq", 2)
    near = swap_core(normed_one)
    far_near = swap_core(far)
    normed_all = jnp.concatenate([normed_one, near, far, far_near], axis=0)
    query = low(project(normed_one, w_query) * query_scale)
    keys_all = low(project(normed_all, w_key))
    values_all = low(project(normed_all, w_value))
    shares, mixed_rows, inverses = attention_forward(query, keys_all, values_all, tables, slopes)
    (
        output,
        act_mine,
        act_send,
        two_mine,
        two_send,
        grad_upward,
        grad_residual,
        grad_mixed,
        grad_gain_two,
        grad_bias_two,
    ) = feed_forward(
        core.reshape(1),
        hidden,
        mixed_rows,
        grad_low,
        w_out,
        norm2_gain.astype(jnp.float32)[None],
        norm2_bias.astype(jnp.float32)[None],
        w_up,
        w_down,
    )
    output = output.reshape(states.shape)
    grad_upward_other = swap_core(grad_upward)

    act_other = swap_core(act_send)
    down_share = pair_product(act_mine, act_other, grad_low, grad_low_other)
    two_other = swap_core(two_send)
    up_share = pair_product(two_mine, two_other, grad_upward, grad_upward_other)
    grad_attn = low(grad_residual)
    grad_attn_other = swap_core(grad_attn)
    mixed_mine = low(back_product(select_mine, mixed_rows))
    mixed_other = swap_core(low(back_product(select_other, mixed_rows)))
    out_share = pair_product(mixed_mine, mixed_other, grad_attn, grad_attn_other)
    grad_query, both_mine, down_sum, up_sum, out_sum = backward(
        query,
        keys_all,
        values_all,
        shares,
        inverses,
        grad_mixed,
        mixed_rows,
        [down_share, up_share, out_share],
        1,
    )
    both_mine = both_mine.reshape(2 * rows_here, 2 * model_width)
    both_far = swap_core(both_mine)
    grad_query_other = swap_core(grad_query)
    w_both = jnp.concatenate([w_key, w_value], axis=1)
    normed_part = back_product(both_mine, w_both)
    normed_far = partner_of(low(normed_part[rows_here:]), "seq", 2)
    grad_normed_one = (
        back_product(grad_query, w_query)
        + normed_part[:rows_here]
        + normed_far.astype(jnp.float32)
    )
    one_rows = low(back_product(select_mine, normed_all))
    query_share = low(
        project(one_rows[:, : 2 * rows_here], jnp.concatenate([grad_query, grad_query_other], axis=0))
    )
    both_rows = jnp.concatenate(
        [both_mine[:rows_here], both_far[:rows_here], both_mine[rows_here:], both_far[rows_here:]],
        axis=0,
    )
    both_share = low(project(one_rows, both_rows))

    grad_hidden_norm, grad_gain_one, grad_bias_one = norm_backward(
        grad_normed_one, unit_one, inverse_one, gain_one
    )
    grad_hidden = low(grad_residual + grad_hidden_norm)
    grad_hidden_other = swap_core(grad_hidden)
    grad_partner = low(back_product(grad_hidden, w_second))
    grad_stored = from_partner(grad_partner, "section", 0)
    grad_own = low(back_product(grad_hidden, w_first))
    joined = jnp.concatenate([own_rows, partner], axis=1)
    joined_mine = low(back_product(core_selector(core, 2 * model_width), joined))
    joined_other = swap_core(low(back_product(core_selector(1 - core, 2 * model_width), joined)))
    skip_share = pair_product(joined_mine, joined_other, grad_hidden, grad_hidden_other)
    vectors = jnp.stack(
        [grad_gain_one, grad_bias_one, grad_gain_two[0], grad_bias_two[0]]
    )
    vectors = vectors.reshape(4, 16, 4, 16).transpose(1, 2, 0, 3).reshape(16, 4, 64)
    vectors = jnp.pad(vectors, ((0, 0), (0, 4), (0, 64)))
    query_sum, both_sum, skip_sum, sums = reduce_shares(
        [by_dp(query_share), by_dp(both_share), skip_share], vectors, 2
    )
    sums = lax.dynamic_index_in_dim(sums, seq, 0, False)[:64].reshape(4, 16)
    return (
        output,
        grad_own.reshape(states.shape),
        grad_stored.reshape(states.shape),
        skip_sum[None],
        sums[0][None],
        sums[1][None],
        query_sum[None],
        both_sum[None, :, :model_width],
        both_sum[None, :, model_width:],
        out_sum[None],
        sums[2][None],
        sums[3][None],
        up_sum[None],
        down_sum[None],
    )


def solution(mesh):
    in_specs = (
        P("section", "dp", "seq", None),
        P("section", "dp", "seq", None),
        P(),
        P(),
        P(),
        P(),
        P(),
        P(),
        P(),
        P(),
        P(),
        P(),
        P(),
        P("section", "dp", "seq", None),
        P("section", "dp", None),
        P("section", "dp", None, None),
    )
    out_specs = (
        P("section", "dp", "seq", None),
        P("section", "dp", "seq", None),
        P("section", "dp", "seq", None),
        P("section", ("dp", "seq"), None),
        P("section", ("dp", "seq")),
        P("section", ("dp", "seq")),
        P("section", ("dp", "seq"), None),
        P("section", ("dp", "seq"), None),
        P("section", ("dp", "seq"), None),
        P("section", ("dp", "seq"), None),
        P("section", ("dp", "seq")),
        P("section", ("dp", "seq")),
        P("section", ("dp", "seq"), None),
        P("section", ("dp", "seq"), None),
    )
    return jax.shard_map(
        on_device, mesh=mesh, in_specs=in_specs, out_specs=out_specs, check_vma=False
    )
```

```python
import functools

import jax
import jax.numpy as jnp
from jax.experimental import pallas as pl
from jax.experimental.pallas import tpu as pltpu
from jax import lax
from jax.sharding import PartitionSpec as P

HEADS = 16
LOG2E = 1.4426950408889634
LN2 = 0.6931471805599453


EPS = 1e-05


def from_partner(value, axis, stride):
    mask = 2**stride
    pairs = [(source, source ^ mask) for source in range(lax.axis_size(axis))]
    return lax.ppermute(value, axis, pairs)


def project(left, right):
    return jnp.dot(left, right, preferred_element_type=jnp.float32)


def rows_product(left, right):
    return lax.dot_general(
        left, right, (((0,), (0,)), ((), ())), preferred_element_type=jnp.float32
    )


def back_product(left, right):
    return lax.dot_general(
        left, right, (((1,), (1,)), ((), ())), preferred_element_type=jnp.float32
    )


def norm_forward(hidden, gain, bias):
    center = hidden - jnp.mean(hidden, axis=-1, keepdims=True)
    variance = jnp.mean(center * center, axis=-1, keepdims=True)
    inverse = lax.rsqrt(variance + EPS)
    unit = center * inverse
    return (unit * gain + bias, unit, inverse)


def segment_tables(lengths_row, spans_row, places):
    ends = jnp.cumsum(lengths_row, dtype=jnp.int32)
    starts = ends - lengths_row
    segment = jnp.sum((places[:, None] >= ends[None, :]).astype(jnp.int32), axis=1)
    lower = starts + spans_row[:, 0]
    upper = starts + spans_row[:, 1]
    inside = jnp.any(
        (places[:, None] >= lower[None, :]) & (places[:, None] < upper[None, :]), axis=1
    )
    return (segment, inside)


def partner_of(value, axis, mask):
    pairs = [(source, source ^ mask) for source in range(lax.axis_size(axis))]
    return lax.ppermute(value, axis, pairs)


def core_selector(core, rows):
    piece = rows // 64
    target = jnp.arange(rows // 2, dtype=jnp.int32)
    source = (target // piece) * (2 * piece) + core * piece + target % piece
    return (source[:, None] == jnp.arange(rows, dtype=jnp.int32)[None, :]).astype(jnp.bfloat16)


def swap_core(value):
    return partner_of(value, "seq", 1)


def low(value):
    return value.astype(jnp.bfloat16)


def pair_product(kept, swapped, grad, grad_swapped):
    left = jnp.concatenate([kept, swapped], axis=1)
    right = jnp.concatenate([grad, grad_swapped], axis=0)
    return by_dp(low(project(left, right)))


def by_dp(value):
    return value.reshape(16, value.shape[0] // 16, value.shape[1])


MESH = pl.DeviceIdType.MESH
NEAR, WRAP = (0, 3, 1, 2), (0, 1, 3, 2)
QUARTERS = (("x", NEAR), ("x", WRAP), ("z", NEAR), ("z", WRAP))


def flip(value, mask):
    if mask == 1:
        return value + 1 - 2 * lax.rem(value, 2)
    if mask == 2:
        return lax.rem(value + 2, 4)
    if mask == 3:
        return 3 - value
    return value


def block_place(quarter, outer, inner, x, z):
    first, order = QUARTERS[quarter]
    if first == "x":
        return flip(z, order[inner]) * 4 + flip(x, order[outer])
    return flip(z, order[outer]) * 4 + flip(x, order[inner])


def stage_partner(quarter, stage, x, z, seq):
    if stage == 4:
        return {"seq": lax.rem(seq + 2, 4)}
    first, order = QUARTERS[quarter]
    mask = order[2] if stage % 2 == 0 else order[1]
    if (first == "x") == (stage < 2):
        return {"dp": z * 4 + flip(x, mask)}
    return {"dp": flip(z, mask) * 4 + x}


def remote(source, target, send, recv, device):
    return pltpu.make_async_remote_copy(
        src_ref=source,
        dst_ref=target,
        send_sem=send,
        recv_sem=recv,
        device_id=device,
        device_id_type=MESH,
    )


def enter(devices):
    barrier = pltpu.get_barrier_semaphore()
    for device in devices:
        pl.semaphore_signal(barrier, inc=1, device_id=device, device_id_type=MESH)
    pl.semaphore_wait(barrier, len(devices))


def add_blocks(count, total, other):
    def one(index, carry):
        total[index] = (
            total[index].astype(jnp.float32) + other[index].astype(jnp.float32)
        ).astype(jnp.bfloat16)
        return carry

    lax.fori_loop(0, count, one, 0)


def place_here():
    dp, seq = lax.axis_index("dp"), lax.axis_index("seq")
    return lax.div(dp, 4), lax.rem(dp, 4), seq


def ring_partners(z, x, seq):
    pairs = ((0, 0), (0, 1), (2, 0), (2, 1), (0, 4))
    return [stage_partner(quarter, stage, x, z, seq) for quarter, stage in pairs]


def relative_place(quarter, z, x, z_there, x_there):
    first, order = QUARTERS[quarter]

    def position(value):
        if order == NEAR:
            return 2 * value - lax.div(value, 2) - 4 * lax.div(value, 3)
        return value + lax.div(value, 2) * (1 - 2 * lax.rem(value, 2))

    z_place, x_place = position(flip(z, z_there)), position(flip(x, x_there))
    return x_place * 4 + z_place if first == "x" else z_place * 4 + x_place


class Halving:
    def __init__(self, shapes, sources, results, scratch):
        self.shapes, self.sources, self.results = shapes, sources, results
        scratch = list(scratch)
        count = len(shapes)
        self.work = scratch[:count]
        self.landings = [scratch[count + 5 * job : count + 5 * job + 5] for job in range(count)]
        self.local_sem, self.send_sem, self.recv_sem = scratch[6 * count :]
        self.z, self.x, self.seq = place_here()
        self.y = lax.div(self.seq, 2)

    @staticmethod
    def scratch(shapes, made):
        count = len(shapes)
        shapes_of = [
            (4, 16 if own else 8, 2 * rows, width // 4) for (rows, width), own in zip(shapes, made)
        ]
        for rows, width in shapes:
            shapes_of += [(4, blocks, 2 * rows, width // 4) for blocks in (8, 4, 2, 1)]
            shapes_of.append((4, rows, width // 4))
        return [pltpu.VMEM(shape, jnp.bfloat16) for shape in shapes_of] + [
            pltpu.SemaphoreType.DMA((count, 4)),
            pltpu.SemaphoreType.DMA((count, 4, 5)),
            pltpu.SemaphoreType.DMA((count, 4, 5)),
        ]

    def start(self, job):
        width = self.shapes[job][1] // 4
        for quarter in range(4):
            columns = pl.ds(quarter * width, width)
            for index in range(8):
                outer, inner = index // 4, index % 4
                there = block_place(quarter, outer + 2, inner, self.x, self.z)
                here = block_place(quarter, outer, inner, self.x, self.z)
                remote(
                    self.sources[job].at[there, :, columns],
                    self.landings[job][0].at[quarter, index],
                    self.send_sem.at[job, quarter, 0],
                    self.recv_sem.at[job, quarter, 0],
                    stage_partner(quarter, 0, self.x, self.z, self.seq),
                ).start()
                pltpu.make_async_copy(
                    self.sources[job].at[here, :, columns],
                    self.work[job].at[quarter, index],
                    self.local_sem.at[job, quarter],
                ).start()

    def store(self, job, quarter, value):
        rows = 2 * self.shapes[job][0]
        for index in range(16):
            place = relative_place(quarter, self.z, self.x, index // 4, index % 4)
            self.work[job][quarter, place] = value[index * rows : (index + 1) * rows].astype(
                jnp.bfloat16
            )
        self.copy(job, quarter, 0).start()

    def copy(self, job, quarter, stage):
        rows = self.shapes[job][0]
        target = self.landings[job][stage].at[quarter]
        if stage == 0:
            made = self.sources[job] is None
            source = self.work[job].at[quarter, pl.ds(8, 8)] if made else target
        elif stage < 4:
            size = 8 >> stage
            source = self.work[job].at[quarter, pl.ds(size, size)]
        else:
            away = pl.multiple_of((1 - self.y) * rows, 16)
            source = self.work[job].at[quarter, 0, pl.ds(away, rows)]
        return remote(
            source,
            target,
            self.send_sem.at[job, quarter, stage],
            self.recv_sem.at[job, quarter, stage],
            stage_partner(quarter, stage, self.x, self.z, self.seq),
        )

    def finish(self, job, stage):
        rows, width = self.shapes[job]
        for quarter in range(4):
            work = self.work[job].at[quarter]
            landing = self.landings[job][stage].at[quarter]
            self.copy(job, quarter, stage).wait_recv()
            if stage == 0 and self.sources[job] is not None:
                pltpu.make_async_copy(landing, work, self.local_sem.at[job, quarter]).wait()
            if stage < 4:
                add_blocks(8 >> stage, work, landing)
                self.copy(job, quarter, stage + 1).start()
            else:
                mine = pl.multiple_of(self.y * rows, 16)
                total = work[0, pl.ds(mine, rows)].astype(jnp.float32)
                first = quarter * width // 4
                result = self.results[job][first // 4096 if width == 4096 else first // 1024]
                result[:, pl.ds(first % result.shape[1], width // 4)] = total + landing[
                    ...
                ].astype(jnp.float32)

    def drain(self):
        for job in range(len(self.shapes)):
            for quarter in range(4):
                for stage in range(5):
                    self.copy(job, quarter, stage).wait_send()


def attention_backward_pair(query, keys, values, share, inverse, grad, mixed, lows):
    span = keys.shape[0]
    here = query.shape[0]
    chunk = 128
    lane = lax.broadcasted_iota(jnp.int32, query.shape, 1)
    zero = jnp.zeros(query.shape, query.dtype)
    queries = jnp.concatenate(
        [jnp.where(lane < 64, query, zero), jnp.where(lane >= 64, query, zero)], axis=0
    )
    turned = grad.astype(jnp.float32).T
    product = turned * mixed.astype(jnp.float32).T
    first = turned[:64] * inverse[:, :here]
    second = turned[64:] * inverse[:, here:]
    none = jnp.zeros_like(first)
    grads = jnp.concatenate(
        [jnp.concatenate([first, none], axis=1), jnp.concatenate([none, second], axis=1)], axis=0
    ).astype(jnp.bfloat16)
    grads_back = grads.T
    centre = inverse * jnp.concatenate(
        [
            jnp.sum(product[:64], axis=0, keepdims=True),
            jnp.sum(product[64:], axis=0, keepdims=True),
        ],
        axis=1,
    )
    grad_keys, grad_values = [], []
    for index in range(span // chunk):
        rows = pl.ds(index * chunk, chunk)
        part = share[rows]
        grad_share = project(values[rows], grads)
        grad_score = (part.astype(jnp.float32) * (grad_share - centre)).astype(jnp.bfloat16)
        lows[rows] = grad_score
        grad_keys.append((project(grad_score, queries) * LN2).astype(jnp.bfloat16))
        grad_values.append(project(part, grads_back).astype(jnp.bfloat16))
    out = rows_product(keys[...], lows[...])
    out = jnp.concatenate([out[:64, :here], out[64:, here:]], axis=0)
    return (out.T * 0.125).astype(jnp.bfloat16), grad_keys, grad_values


def attention_forward_kernel(
    query, keys, values, key_places, key_segments, query_places, query_segments, slopes,
    shares, mixed, inverses, distance, scores,
):
    span = keys.shape[0]
    chunk = 128
    here = query.shape[0]

    @pl.when(pl.program_id(0) == 0)
    def _():
        gap = jnp.abs(query_places[...] - key_places[...]).astype(jnp.float32)
        same = query_segments[...] == key_segments[...]
        distance[...] = jnp.where(same, gap, 1e30)

    lane = lax.broadcasted_iota(jnp.int32, query.shape, 1)
    zero = jnp.zeros(query.shape, query.dtype)
    both = jnp.concatenate(
        [jnp.where(lane < 64, query[...], zero), jnp.where(lane >= 64, query[...], zero)], axis=0
    )
    slope = slopes[0]

    def raw(index, top):
        rows = pl.ds(pl.multiple_of(index * chunk, chunk), chunk)
        part = back_product(keys[rows], both)
        gap = distance[rows]
        part = part - slope * jnp.concatenate([gap, gap], axis=1)
        scores[rows] = part
        return jnp.maximum(top, jnp.max(part.reshape(chunk // 8, 8, 2 * here), axis=0))

    top = lax.fori_loop(
        0, span // chunk, raw, jnp.full((8, 2 * here), -jnp.inf, jnp.float32), unroll=True
    )
    top = jnp.max(top, axis=0, keepdims=True)

    def exponent(index, carry):
        rows = pl.ds(pl.multiple_of(index * chunk, chunk), chunk)
        shares[0, rows] = jnp.exp2(scores[rows] - top).astype(jnp.bfloat16)
        return carry

    lax.fori_loop(0, span // chunk, exponent, 0, unroll=True)
    turned = jnp.concatenate([values[...].T, jnp.ones((16, span), jnp.bfloat16)], axis=0)
    out = project(turned, shares[0])
    inverse = 1.0 / out[128:129]
    inverses[0] = inverse
    out = out[:128] * inverse
    out = jnp.concatenate([out[:64, :here], out[64:, here:]], axis=0)
    mixed[...] = out.T.astype(jnp.bfloat16)


def attention_forward(query, keys, values, tables, slopes):
    here, width = query.shape
    span = keys.shape[0]
    pairs = width // 128
    whole = lambda a: pl.BlockSpec(a.shape, lambda i: (0,) * a.ndim)
    return pl.pallas_call(
        attention_forward_kernel,
        grid=(pairs,),
        in_specs=[
            pl.BlockSpec((here, 128), lambda i: (0, i)),
            pl.BlockSpec((span, 128), lambda i: (0, i)),
            pl.BlockSpec((span, 128), lambda i: (0, i)),
            *[whole(table) for table in tables],
            pl.BlockSpec((1, 1, 2 * here), lambda i: (i, 0, 0)),
        ],
        out_specs=[
            pl.BlockSpec((1, span, 2 * here), lambda i: (i, 0, 0)),
            pl.BlockSpec((here, 128), lambda i: (0, i)),
            pl.BlockSpec((1, 1, 2 * here), lambda i: (i, 0, 0)),
        ],
        out_shape=[
            jax.ShapeDtypeStruct((pairs, span, 2 * here), jnp.bfloat16),
            jax.ShapeDtypeStruct((here, width), jnp.bfloat16),
            jax.ShapeDtypeStruct((pairs, 1, 2 * here), jnp.float32),
        ],
        scratch_shapes=[
            pltpu.VMEM((span, here), jnp.float32),
            pltpu.VMEM((span, 2 * here), jnp.float32),
        ],
        compiler_params=pltpu.CompilerParams(vmem_limit_bytes=40 * 2**20),
    )(query, keys, values, *tables, slopes)


def backward_kernel(
    shapes, query, keys, values, shares, inverses, grad, mixed, share_one, share_two, share_three,
    w_query, w_key, w_value, w_skip, one_rows, joined_kept, joined_other, unit, grad_residual,
    inverse_one, gain_one, gain_two_sum, bias_two_sum,
    grad_own, grad_stored, vectors, *refs,
):
    refs = list(refs)
    take = lambda n: [refs.pop(0) for _ in range(n)]
    results = [take(1), take(1), take(1), take(1), take(2), take(1)]
    lows, held, held_sem, parts, landing, swap_send, swap_recv = take(7)
    far_landing, grad_query, query_landing, side_send, side_recv = take(5)
    columns_two, heads, load_sem, rows_one, kept, other, units, residuals = take(8)
    grad_normed, normed_send, normed_landing, grad_hidden, hidden_landing = take(5)
    stored_send, stored_landing, vector_landing, vector_send, vector_recv = take(5)
    halving = Halving(shapes, (share_one, share_two, share_three, None, None, None), results, refs)
    z, x, seq = place_here()
    core = {"seq": flip(seq, 1)}
    far = {"seq": flip(seq, 2)}
    section = {"section": 1 - lax.axis_index("section")}
    pairs = shares.shape[0]
    here, width = query.shape

    def fetch(pair):
        slot = lax.rem(pair, 2)
        return pltpu.make_async_copy(shares.at[pair], held.at[slot], held_sem.at[slot])

    def load(index):
        source, target = (
            (keys, columns_two.at[pl.ds(0, width)]),
            (values, columns_two.at[pl.ds(width, width)]),
            (w_query, heads.at[0]),
            (w_key, heads.at[1]),
            (w_value, heads.at[2]),
            (one_rows, rows_one),
            (unit, units),
            (grad_residual, residuals),
            (joined_kept, kept),
            (joined_other, other),
            (w_skip, columns_two),
        )[index]
        return pltpu.make_async_copy(source, target, load_sem.at[index])

    def side(index):
        source, target, device = (
            (parts.at[0], far_landing.at[0], core),
            (parts.at[2], far_landing.at[1], core),
            (grad_query, query_landing, core),
            (normed_send, normed_landing, far),
            (grad_hidden, hidden_landing, core),
            (stored_send, stored_landing, section),
        )[index]
        return remote(source, target, side_send.at[index], side_recv.at[index], device)

    vector_devices = [core] + [stage_partner(0, stage, x, z, seq) for stage in range(5)]

    def vector_copy(step):
        return remote(
            vectors,
            vector_landing.at[step],
            vector_send.at[step],
            vector_recv.at[step],
            vector_devices[step],
        )

    def vector_finish(step):
        vector_copy(step).wait()
        vectors[...] += vector_landing[step]
        if step < 5:
            vector_copy(step + 1).start()

    load(0).start()
    load(1).start()
    fetch(0).start()
    enter(ring_partners(z, x, seq) + [core, section])
    for job in range(3):
        halving.start(job)
    for index in range(2, 10):
        load(index).start()
    load(0).wait()
    load(1).wait()

    def one_pair(pair, carry):
        @pl.when(pair + 1 < pairs)
        def _():
            fetch(pair + 1).start()

        fetch(pair).wait()
        columns = pl.ds(pl.multiple_of(pair * 128, 128), 128)
        others = pl.ds(pl.multiple_of(width + pair * 128, 128), 128)
        out, grad_keys, grad_values = attention_backward_pair(
            query[:, columns],
            columns_two.at[pl.ds(0, width), columns],
            columns_two.at[pl.ds(width, width), columns],
            held.at[lax.rem(pair, 2)],
            inverses[pair],
            grad[:, columns],
            mixed[:, columns],
            lows,
        )
        grad_query[:, columns] = out
        for index, (one, two) in enumerate(zip(grad_keys, grad_values)):
            part, rows = index * 128 // here, pl.ds(index * 128 % here, 128)
            parts[part, rows, columns] = one
            parts[part, rows, others] = two
        for step in range(2):
            for place in (columns, others):
                remote(
                    parts.at[2 * step + 1, :, place],
                    landing.at[step, :, place],
                    swap_send,
                    swap_recv,
                    core,
                ).start()
        return carry

    lax.fori_loop(0, 5, one_pair, 0)
    halving.finish(0, 0)
    lax.fori_loop(5, pairs, one_pair, 0)
    side(2).start()
    load(10).start()
    swapped = remote(landing, landing, swap_send, swap_recv, core)
    swapped.wait_recv()
    for step in (1, 0):

        def add_rows(index, carry):
            rows = pl.ds(pl.multiple_of(index * 64, 64), 64)
            parts[2 * step, rows] = (
                parts[2 * step, rows].astype(jnp.float32)
                + landing[step, rows].astype(jnp.float32)
            ).astype(jnp.bfloat16)
            return carry

        lax.fori_loop(0, here // 64, add_rows, 0)
        side(step).start()
    for index in range(2, 5):
        load(index).wait()

    def from_parts(part, rows):
        return back_product(parts[part, :, pl.ds(0, width)], heads[1, rows]) + back_product(
            parts[part, :, pl.ds(width, width)], heads[2, rows]
        )

    def far_rows(index, carry):
        rows = pl.ds(pl.multiple_of(index * 256, 256), 256)
        normed_send[:, rows] = from_parts(2, rows).astype(jnp.bfloat16)
        return carry

    lax.fori_loop(0, width // 256, far_rows, 0)
    side(3).start()
    halving.finish(1, 0)
    halving.finish(2, 0)

    def own_rows(index, carry):
        rows = pl.ds(pl.multiple_of(index * 256, 256), 256)
        grad_normed[:, rows] = from_parts(0, rows) + back_product(grad_query[...], heads[0, rows])
        return carry

    lax.fori_loop(0, width // 256, own_rows, 0)
    load(5).wait()
    side(2).wait_recv()
    for quarter in range(4):
        columns = pl.ds(quarter * 256, 256)
        halving.store(
            3,
            quarter,
            project(rows_one[:, pl.ds(0, here)], grad_query[:, columns])
            + project(rows_one[:, pl.ds(here, here)], query_landing[:, columns]),
        )
    side(0).wait_recv()
    side(1).wait_recv()
    for quarter in range(4):
        columns = pl.ds(quarter * 512, 512)
        halving.store(
            4,
            quarter,
            project(rows_one[:, pl.ds(0, here)], parts[0, :, columns])
            + project(rows_one[:, pl.ds(here, here)], far_landing[0, :, columns])
            + project(rows_one[:, pl.ds(2 * here, here)], parts[2, :, columns])
            + project(rows_one[:, pl.ds(3 * here, here)], far_landing[1, :, columns]),
        )
    halving.finish(0, 1)
    load(6).wait()
    load(7).wait()
    side(3).wait_recv()

    def norm_rows(index, sums):
        rows = pl.ds(pl.multiple_of(index * 32, 32), 32)
        grads = grad_normed[rows] + normed_landing[rows].astype(jnp.float32)
        ones = units[rows]
        scaled = grads * gain_one[...]
        value = scaled - mean_rows(scaled) - ones * mean_rows(scaled * ones)
        grad_hidden[rows] = (residuals[rows] + inverse_one[rows] * value).astype(jnp.bfloat16)
        return (
            sums[0] + jnp.sum(grads * ones, axis=0, keepdims=True),
            sums[1] + jnp.sum(grads, axis=0, keepdims=True),
        )

    nothing = jnp.zeros((1, width), jnp.float32)
    gain_sum, bias_sum = lax.fori_loop(0, here // 32, norm_rows, (nothing, nothing))
    side(4).start()
    vectors[...] = jnp.concatenate(
        [gain_sum, bias_sum, gain_two_sum[...], bias_two_sum[...], jnp.zeros((4, width), jnp.float32)],
        axis=0,
    )
    vector_copy(0).start()
    load(10).wait()

    def stored_rows(index, carry):
        rows = pl.ds(pl.multiple_of(index * 256, 256), 256)
        below = pl.ds(pl.multiple_of(width + index * 256, 256), 256)
        stored_send[:, rows] = back_product(grad_hidden[...], columns_two[below]).astype(
            jnp.bfloat16
        )
        return carry

    lax.fori_loop(0, width // 256, stored_rows, 0)
    side(5).start()
    halving.finish(1, 1)
    halving.finish(2, 1)
    load(8).wait()
    load(9).wait()
    side(4).wait_recv()
    for quarter in range(4):
        columns = pl.ds(quarter * 256, 256)
        halving.store(
            5,
            quarter,
            project(kept[...], grad_hidden[:, columns])
            + project(other[...], hidden_landing[:, columns]),
        )
    vector_finish(0)

    def own_grads(index, carry):
        rows = pl.ds(pl.multiple_of(index * 256, 256), 256)
        grad_own[:, rows] = back_product(grad_hidden[...], columns_two[rows]).astype(jnp.bfloat16)
        return carry

    lax.fori_loop(0, width // 256, own_grads, 0)
    for stage in range(2, 7):
        if stage < 5:
            for job in range(3):
                halving.finish(job, stage)
        for job in range(3, 6):
            halving.finish(job, stage - 2)
        vector_finish(stage - 1)
    side(5).wait_recv()
    grad_stored[...] = stored_landing[...]
    halving.drain()
    swapped.wait_send()
    for index in range(6):
        side(index).wait_send()


def backward(
    query, keys, values, shares, inverses, grad, mixed, weights, tail, small, collective_id
):
    here, width = query.shape
    span = keys.shape[0]
    shapes = [(share.shape[1] // 2, share.shape[2]) for share in weights]
    shapes += [(width // 64, width), (width // 64, 2 * width), (width // 32, width)]
    made = (False, False, False, True, True, True)
    inside = pl.BlockSpec(memory_space=pltpu.VMEM)
    outside = pl.BlockSpec(memory_space=pl.ANY)
    result_shapes = shapes[:4] + [shapes[3], shapes[3]] + shapes[5:]
    rows_shape = (here, width)
    low_rows = pltpu.VMEM(rows_shape, jnp.bfloat16)
    full_rows = pltpu.VMEM(rows_shape, jnp.float32)
    dma = pltpu.SemaphoreType.DMA
    return pl.pallas_call(
        functools.partial(backward_kernel, shapes),
        in_specs=[inside, outside, outside, outside, inside, inside, inside]
        + [outside] * (3 + len(tail))
        + [inside] * len(small),
        out_specs=[inside] * (3 + len(result_shapes)),
        out_shape=[
            jax.ShapeDtypeStruct(rows_shape, jnp.bfloat16),
            jax.ShapeDtypeStruct(rows_shape, jnp.bfloat16),
            jax.ShapeDtypeStruct((8, width), jnp.float32),
        ]
        + [jax.ShapeDtypeStruct(shape, jnp.float32) for shape in result_shapes],
        scratch_shapes=[
            pltpu.VMEM((span, 2 * here), jnp.bfloat16),
            pltpu.VMEM((2, span, 2 * here), jnp.bfloat16),
            dma((2,)),
            pltpu.VMEM((4, here, 2 * width), jnp.bfloat16),
            pltpu.VMEM((2, here, 2 * width), jnp.bfloat16),
            dma,
            dma,
            pltpu.VMEM((2, here, 2 * width), jnp.bfloat16),
            low_rows,
            low_rows,
            dma((6,)),
            dma((6,)),
            pltpu.VMEM((2 * width, width), jnp.bfloat16),
            pltpu.VMEM((3, width, width), jnp.bfloat16),
            dma((11,)),
            pltpu.VMEM((width // 2, span), jnp.bfloat16),
            pltpu.VMEM((width, here), jnp.bfloat16),
            pltpu.VMEM((width, here), jnp.bfloat16),
            full_rows,
            full_rows,
            full_rows,
            low_rows,
            low_rows,
            low_rows,
            low_rows,
            low_rows,
            low_rows,
            pltpu.VMEM((6, 8, width), jnp.float32),
            dma((6,)),
            dma((6,)),
        ]
        + Halving.scratch(shapes, made),
        compiler_params=pltpu.CompilerParams(
            collective_id=collective_id,
            has_side_effects=True,
            vmem_limit_bytes=62 * 2**20,
        ),
    )(query, keys, values, shares, inverses, grad, mixed, *weights, *tail, *small)


def mean_rows(value):
    return jnp.mean(value, axis=-1, keepdims=True)


def ffn_kernel(
    core, hidden, mixed, grad_low, w_out, gain, bias, w_up, w_down,
    output, act_kept, act_sent, two_kept, two_sent, grad_up, grad_attn, grad_mixed, gain_sum, bias_sum,
    residual, unit, inverse, normed, total, grad_normed, turned,
):
    step = pl.program_id(0)
    last = pl.num_programs(0) - 1
    here = hidden.shape[0]
    mine = core[0]
    root = 0.7071067811865476

    @pl.when(step == 0)
    def _():
        value = hidden[...] + project(mixed[...], w_out[...])
        center = value - mean_rows(value)
        scale = lax.rsqrt(mean_rows(center * center) + EPS)
        residual[...] = value
        unit[...] = center * scale
        inverse[...] = scale
        two = (unit[...] * gain[...] + bias[...]).astype(jnp.bfloat16)
        normed[...] = two
        total[...] = jnp.zeros_like(total)
        grad_normed[...] = jnp.zeros_like(grad_normed)
        turned[...] = two.T

        def split(index, carry):
            place = pl.ds(pl.multiple_of(index * 16, 16), 16)
            two_kept[place] = turned[pl.ds(pl.multiple_of(index * 32 + mine * 16, 16), 16)]
            two_sent[place] = turned[pl.ds(pl.multiple_of(index * 32 + (1 - mine) * 16, 16), 16)]
            return carry

        lax.fori_loop(0, two_kept.shape[0] // 16, split, 0)

    upward = project(normed[...], w_up[...])
    cdf = 0.5 * (1.0 + lax.erf(upward * root))
    act = (upward * cdf).astype(jnp.bfloat16)
    density = jnp.exp(upward * upward * -0.5) * 0.3989422804014327
    slope = cdf + upward * density
    back = back_product(grad_low[...], w_down[...])
    grad = (back * slope).astype(jnp.bfloat16)
    grad_up[...] = grad
    total[...] += project(act, w_down[...])
    grad_normed[...] += back_product(grad, w_up[...])
    width = act.shape[1]
    turned[pl.ds(0, width)] = act.T
    for index in range(width // 128):
        place = pl.ds(index * 64, 64)
        act_kept[place] = turned[pl.ds(pl.multiple_of(index * 128 + mine * 64, 64), 64)]
        act_sent[place] = turned[pl.ds(pl.multiple_of(index * 128 + (1 - mine) * 64, 64), 64)]

    @pl.when(step == last)
    def _():
        output[...] = (residual[...] + total[...]).astype(jnp.bfloat16)
        grads = grad_normed[...]
        scaled = grads * gain[...]
        units = unit[...]
        step_one = scaled - mean_rows(scaled) - units * mean_rows(scaled * units)
        value = grad_low[...].astype(jnp.float32) + inverse[...] * step_one
        gain_sum[...] = jnp.sum(grads * units, axis=0, keepdims=True)
        bias_sum[...] = jnp.sum(grads, axis=0, keepdims=True)
        grad_attn[...] = value
        grad_mixed[...] = back_product(value.astype(jnp.bfloat16), w_out[...]).astype(jnp.bfloat16)


def feed_forward(core, hidden, mixed, grad_low, w_out, gain, bias, w_up, w_down):
    here, width = hidden.shape
    full = w_up.shape[1]
    block = 512
    whole = lambda shape: pl.BlockSpec(shape, lambda i: (0,) * len(shape))
    return pl.pallas_call(
        ffn_kernel,
        grid=(full // block,),
        in_specs=[
            pl.BlockSpec(memory_space=pltpu.SMEM),
            whole((here, width)),
            whole((here, width)),
            whole((here, width)),
            whole((width, width)),
            whole((1, width)),
            whole((1, width)),
            pl.BlockSpec((width, block), lambda i: (0, i)),
            pl.BlockSpec((block, width), lambda i: (i, 0)),
        ],
        out_specs=[
            whole((here, width)),
            pl.BlockSpec((block // 2, here), lambda i: (i, 0)),
            pl.BlockSpec((block // 2, here), lambda i: (i, 0)),
            whole((width // 2, here)),
            whole((width // 2, here)),
            pl.BlockSpec((here, block), lambda i: (0, i)),
            whole((here, width)),
            whole((here, width)),
            whole((1, width)),
            whole((1, width)),
        ],
        out_shape=[
            jax.ShapeDtypeStruct((here, width), jnp.bfloat16),
            jax.ShapeDtypeStruct((full // 2, here), jnp.bfloat16),
            jax.ShapeDtypeStruct((full // 2, here), jnp.bfloat16),
            jax.ShapeDtypeStruct((width // 2, here), jnp.bfloat16),
            jax.ShapeDtypeStruct((width // 2, here), jnp.bfloat16),
            jax.ShapeDtypeStruct((here, full), jnp.bfloat16),
            jax.ShapeDtypeStruct((here, width), jnp.float32),
            jax.ShapeDtypeStruct((here, width), jnp.bfloat16),
            jax.ShapeDtypeStruct((1, width), jnp.float32),
            jax.ShapeDtypeStruct((1, width), jnp.float32),
        ],
        scratch_shapes=[
            pltpu.VMEM((here, width), jnp.float32),
            pltpu.VMEM((here, width), jnp.float32),
            pltpu.VMEM((here, 1), jnp.float32),
            pltpu.VMEM((here, width), jnp.bfloat16),
            pltpu.VMEM((here, width), jnp.float32),
            pltpu.VMEM((here, width), jnp.float32),
            pltpu.VMEM((width, here), jnp.bfloat16),
        ],
        compiler_params=pltpu.CompilerParams(vmem_limit_bytes=48 * 2**20),
    )(core, hidden, mixed, grad_low, w_out, gain, bias, w_up, w_down)


def on_device(
    states,
    mirror,
    w_skip,
    norm1_gain,
    norm1_bias,
    w_query,
    w_key,
    w_value,
    w_out,
    norm2_gain,
    norm2_bias,
    w_up,
    w_down,
    out_grad,
    lengths,
    infill_spans,
):
    rows_here = states.shape[2]
    model_width = states.shape[3]
    head_count = HEADS
    head_dim = model_width // head_count
    query_scale = head_dim ** (-0.5) * LOG2E
    seq = lax.axis_index("seq")
    own_rows = states.reshape(rows_here, model_width)
    stored = mirror.reshape(rows_here, model_width)
    partner = from_partner(stored, "section", 0)
    lengths_row = lengths.reshape(-1)
    spans_row = infill_spans.reshape(-1, 2)
    row_length = rows_here * lax.axis_size("seq")
    local = jnp.arange(rows_here, dtype=jnp.int32)
    query_place = seq * rows_here + local
    key_place = jnp.concatenate([(seq ^ step) * rows_here + local for step in range(4)])
    query_segment, inside = segment_tables(lengths_row, spans_row, query_place)
    key_segment = segment_tables(lengths_row, spans_row, key_place)[0]
    tables = (key_place[:, None], key_segment[:, None], query_place[None], query_segment[None])
    slopes = 2.0 ** (-8.0 * (jnp.arange(head_count, dtype=jnp.float32) + 1.0) / head_count)
    slopes = jnp.repeat(LOG2E * slopes.reshape(-1, 2), rows_here, axis=1)[:, None, :]
    gain_one = norm1_gain.astype(jnp.float32)
    bias_one = norm1_bias.astype(jnp.float32)
    w_first = w_skip[:model_width]
    w_second = w_skip[model_width:]
    core = seq % 2
    select_mine = core_selector(core, model_width)
    select_other = core_selector(1 - core, model_width)

    grad_low = jnp.where(
        inside[:, None], out_grad.reshape(rows_here, model_width), jnp.bfloat16(0)
    )
    grad_low_other = swap_core(grad_low)
    hidden = project(own_rows, w_first) + project(partner, w_second)
    normed_one, unit_one, inverse_one = norm_forward(hidden, gain_one, bias_one)
    normed_one = low(normed_one)
    far = partner_of(normed_one, "seq", 2)
    near = swap_core(normed_one)
    far_near = swap_core(far)
    normed_all = jnp.concatenate([normed_one, near, far, far_near], axis=0)
    query = low(project(normed_one, w_query) * query_scale)
    keys_all = low(project(normed_all, w_key))
    values_all = low(project(normed_all, w_value))
    shares, mixed_rows, inverses = attention_forward(query, keys_all, values_all, tables, slopes)
    (
        output,
        act_mine,
        act_send,
        two_mine,
        two_send,
        grad_upward,
        grad_residual,
        grad_mixed,
        grad_gain_two,
        grad_bias_two,
    ) = feed_forward(
        core.reshape(1),
        hidden,
        mixed_rows,
        grad_low,
        w_out,
        norm2_gain.astype(jnp.float32)[None],
        norm2_bias.astype(jnp.float32)[None],
        w_up,
        w_down,
    )
    output = output.reshape(states.shape)
    grad_upward_other = swap_core(grad_upward)

    act_other = swap_core(act_send)
    down_share = pair_product(act_mine, act_other, grad_low, grad_low_other)
    two_other = swap_core(two_send)
    up_share = pair_product(two_mine, two_other, grad_upward, grad_upward_other)
    grad_attn = low(grad_residual)
    grad_attn_other = swap_core(grad_attn)
    mixed_mine = low(back_product(select_mine, mixed_rows))
    mixed_other = swap_core(low(back_product(select_other, mixed_rows)))
    out_share = pair_product(mixed_mine, mixed_other, grad_attn, grad_attn_other)
    one_rows = low(back_product(select_mine, normed_all))
    joined = jnp.concatenate([own_rows, partner], axis=1)
    joined_mine = low(back_product(core_selector(core, 2 * model_width), joined))
    joined_other = swap_core(low(back_product(core_selector(1 - core, 2 * model_width), joined)))
    (
        grad_own,
        grad_stored,
        sums,
        down_sum,
        up_sum,
        out_sum,
        query_sum,
        key_sum,
        value_sum,
        skip_sum,
    ) = backward(
        query,
        keys_all,
        values_all,
        shares,
        inverses,
        grad_mixed,
        mixed_rows,
        [down_share, up_share, out_share],
        [
            w_query,
            w_key,
            w_value,
            w_skip,
            one_rows,
            joined_mine,
            joined_other,
            unit_one,
            grad_residual,
        ],
        [inverse_one, gain_one[None], grad_gain_two, grad_bias_two],
        1,
    )
    shard = lax.axis_index("dp") * 4 + seq
    piece = model_width // 64
    sums = lax.dynamic_slice(sums, (0, shard * piece), (4, piece))
    return (
        output,
        grad_own.reshape(states.shape),
        grad_stored.reshape(states.shape),
        skip_sum[None],
        sums[0][None],
        sums[1][None],
        query_sum[None],
        key_sum[None],
        value_sum[None],
        out_sum[None],
        sums[2][None],
        sums[3][None],
        up_sum[None],
        down_sum[None],
    )


def solution(mesh):
    in_specs = (
        P("section", "dp", "seq", None),
        P("section", "dp", "seq", None),
        P(),
        P(),
        P(),
        P(),
        P(),
        P(),
        P(),
        P(),
        P(),
        P(),
        P(),
        P("section", "dp", "seq", None),
        P("section", "dp", None),
        P("section", "dp", None, None),
    )
    out_specs = (
        P("section", "dp", "seq", None),
        P("section", "dp", "seq", None),
        P("section", "dp", "seq", None),
        P("section", ("dp", "seq"), None),
        P("section", ("dp", "seq")),
        P("section", ("dp", "seq")),
        P("section", ("dp", "seq"), None),
        P("section", ("dp", "seq"), None),
        P("section", ("dp", "seq"), None),
        P("section", ("dp", "seq"), None),
        P("section", ("dp", "seq")),
        P("section", ("dp", "seq")),
        P("section", ("dp", "seq"), None),
        P("section", ("dp", "seq"), None),
    )
    return jax.shard_map(
        on_device, mesh=mesh, in_specs=in_specs, out_specs=out_specs, check_vma=False
    )
```

```python
import functools

import jax
import jax.numpy as jnp
from jax.experimental import pallas as pl
from jax.experimental.pallas import tpu as pltpu
from jax import lax
from jax.sharding import PartitionSpec as P

HEADS = 16
LOG2E = 1.4426950408889634
LN2 = 0.6931471805599453


EPS = 1e-05


def from_partner(value, axis, stride):
    mask = 2**stride
    pairs = [(source, source ^ mask) for source in range(lax.axis_size(axis))]
    return lax.ppermute(value, axis, pairs)


def project(left, right):
    return jnp.dot(left, right, preferred_element_type=jnp.float32)


def rows_product(left, right):
    return lax.dot_general(
        left, right, (((0,), (0,)), ((), ())), preferred_element_type=jnp.float32
    )


def back_product(left, right):
    return lax.dot_general(
        left, right, (((1,), (1,)), ((), ())), preferred_element_type=jnp.float32
    )


def norm_forward(hidden, gain, bias):
    center = hidden - jnp.mean(hidden, axis=-1, keepdims=True)
    variance = jnp.mean(center * center, axis=-1, keepdims=True)
    inverse = lax.rsqrt(variance + EPS)
    return center * inverse * gain + bias


def segment_tables(lengths_row, spans_row, places):
    ends = jnp.cumsum(lengths_row, dtype=jnp.int32)
    starts = ends - lengths_row
    segment = jnp.sum((places[:, None] >= ends[None, :]).astype(jnp.int32), axis=1)
    lower = starts + spans_row[:, 0]
    upper = starts + spans_row[:, 1]
    inside = jnp.any(
        (places[:, None] >= lower[None, :]) & (places[:, None] < upper[None, :]), axis=1
    )
    return (segment, inside)


def partner_of(value, axis, mask):
    pairs = [(source, source ^ mask) for source in range(lax.axis_size(axis))]
    return lax.ppermute(value, axis, pairs)


def core_selector(core, rows):
    piece = rows // 32
    target = jnp.arange(rows // 2, dtype=jnp.int32)
    source = (target // piece) * (2 * piece) + core * piece + target % piece
    return (source[:, None] == jnp.arange(rows, dtype=jnp.int32)[None, :]).astype(jnp.bfloat16)


def swap_core(value):
    return partner_of(value, "seq", 1)


def low(value):
    return value.astype(jnp.bfloat16)


MESH = pl.DeviceIdType.MESH
NEAR, WRAP = (0, 3, 1, 2), (0, 1, 3, 2)
QUARTERS = (("x", NEAR), ("x", WRAP), ("z", NEAR), ("z", WRAP))


def flip(value, mask):
    if mask == 1:
        return value + 1 - 2 * lax.rem(value, 2)
    if mask == 2:
        return lax.rem(value + 2, 4)
    if mask == 3:
        return 3 - value
    return value


def block_place(quarter, outer, inner, x, z):
    first, order = QUARTERS[quarter]
    if first == "x":
        return flip(z, order[inner]) * 4 + flip(x, order[outer])
    return flip(z, order[outer]) * 4 + flip(x, order[inner])


def stage_partner(quarter, stage, x, z, seq):
    if stage == 4:
        return {"seq": lax.rem(seq + 2, 4)}
    first, order = QUARTERS[quarter]
    mask = order[2] if stage % 2 == 0 else order[1]
    if (first == "x") == (stage < 2):
        return {"dp": z * 4 + flip(x, mask)}
    return {"dp": flip(z, mask) * 4 + x}


def remote(source, target, send, recv, device):
    return pltpu.make_async_remote_copy(
        src_ref=source,
        dst_ref=target,
        send_sem=send,
        recv_sem=recv,
        device_id=device,
        device_id_type=MESH,
    )


def enter(devices):
    barrier = pltpu.get_barrier_semaphore()
    for device in devices:
        pl.semaphore_signal(barrier, inc=1, device_id=device, device_id_type=MESH)
    pl.semaphore_wait(barrier, len(devices))


def add_blocks(count, total, other):
    def one(index, carry):
        total[index] = (
            total[index].astype(jnp.float32) + other[index].astype(jnp.float32)
        ).astype(jnp.bfloat16)
        return carry

    lax.fori_loop(0, count, one, 0)


def place_here():
    dp, seq = lax.axis_index("dp"), lax.axis_index("seq")
    return lax.div(dp, 4), lax.rem(dp, 4), seq


def ring_partners(z, x, seq):
    pairs = ((0, 0), (0, 1), (2, 0), (2, 1), (0, 4))
    return [stage_partner(quarter, stage, x, z, seq) for quarter, stage in pairs]


def either(one, two):
    return 2 * lax.rem(lax.div(one, 2) + lax.div(two, 2), 2) + lax.rem(one + two, 2)


def relative_place(quarter, z, x, there):
    first, order = QUARTERS[quarter]

    def position(value):
        if order == NEAR:
            return 2 * value - lax.div(value, 2) - 4 * lax.div(value, 3)
        return value + lax.div(value, 2) * (1 - 2 * lax.rem(value, 2))

    z_place = position(either(z, lax.div(there, 4)))
    x_place = position(either(x, lax.rem(there, 4)))
    return x_place * 4 + z_place if first == "x" else z_place * 4 + x_place


class Halving:
    def __init__(self, shapes, results, scratch):
        self.shapes, self.results = shapes, results
        scratch = list(scratch)
        count = len(shapes)
        self.work = scratch[:count]
        self.landings = [scratch[count + 5 * job : count + 5 * job + 5] for job in range(count)]
        self.send_sem, self.recv_sem = scratch[6 * count :]
        self.z, self.x, self.seq = place_here()
        self.y = lax.div(self.seq, 2)

    @staticmethod
    def scratch(shapes):
        shapes_of = [(4, 16, 2 * rows, width // 4) for rows, width in shapes]
        for rows, width in shapes:
            shapes_of += [(4, blocks, 2 * rows, width // 4) for blocks in (8, 4, 2, 1)]
            shapes_of.append((4, rows, width // 4))
        sems = pltpu.SemaphoreType.DMA((len(shapes), 4, 5))
        return [pltpu.VMEM(shape, jnp.bfloat16) for shape in shapes_of] + [sems, sems]

    def put(self, job, quarter, there, value):
        place = relative_place(quarter, self.z, self.x, there)
        self.work[job][quarter, place] = value.astype(jnp.bfloat16)
        return place

    def put_and_send(self, job, quarter, there, value):
        place = self.put(job, quarter, there, value)

        @pl.when(place >= 8)
        def _():
            remote(
                self.work[job].at[quarter, place],
                self.landings[job][0].at[quarter, place - 8],
                self.send_sem.at[job, quarter, 0],
                self.recv_sem.at[job, quarter, 0],
                stage_partner(quarter, 0, self.x, self.z, self.seq),
            ).start()

    def store(self, job, quarter, value):
        rows = 2 * self.shapes[job][0]
        for index in range(16):
            self.put(job, quarter, index, value[index * rows : (index + 1) * rows])
        self.copy(job, quarter, 0).start()

    def copy(self, job, quarter, stage):
        rows = self.shapes[job][0]
        if stage < 4:
            size = 8 >> stage
            source = self.work[job].at[quarter, pl.ds(size, size)]
        else:
            away = pl.multiple_of((1 - self.y) * rows, 16)
            source = self.work[job].at[quarter, 0, pl.ds(away, rows)]
        return remote(
            source,
            self.landings[job][stage].at[quarter],
            self.send_sem.at[job, quarter, stage],
            self.recv_sem.at[job, quarter, stage],
            stage_partner(quarter, stage, self.x, self.z, self.seq),
        )

    def finish(self, job, stage):
        rows, width = self.shapes[job]
        for quarter in range(4):
            work = self.work[job].at[quarter]
            landing = self.landings[job][stage].at[quarter]
            self.copy(job, quarter, stage).wait_recv()
            if stage < 4:
                add_blocks(8 >> stage, work, landing)
                self.copy(job, quarter, stage + 1).start()
            else:
                mine = pl.multiple_of(self.y * rows, 16)
                total = work[0, pl.ds(mine, rows)].astype(jnp.float32)
                first = quarter * width // 4
                result = self.results[job][first // 4096 if width == 4096 else first // 1024]
                result[:, pl.ds(first % result.shape[1], width // 4)] = total + landing[
                    ...
                ].astype(jnp.float32)

    def drain(self):
        for job in range(len(self.shapes)):
            for quarter in range(4):
                for stage in range(5):
                    self.copy(job, quarter, stage).wait_send()


def attention_backward_pair(query, keys, values, share, inverse, grad, mixed, lows):
    span = keys.shape[0]
    here = query.shape[0]
    chunk = 128
    lane = lax.broadcasted_iota(jnp.int32, query.shape, 1)
    zero = jnp.zeros(query.shape, query.dtype)
    queries = jnp.concatenate(
        [jnp.where(lane < 64, query, zero), jnp.where(lane >= 64, query, zero)], axis=0
    )
    turned = grad.astype(jnp.float32).T
    product = turned * mixed.astype(jnp.float32).T
    first = turned[:64] * inverse[:, :here]
    second = turned[64:] * inverse[:, here:]
    none = jnp.zeros_like(first)
    grads = jnp.concatenate(
        [jnp.concatenate([first, none], axis=1), jnp.concatenate([none, second], axis=1)], axis=0
    ).astype(jnp.bfloat16)
    grads_back = grads.T
    centre = inverse * jnp.concatenate(
        [
            jnp.sum(product[:64], axis=0, keepdims=True),
            jnp.sum(product[64:], axis=0, keepdims=True),
        ],
        axis=1,
    )
    grad_keys, grad_values = [], []
    for index in range(span // chunk):
        rows = pl.ds(index * chunk, chunk)
        part = share[rows]
        grad_share = project(values[rows], grads)
        grad_score = (part.astype(jnp.float32) * (grad_share - centre)).astype(jnp.bfloat16)
        lows[rows] = grad_score
        grad_keys.append((project(grad_score, queries) * LN2).astype(jnp.bfloat16))
        grad_values.append(project(part, grads_back).astype(jnp.bfloat16))
    out = rows_product(keys[...], lows[...])
    out = jnp.concatenate([out[:64, :here], out[64:, here:]], axis=0)
    return (out.T * 0.125).astype(jnp.bfloat16), grad_keys, grad_values


def attention_forward_kernel(
    query, keys, values, key_places, key_segments, query_places, query_segments, slopes,
    shares, mixed, inverses, distance, scores,
):
    span = keys.shape[0]
    chunk = 128
    here = query.shape[0]

    @pl.when(pl.program_id(0) == 0)
    def _():
        gap = jnp.abs(query_places[...] - key_places[...]).astype(jnp.float32)
        same = query_segments[...] == key_segments[...]
        distance[...] = jnp.where(same, gap, 1e30)

    lane = lax.broadcasted_iota(jnp.int32, query.shape, 1)
    zero = jnp.zeros(query.shape, query.dtype)
    both = jnp.concatenate(
        [jnp.where(lane < 64, query[...], zero), jnp.where(lane >= 64, query[...], zero)], axis=0
    )
    slope = slopes[0]

    def raw(index, top):
        rows = pl.ds(pl.multiple_of(index * chunk, chunk), chunk)
        part = back_product(keys[rows], both)
        gap = distance[rows]
        part = part - slope * jnp.concatenate([gap, gap], axis=1)
        scores[rows] = part
        return jnp.maximum(top, jnp.max(part.reshape(chunk // 8, 8, 2 * here), axis=0))

    top = lax.fori_loop(
        0, span // chunk, raw, jnp.full((8, 2 * here), -jnp.inf, jnp.float32), unroll=True
    )
    top = jnp.max(top, axis=0, keepdims=True)

    def exponent(index, carry):
        rows = pl.ds(pl.multiple_of(index * chunk, chunk), chunk)
        shares[0, rows] = jnp.exp2(scores[rows] - top).astype(jnp.bfloat16)
        return carry

    lax.fori_loop(0, span // chunk, exponent, 0, unroll=True)
    turned = jnp.concatenate([values[...].T, jnp.ones((16, span), jnp.bfloat16)], axis=0)
    out = project(turned, shares[0])
    inverse = 1.0 / out[128:129]
    inverses[0] = inverse
    out = out[:128] * inverse
    out = jnp.concatenate([out[:64, :here], out[64:, here:]], axis=0)
    mixed[...] = out.T.astype(jnp.bfloat16)


def attention_forward(query, keys, values, tables, slopes):
    here, width = query.shape
    span = keys.shape[0]
    pairs = width // 128
    whole = lambda a: pl.BlockSpec(a.shape, lambda i: (0,) * a.ndim)
    return pl.pallas_call(
        attention_forward_kernel,
        grid=(pairs,),
        in_specs=[
            pl.BlockSpec((here, 128), lambda i: (0, i)),
            pl.BlockSpec((span, 128), lambda i: (0, i)),
            pl.BlockSpec((span, 128), lambda i: (0, i)),
            *[whole(table) for table in tables],
            pl.BlockSpec((1, 1, 2 * here), lambda i: (i, 0, 0)),
        ],
        out_specs=[
            pl.BlockSpec((1, span, 2 * here), lambda i: (i, 0, 0)),
            pl.BlockSpec((here, 128), lambda i: (0, i)),
            pl.BlockSpec((1, 1, 2 * here), lambda i: (i, 0, 0)),
        ],
        out_shape=[
            jax.ShapeDtypeStruct((pairs, span, 2 * here), jnp.bfloat16),
            jax.ShapeDtypeStruct((here, width), jnp.bfloat16),
            jax.ShapeDtypeStruct((pairs, 1, 2 * here), jnp.float32),
        ],
        scratch_shapes=[
            pltpu.VMEM((span, here), jnp.float32),
            pltpu.VMEM((span, 2 * here), jnp.float32),
        ],
        compiler_params=pltpu.CompilerParams(vmem_limit_bytes=40 * 2**20),
    )(query, keys, values, *tables, slopes)


def split_cores(core, source, kept, sent, rows):
    for index in range(source.shape[0] // (2 * rows)):
        mine = pl.multiple_of(index * 2 * rows + core * rows, rows)
        away = pl.multiple_of(index * 2 * rows + (1 - core) * rows, rows)
        kept(index * rows, source[pl.ds(mine, rows)])
        sent(index * rows, source[pl.ds(away, rows)])


def backward_kernel(
    shapes, query, keys, values, shares, inverses, mixed, grad_low, hidden, w_out, w_up, w_down,
    w_query, w_key, w_value, w_skip, normed_own, normed_near, normed_far, normed_far_near,
    joined_kept, joined_other, gain_one, gain_two, bias_two,
    output, grad_own, grad_stored, vectors, *refs,
):
    refs = list(refs)
    take = lambda n: [refs.pop(0) for _ in range(n)]
    results = [take(1), take(1), take(1), take(1), take(2), take(1)]
    lows, held, held_sem, parts, free_sem, swap_send, swap_recv = take(7)
    grad_query, query_landing, side_send, side_recv = take(4)
    columns_two, heads, load_sem, units, residuals = take(5)
    grad_normed, normed_send, normed_landing, grad_hidden, hidden_landing = take(5)
    stored_send, stored_landing, vector_landing, vector_send, vector_recv = take(5)
    turned, inverse_two, block_sem, pair_send, pair_recv, act_recv, part_sem = take(7)
    grad = grad_hidden
    halving = Halving(shapes, results, refs)
    z, x, seq = place_here()
    core_index = lax.rem(seq, 2)
    core = {"seq": flip(seq, 1)}
    far = {"seq": flip(seq, 2)}
    section = {"section": 1 - lax.axis_index("section")}
    pairs = shares.shape[0]
    here, width = query.shape
    block = 512
    blocks = w_up.shape[1] // block
    half = width // 2

    def fetch(pair):
        slot = lax.rem(pair, 2)
        return pltpu.make_async_copy(shares.at[pair], held.at[slot], held_sem.at[slot])

    def load(index):
        source, target = (
            (keys, columns_two.at[pl.ds(0, width)]),
            (values, columns_two.at[pl.ds(width, width)]),
            (w_query, heads.at[0]),
            (w_key, heads.at[1]),
            (w_value, heads.at[2]),
            (hidden, units),
            (hidden, residuals),
            (w_skip, columns_two),
            (joined_kept, held.at[0, :, pl.ds(0, here)]),
            (joined_other, held.at[0, :, pl.ds(here, here)]),
            (w_out.at[:, pl.ds(0, half)], held.at[0]),
            (w_out.at[:, pl.ds(half, half)], held.at[1]),
        )[index]
        return pltpu.make_async_copy(source, target, load_sem.at[index])

    def load_part(part, index):
        return pltpu.make_async_copy(
            (normed_own, normed_near, normed_far, normed_far_near)[part].at[
                :, pl.ds(index * half, half)
            ],
            held.at[index, pl.ds(part * here, here)],
            part_sem.at[part, index],
        )

    def load_block(step):
        slot = lax.rem(step, 2)
        place = pl.ds(pl.multiple_of(step * block, block), block)
        there = pl.ds(pl.multiple_of(slot * block, block), block)
        return (
            pltpu.make_async_copy(
                w_up.at[:, place], columns_two.at[pl.ds(width, width), there], block_sem.at[slot, 0]
            ),
            pltpu.make_async_copy(
                w_down.at[place], columns_two.at[there], block_sem.at[slot, 1]
            ),
        )

    def side(index):
        source, target, device = (
            (parts.at[0], parts.at[1], core),
            (parts.at[2], parts.at[3], core),
            (grad_query, query_landing, core),
            (normed_send, normed_landing, far),
            (grad_hidden, hidden_landing, core),
            (stored_send, stored_landing, section),
            (grad_low, parts.at[0, :, pl.ds(0, width)], core),
            (parts.at[1, :, pl.ds(0, width)], parts.at[0, :, pl.ds(width, width)], core),
        )[index]
        return remote(source, target, side_send.at[index], side_recv.at[index], device)

    def pair_half(index, part):
        lanes = pl.ds((1 - index) * here, here)
        return remote(
            parts.at[3, :, pl.ds((2 * index + part) * here, here)],
            lows.at[pl.ds(half + part * here, here), lanes],
            pair_send.at[index],
            pair_recv.at[index],
            core,
        )

    def pair_whole(index):
        if index == 2:
            source = target = parts.at[2]
        elif index == 3:
            source = target = heads.at[1]
        else:
            source = target = lows.at[pl.ds(half, half), pl.ds((1 - index) * here, here)]
        return remote(source, target, pair_send.at[index], pair_recv.at[index], core)

    def act_place(step, base):
        rows = pl.ds(pl.multiple_of(base + lax.rem(step, 2) * here, here), here)
        return rows, pl.ds(pl.multiple_of(lax.div(step, 2) * here, here), here)

    def act_copy(step):
        rows, lanes = act_place(step, half)
        return remote(
            parts.at[2, :, pl.ds(pl.multiple_of(step * here, here), here)],
            heads.at[2, rows, lanes],
            pair_send.at[2],
            act_recv.at[step],
            core,
        )

    def up_copy(step):
        rows = pl.ds(pl.multiple_of(lax.div(step, 2) * here, here), here)
        lanes = pl.ds(pl.multiple_of(lax.rem(step, 2) * block, block), block)
        return remote(
            heads.at[0, rows, lanes],
            heads.at[1, rows, lanes],
            pair_send.at[3],
            pair_recv.at[3],
            core,
        )

    vector_devices = [core] + [stage_partner(0, stage, x, z, seq) for stage in range(5)]

    def vector_copy(step):
        return remote(
            vectors,
            vector_landing.at[step],
            vector_send.at[step],
            vector_recv.at[step],
            vector_devices[step],
        )

    def vector_finish(step):
        vector_copy(step).wait()
        vectors[...] += vector_landing[step]
        if step < 5:
            vector_copy(step + 1).start()

    for index in (6, 10, 11):
        load(index).start()
    for copy in load_block(0):
        copy.start()
    enter(ring_partners(z, x, seq) + [core, section])
    side(6).start()

    def share_rows(index):
        def kept(row, value):
            lows[pl.ds(row, 16), pl.ds((1 - index) * here, here)] = value

        def sent(row, value):
            lanes = pl.ds((2 * index + row // here) * here, here)
            parts[3, pl.ds(row % here, 16), lanes] = value

        split_cores(core_index, turned, kept, sent, 16)
        pair_half(index, 0).start()
        pair_half(index, 1).start()

    turned[...] = mixed[...].T
    share_rows(0)
    load(6).wait()
    for index in range(2):
        load(10 + index).wait()
        columns = pl.ds(index * half, half)
        residuals[:, columns] += project(mixed[...], held[index])

    def norm_two_rows(index, carry):
        rows = pl.ds(pl.multiple_of(index * 32, 32), 32)
        value = residuals[rows]
        center = value - mean_rows(value)
        scale = lax.rsqrt(mean_rows(center * center) + EPS)
        center = center * scale
        units[rows] = center
        inverse_two[rows] = scale
        stored_send[rows] = (center * gain_two[...] + bias_two[...]).astype(jnp.bfloat16)
        grad_normed[rows] = jnp.zeros_like(value)
        return carry

    lax.fori_loop(0, here // 32, norm_two_rows, 0)
    turned[...] = stored_send[...].T
    share_rows(1)
    side(6).wait_recv()

    def down_share(step):
        act_copy(step).wait_recv()
        rows, lanes = act_place(step, 0)
        rows_other, _ = act_place(step, half)
        value = project(heads[2, rows, lanes], grad_low[...]) + project(
            heads[2, rows_other, lanes], parts[0, :, pl.ds(0, width)]
        )
        for index in range(2):
            for quarter in range(4):
                halving.put_and_send(
                    0,
                    quarter,
                    2 * step + index,
                    value[index * 128 : index * 128 + 128, quarter * 256 : quarter * 256 + 256],
                )

    def one_block(step, carry):
        @pl.when(step + 1 < blocks)
        def _():
            for copy in load_block(step + 1):
                copy.start()

        for copy in load_block(step):
            copy.wait()
        there = pl.ds(pl.multiple_of(lax.rem(step, 2) * block, block), block)
        up_part = columns_two.at[pl.ds(width, width), there]
        down_part = columns_two.at[there]
        upward = project(stored_send[...], up_part[...])
        cdf = 0.5 * (1.0 + lax.erf(upward * 0.7071067811865476))
        act = (upward * cdf).astype(jnp.bfloat16)
        density = jnp.exp(upward * upward * -0.5) * 0.3989422804014327
        slope = cdf + upward * density
        grad_up = (back_product(grad_low[...], down_part[...]) * slope).astype(jnp.bfloat16)
        residuals[...] += project(act, down_part[...])
        grad_normed[...] += back_product(grad_up, up_part[...])
        up_rows = pl.ds(pl.multiple_of(lax.div(step, 2) * here, here), here)
        heads[0, up_rows, there] = grad_up
        up_copy(step).start()
        turned[pl.ds(0, block)] = act.T
        rows, lanes = act_place(step, 0)
        first = lax.rem(step, 2) * here
        sent_lanes = pl.ds(pl.multiple_of(step * here, here), here)

        def kept(row, value):
            heads[2, pl.ds(pl.multiple_of(first + row, 64), 64), lanes] = value

        def sent(row, value):
            parts[2, pl.ds(row, 64), sent_lanes] = value

        split_cores(core_index, turned.at[pl.ds(0, block)], kept, sent, 64)
        act_copy(step).start()

        @pl.when(step > 0)
        def _():
            down_share(step - 1)

        return carry

    lax.fori_loop(0, blocks, one_block, 0)
    load(0).start()
    load(1).start()

    def norm_back(ones, grads, gain, inverse):
        scaled = grads * gain
        value = scaled - mean_rows(scaled) - ones * mean_rows(scaled * ones)
        return (
            inverse * value,
            jnp.sum(grads * ones, axis=0, keepdims=True),
            jnp.sum(grads, axis=0, keepdims=True),
        )

    def norm_two_back(index, sums):
        rows = pl.ds(pl.multiple_of(index * 32, 32), 32)
        value, gain_part, bias_part = norm_back(
            units[rows], grad_normed[rows], gain_two[...], inverse_two[rows]
        )
        output[rows] = residuals[rows].astype(jnp.bfloat16)
        value = grad_low[rows].astype(jnp.float32) + value
        residuals[rows] = value
        parts[1, rows, pl.ds(0, width)] = value.astype(jnp.bfloat16)
        return sums[0] + gain_part, sums[1] + bias_part

    nothing = jnp.zeros((1, width), jnp.float32)
    gain_sum, bias_sum = lax.fori_loop(0, here // 32, norm_two_back, (nothing, nothing))
    side(7).start()
    load(5).start()
    vectors[pl.ds(2, 1)] = gain_sum
    vectors[pl.ds(3, 1)] = bias_sum
    vectors[pl.ds(4, 4)] = jnp.zeros((4, width), jnp.float32)
    down_share(blocks - 1)
    for index in range(2):
        columns = pl.ds(index * half, half)
        part = back_product(parts[1, :, columns], held[index])
        grad_normed[...] = part if index == 0 else grad_normed[...] + part
    grad[...] = grad_normed[...].astype(jnp.bfloat16)
    fetch(0).start()
    pair_whole(1).wait_recv()
    pair_whole(3).wait_recv()
    for quarter in range(4):
        rows = pl.ds(quarter * here, here)
        halving.store(
            1,
            quarter,
            project(lows[pl.ds(0, half), pl.ds(0, here)], heads[0, rows])
            + project(lows[pl.ds(half, half), pl.ds(0, here)], heads[1, rows]),
        )
    pair_whole(3).wait_send()
    pl.semaphore_signal(free_sem.at[0], inc=1, device_id=core, device_id_type=MESH)
    pair_whole(0).wait_recv()
    side(7).wait_recv()
    for quarter in range(4):
        halving.store(
            2,
            quarter,
            project(
                lows[pl.ds(0, half), pl.ds(here, here)], parts[1, :, pl.ds(quarter * 256, 256)]
            )
            + project(
                lows[pl.ds(half, half), pl.ds(here, here)],
                parts[0, :, pl.ds(width + quarter * 256, 256)],
            ),
        )
    for index in range(3):
        pair_whole(index).wait_send()
    side(7).wait_send()
    for index in range(3, 5):
        load(index).start()
    pl.semaphore_wait(free_sem.at[0], 1)
    halving.finish(0, 0)
    load(0).wait()
    load(1).wait()

    def one_pair(pair, carry):
        @pl.when(pair + 1 < pairs)
        def _():
            fetch(pair + 1).start()

        fetch(pair).wait()
        columns = pl.ds(pl.multiple_of(pair * 128, 128), 128)
        others = pl.ds(pl.multiple_of(width + pair * 128, 128), 128)
        out, grad_keys, grad_values = attention_backward_pair(
            query[:, columns],
            columns_two.at[pl.ds(0, width), columns],
            columns_two.at[pl.ds(width, width), columns],
            held.at[lax.rem(pair, 2)],
            inverses[pair],
            grad[:, columns],
            mixed[:, columns],
            lows,
        )
        grad_query[:, columns] = out
        for index, (one, two) in enumerate(zip(grad_keys, grad_values)):
            part, rows = index * 128 // here, pl.ds(index * 128 % here, 128)
            parts[part, rows, columns] = one
            parts[part, rows, others] = two
        for step in range(2):
            for index, place in enumerate((columns, others)):
                remote(
                    parts.at[2 * step + 1, :, place],
                    heads.at[0, pl.ds((2 * step + index) * here, here), columns],
                    swap_send,
                    swap_recv,
                    core,
                ).start()
        return carry

    lax.fori_loop(0, pairs, one_pair, 0)
    side(2).start()
    load(7).start()
    for part in range(4):
        load_part(part, 0).start()
        load_part(part, 1).start()
    swapped = remote(heads.at[0], heads.at[0], swap_send, swap_recv, core)
    swapped.wait()
    pl.semaphore_signal(free_sem.at[1], inc=1, device_id=core, device_id_type=MESH)
    for step in (1, 0):

        def add_rows(index, carry):
            rows = pl.ds(pl.multiple_of(index * 64, 64), 64)
            for index in range(2):
                columns = pl.ds(index * width, width)
                first = pl.multiple_of((2 * step + index) * here + rows.start, 64)
                parts[2 * step, rows, columns] = (
                    parts[2 * step, rows, columns].astype(jnp.float32)
                    + heads[0, pl.ds(first, 64)].astype(jnp.float32)
                ).astype(jnp.bfloat16)
            return carry

        lax.fori_loop(0, here // 64, add_rows, 0)
    load(2).start()
    for index in range(3, 5):
        load(index).wait()

    def from_parts(part, rows):
        return back_product(parts[part, :, pl.ds(0, width)], heads[1, rows]) + back_product(
            parts[part, :, pl.ds(width, width)], heads[2, rows]
        )

    def far_rows(index, carry):
        rows = pl.ds(pl.multiple_of(index * 256, 256), 256)
        normed_send[:, rows] = from_parts(2, rows).astype(jnp.bfloat16)
        return carry

    lax.fori_loop(0, width // 256, far_rows, 0)
    side(3).start()
    pl.semaphore_wait(free_sem.at[1], 1)
    side(0).start()
    side(1).start()
    halving.finish(1, 0)
    halving.finish(2, 0)
    halving.finish(0, 1)

    load(2).wait()

    def own_rows(index, carry):
        rows = pl.ds(pl.multiple_of(index * 256, 256), 256)
        grad_normed[:, rows] = from_parts(0, rows) + back_product(grad_query[...], heads[0, rows])
        return carry

    lax.fori_loop(0, width // 256, own_rows, 0)
    for part in range(4):
        load_part(part, 0).wait()
        load_part(part, 1).wait()

    def select_rows(index, carry):
        first = pl.multiple_of(index * 128, 128)
        row = first + lax.broadcasted_iota(jnp.int32, (128, width), 0)
        lane = lax.broadcasted_iota(jnp.int32, (128, width), 1)
        source = lax.div(row, 16) * 32 + core_index * 16 + lax.rem(row, 16)
        pick = jnp.where(lane == source, 1.0, 0.0).astype(jnp.bfloat16)
        value = back_product(pick[:, :half], held[0]) + back_product(pick[:, half:], held[1])
        value = value.astype(jnp.bfloat16)
        lows[pl.ds(first, 128)] = value[:, :half]
        lows[pl.ds(pl.multiple_of(half + first, 128), 128)] = value[:, half:]
        return carry

    lax.fori_loop(0, half // 128, select_rows, 0)
    load(8).start()
    load(9).start()

    def rows_one(part):
        return lows[pl.ds(part // 2 * half, half), pl.ds(part % 2 * here, here)]

    side(2).wait_recv()
    for quarter in range(4):
        columns = pl.ds(quarter * 256, 256)
        halving.store(
            3,
            quarter,
            project(rows_one(0), grad_query[:, columns])
            + project(rows_one(1), query_landing[:, columns]),
        )
    side(0).wait_recv()
    side(1).wait_recv()
    for quarter in range(4):
        columns = pl.ds(quarter * 512, 512)
        halving.store(
            4,
            quarter,
            project(rows_one(0), parts[0, :, columns])
            + project(rows_one(1), parts[1, :, columns])
            + project(rows_one(2), parts[2, :, columns])
            + project(rows_one(3), parts[3, :, columns]),
        )
    halving.finish(0, 2)
    halving.finish(1, 1)
    halving.finish(2, 1)
    load(5).wait()
    side(3).wait_recv()

    def norm_rows(index, sums):
        rows = pl.ds(pl.multiple_of(index * 32, 32), 32)
        grads = grad_normed[rows] + normed_landing[rows].astype(jnp.float32)
        center = units[rows] - mean_rows(units[rows])
        scale = lax.rsqrt(mean_rows(center * center) + EPS)
        value, gain_part, bias_part = norm_back(center * scale, grads, gain_one[...], scale)
        grad_hidden[rows] = (residuals[rows] + value).astype(jnp.bfloat16)
        return sums[0] + gain_part, sums[1] + bias_part

    gain_sum, bias_sum = lax.fori_loop(0, here // 32, norm_rows, (nothing, nothing))
    side(4).start()
    vectors[pl.ds(0, 1)] = gain_sum
    vectors[pl.ds(1, 1)] = bias_sum
    vector_copy(0).start()
    load(7).wait()

    def stored_rows(index, carry):
        rows = pl.ds(pl.multiple_of(index * 256, 256), 256)
        below = pl.ds(pl.multiple_of(width + index * 256, 256), 256)
        stored_send[:, rows] = back_product(grad_hidden[...], columns_two[below]).astype(
            jnp.bfloat16
        )
        return carry

    lax.fori_loop(0, width // 256, stored_rows, 0)
    side(5).start()
    load(8).wait()
    load(9).wait()
    side(4).wait_recv()
    for quarter in range(4):
        columns = pl.ds(quarter * 256, 256)
        halving.store(
            5,
            quarter,
            project(held[0, :, pl.ds(0, here)], grad_hidden[:, columns])
            + project(held[0, :, pl.ds(here, here)], hidden_landing[:, columns]),
        )
    halving.finish(0, 3)
    halving.finish(1, 2)
    halving.finish(2, 2)
    halving.finish(3, 0)
    halving.finish(4, 0)
    vector_finish(0)

    def own_grads(index, carry):
        rows = pl.ds(pl.multiple_of(index * 256, 256), 256)
        grad_own[:, rows] = back_product(grad_hidden[...], columns_two[rows]).astype(jnp.bfloat16)
        return carry

    lax.fori_loop(0, width // 256, own_grads, 0)
    for stage in range(5):
        halving.finish(5, stage)
        if stage == 0:
            halving.finish(0, 4)
        if stage < 2:
            halving.finish(1, stage + 3)
            halving.finish(2, stage + 3)
        if stage < 4:
            halving.finish(3, stage + 1)
            halving.finish(4, stage + 1)
        vector_finish(stage + 1)
    side(5).wait_recv()
    grad_stored[...] = stored_landing[...]
    halving.drain()
    for index in range(7):
        side(index).wait_send()


def backward(inputs, large, small, collective_id):
    query = inputs[0]
    keys = large[0]
    here, width = query.shape
    span = keys.shape[0]
    shapes = [(width // 16, width), (width // 64, 4 * width), (width // 64, width)]
    shapes += [(width // 64, width), (width // 64, 2 * width), (width // 32, width)]
    inside = pl.BlockSpec(memory_space=pltpu.VMEM)
    outside = pl.BlockSpec(memory_space=pl.ANY)
    result_shapes = shapes[:4] + [shapes[3], shapes[3]] + shapes[5:]
    rows_shape = (here, width)
    low_rows = pltpu.VMEM(rows_shape, jnp.bfloat16)
    full_rows = pltpu.VMEM(rows_shape, jnp.float32)
    dma = pltpu.SemaphoreType.DMA
    operands = [query, *large[:3], *inputs[1:], *large[3:], *small]
    specs = [inside] + [outside] * 3 + [inside] * 3 + [outside] * (len(large) - 3)
    specs += [inside] * len(small)
    return pl.pallas_call(
        functools.partial(backward_kernel, shapes),
        in_specs=specs,
        out_specs=[inside] * (4 + len(result_shapes)),
        out_shape=[jax.ShapeDtypeStruct(rows_shape, jnp.bfloat16)] * 3
        + [jax.ShapeDtypeStruct((8, width), jnp.float32)]
        + [jax.ShapeDtypeStruct(shape, jnp.float32) for shape in result_shapes],
        scratch_shapes=[
            pltpu.VMEM((span, 2 * here), jnp.bfloat16),
            pltpu.VMEM((2, span, 2 * here), jnp.bfloat16),
            dma((2,)),
            pltpu.VMEM((4, here, 2 * width), jnp.bfloat16),
            pltpu.SemaphoreType.REGULAR((2,)),
            dma,
            dma,
            low_rows,
            low_rows,
            dma((8,)),
            dma((8,)),
            pltpu.VMEM((2 * width, width), jnp.bfloat16),
            pltpu.VMEM((3, width, width), jnp.bfloat16),
            dma((12,)),
            full_rows,
            full_rows,
            full_rows,
            low_rows,
            low_rows,
            low_rows,
            low_rows,
            low_rows,
            low_rows,
            pltpu.VMEM((6, 8, width), jnp.float32),
            dma((6,)),
            dma((6,)),
            pltpu.VMEM((width, here), jnp.bfloat16),
            pltpu.VMEM((here, 1), jnp.float32),
            dma((2, 2)),
            dma((4,)),
            dma((4,)),
            dma((8,)),
            dma((4, 2)),
        ]
        + Halving.scratch(shapes),
        compiler_params=pltpu.CompilerParams(
            collective_id=collective_id,
            has_side_effects=True,
            vmem_limit_bytes=62 * 2**20,
        ),
    )(*operands)


def mean_rows(value):
    return jnp.mean(value, axis=-1, keepdims=True)


def copy_kernel(*refs):
    count = (len(refs) - 1) // 3
    ways = []
    for index in range(count):
        source, target, stop = refs[index], refs[count + index], refs[2 * count + index]
        ways.append(
            (
                pltpu.make_async_copy(source, stop, refs[-1].at[0, index]),
                pltpu.make_async_copy(stop, target, refs[-1].at[1, index]),
            )
        )
    for into, _ in ways:
        into.start()
    for into, out in ways:
        into.wait()
        out.start()
    for _, out in ways:
        out.wait()


def copied(arrays):
    outside = pl.BlockSpec(memory_space=pl.ANY)
    return pl.pallas_call(
        copy_kernel,
        in_specs=[outside] * len(arrays),
        out_specs=[outside] * len(arrays),
        out_shape=[jax.ShapeDtypeStruct(array.shape, array.dtype) for array in arrays],
        scratch_shapes=[pltpu.VMEM(array.shape, array.dtype) for array in arrays]
        + [pltpu.SemaphoreType.DMA((2, len(arrays)))],
    )(*arrays)


def on_device(
    states,
    mirror,
    w_skip,
    norm1_gain,
    norm1_bias,
    w_query,
    w_key,
    w_value,
    w_out,
    norm2_gain,
    norm2_bias,
    w_up,
    w_down,
    out_grad,
    lengths,
    infill_spans,
):
    rows_here = states.shape[2]
    model_width = states.shape[3]
    head_count = HEADS
    head_dim = model_width // head_count
    query_scale = head_dim ** (-0.5) * LOG2E
    seq = lax.axis_index("seq")
    own_rows = states.reshape(rows_here, model_width)
    stored = mirror.reshape(rows_here, model_width)
    partner = from_partner(stored, "section", 0)
    lengths_row = lengths.reshape(-1)
    spans_row = infill_spans.reshape(-1, 2)
    row_length = rows_here * lax.axis_size("seq")
    local = jnp.arange(rows_here, dtype=jnp.int32)
    query_place = seq * rows_here + local
    key_place = jnp.concatenate([(seq ^ step) * rows_here + local for step in range(4)])
    query_segment, inside = segment_tables(lengths_row, spans_row, query_place)
    key_segment = segment_tables(lengths_row, spans_row, key_place)[0]
    tables = (key_place[:, None], key_segment[:, None], query_place[None], query_segment[None])
    slopes = 2.0 ** (-8.0 * (jnp.arange(head_count, dtype=jnp.float32) + 1.0) / head_count)
    slopes = jnp.repeat(LOG2E * slopes.reshape(-1, 2), rows_here, axis=1)[:, None, :]
    gain_one = norm1_gain.astype(jnp.float32)
    bias_one = norm1_bias.astype(jnp.float32)
    w_first = w_skip[:model_width]
    w_second = w_skip[model_width:]
    core = seq % 2
    select = jnp.concatenate(
        [core_selector(core, model_width), core_selector(1 - core, model_width)], axis=0
    )

    grad_low = jnp.where(
        inside[:, None], out_grad.reshape(rows_here, model_width), jnp.bfloat16(0)
    )
    hidden = project(own_rows, w_first) + project(partner, w_second)
    normed_one = low(norm_forward(hidden, gain_one, bias_one))
    own_split = low(back_product(select, own_rows))
    partner_split = low(back_product(select, partner))
    half = model_width // 2
    joined_mine = jnp.concatenate([own_split[:half], partner_split[:half]], axis=0)
    joined_other = swap_core(jnp.concatenate([own_split[half:], partner_split[half:]], axis=0))
    far = partner_of(normed_one, "seq", 2)
    near = swap_core(normed_one)
    far_near = swap_core(far)
    normed_all = jnp.concatenate([normed_one, near, far, far_near], axis=0)
    query = low(project(normed_one, w_query) * query_scale)
    keys_all = low(project(normed_all, w_key))
    values_all = low(project(normed_all, w_value))
    shares, mixed_rows, inverses = attention_forward(query, keys_all, values_all, tables, slopes)
    results = backward(
        [query, inverses, mixed_rows, grad_low],
        [
            keys_all,
            values_all,
            shares,
            hidden,
            w_out,
            w_up,
            w_down,
            w_query,
            w_key,
            w_value,
            w_skip,
            normed_one,
            near,
            far,
            far_near,
            joined_mine,
            joined_other,
        ],
        [
            gain_one[None],
            norm2_gain.astype(jnp.float32)[None],
            norm2_bias.astype(jnp.float32)[None],
        ],
        1,
    )
    sums = results[3]
    (
        output,
        grad_own,
        grad_stored,
        down_sum,
        up_sum,
        out_sum,
        query_sum,
        key_sum,
        value_sum,
        skip_sum,
    ) = copied(results[:3] + results[4:])
    shard = lax.axis_index("dp") * 4 + seq
    piece = model_width // 64
    sums = lax.dynamic_slice(sums, (0, shard * piece), (4, piece))
    return (
        output.reshape(states.shape),
        grad_own.reshape(states.shape),
        grad_stored.reshape(states.shape),
        skip_sum[None],
        sums[0][None],
        sums[1][None],
        query_sum[None],
        key_sum[None],
        value_sum[None],
        out_sum[None],
        sums[2][None],
        sums[3][None],
        up_sum[None],
        down_sum[None],
    )


def solution(mesh):
    in_specs = (
        P("section", "dp", "seq", None),
        P("section", "dp", "seq", None),
        P(),
        P(),
        P(),
        P(),
        P(),
        P(),
        P(),
        P(),
        P(),
        P(),
        P(),
        P("section", "dp", "seq", None),
        P("section", "dp", None),
        P("section", "dp", None, None),
    )
    out_specs = (
        P("section", "dp", "seq", None),
        P("section", "dp", "seq", None),
        P("section", "dp", "seq", None),
        P("section", ("dp", "seq"), None),
        P("section", ("dp", "seq")),
        P("section", ("dp", "seq")),
        P("section", ("dp", "seq"), None),
        P("section", ("dp", "seq"), None),
        P("section", ("dp", "seq"), None),
        P("section", ("dp", "seq"), None),
        P("section", ("dp", "seq")),
        P("section", ("dp", "seq")),
        P("section", ("dp", "seq"), None),
        P("section", ("dp", "seq"), None),
    )
    return jax.shard_map(
        on_device, mesh=mesh, in_specs=in_specs, out_specs=out_specs, check_vma=False
    )
```

```python
import functools

import jax
import jax.numpy as jnp
from jax.experimental import pallas as pl
from jax.experimental.pallas import tpu as pltpu
from jax import lax
from jax.sharding import PartitionSpec as P

LOG2E = 1.4426950408889634
LN2 = 0.6931471805599453


EPS = 1e-05


def project(left, right):
    return jnp.dot(left, right, preferred_element_type=jnp.float32)


def rows_product(left, right):
    return lax.dot_general(
        left, right, (((0,), (0,)), ((), ())), preferred_element_type=jnp.float32
    )


def back_product(left, right):
    return lax.dot_general(
        left, right, (((1,), (1,)), ((), ())), preferred_element_type=jnp.float32
    )


MESH = pl.DeviceIdType.MESH
NEAR, WRAP = (0, 3, 1, 2), (0, 1, 3, 2)
QUARTERS = (("x", NEAR), ("x", WRAP), ("z", NEAR), ("z", WRAP))


def flip(value, mask):
    if mask == 1:
        return value + 1 - 2 * lax.rem(value, 2)
    if mask == 2:
        return lax.rem(value + 2, 4)
    if mask == 3:
        return 3 - value
    return value


def block_place(quarter, outer, inner, x, z):
    first, order = QUARTERS[quarter]
    if first == "x":
        return flip(z, order[inner]) * 4 + flip(x, order[outer])
    return flip(z, order[outer]) * 4 + flip(x, order[inner])


def stage_partner(quarter, stage, x, z, seq):
    if stage == 4:
        return {"seq": lax.rem(seq + 2, 4)}
    first, order = QUARTERS[quarter]
    mask = order[2] if stage % 2 == 0 else order[1]
    if (first == "x") == (stage < 2):
        return {"dp": z * 4 + flip(x, mask)}
    return {"dp": flip(z, mask) * 4 + x}


def remote(source, target, send, recv, device):
    return pltpu.make_async_remote_copy(
        src_ref=source,
        dst_ref=target,
        send_sem=send,
        recv_sem=recv,
        device_id=device,
        device_id_type=MESH,
    )


def enter(devices):
    barrier = pltpu.get_barrier_semaphore()
    for device in devices:
        pl.semaphore_signal(barrier, inc=1, device_id=device, device_id_type=MESH)
    pl.semaphore_wait(barrier, len(devices))


def add_blocks(count, total, other):
    def one(index, carry):
        total[index] = (
            total[index].astype(jnp.float32) + other[index].astype(jnp.float32)
        ).astype(jnp.bfloat16)
        return carry

    lax.fori_loop(0, count, one, 0)


def place_here():
    dp, seq = lax.axis_index("dp"), lax.axis_index("seq")
    return lax.div(dp, 4), lax.rem(dp, 4), seq


def either(one, two):
    return 2 * lax.rem(lax.div(one, 2) + lax.div(two, 2), 2) + lax.rem(one + two, 2)


def relative_place(quarter, z, x, there):
    first, order = QUARTERS[quarter]

    def position(value):
        if order == NEAR:
            return 2 * value - lax.div(value, 2) - 4 * lax.div(value, 3)
        return value + lax.div(value, 2) * (1 - 2 * lax.rem(value, 2))

    z_place = position(either(z, lax.div(there, 4)))
    x_place = position(either(x, lax.rem(there, 4)))
    return x_place * 4 + z_place if first == "x" else z_place * 4 + x_place


class Halving:
    def __init__(self, shapes, results, scratch):
        self.shapes, self.results = shapes, results
        scratch = list(scratch)
        count = len(shapes)
        self.work = scratch[:count]
        self.landings = [scratch[count + 5 * job : count + 5 * job + 5] for job in range(count)]
        self.landings[-1] = self.landings[-1][:3]
        self.send_sem, self.recv_sem = scratch[-2:]
        self.z, self.x, self.seq = place_here()
        self.y = lax.div(self.seq, 2)

    @staticmethod
    def scratch(shapes):
        shapes_of = [(4, 16, 2 * rows, width // 4) for rows, width in shapes]
        for job, (rows, width) in enumerate(shapes):
            direct = job == len(shapes) - 1
            shapes_of += [(4, blocks, 2 * rows, width // 4) for blocks in (8, 4)]
            if direct:
                shapes_of.append((4, 7, rows, width // 4))
            else:
                shapes_of += [(4, blocks, 2 * rows, width // 4) for blocks in (2, 1)]
                shapes_of.append((4, rows, width // 4))
        sems = pltpu.SemaphoreType.DMA((len(shapes), 4, 5))
        return [pltpu.VMEM(shape, jnp.bfloat16) for shape in shapes_of] + [sems, sems]

    def put(self, job, quarter, there, value):
        place = relative_place(quarter, self.z, self.x, there)
        self.work[job][quarter, place] = value.astype(jnp.bfloat16)
        return place

    def put_and_send(self, job, quarter, there, value):
        place = self.put(job, quarter, there, value)

        @pl.when(place >= 8)
        def _():
            remote(
                self.work[job].at[quarter, place],
                self.landings[job][0].at[quarter, place - 8],
                self.send_sem.at[job, quarter, 0],
                self.recv_sem.at[job, quarter, 0],
                stage_partner(quarter, 0, self.x, self.z, self.seq),
            ).start()

    def store(self, job, quarter, value):
        rows = 2 * self.shapes[job][0]
        for index in range(16):
            self.put(job, quarter, index, value[index * rows : (index + 1) * rows])
        self.copy(job, quarter, 0).start()

    def copy(self, job, quarter, stage):
        rows = self.shapes[job][0]
        if stage < 4:
            size = 8 >> stage
            source = self.work[job].at[quarter, pl.ds(size, size)]
        else:
            away = pl.multiple_of((1 - self.y) * rows, 16)
            source = self.work[job].at[quarter, 0, pl.ds(away, rows)]
        return remote(
            source,
            self.landings[job][stage].at[quarter],
            self.send_sem.at[job, quarter, stage],
            self.recv_sem.at[job, quarter, stage],
            stage_partner(quarter, stage, self.x, self.z, self.seq),
        )

    def finish(self, job, stage):
        rows, width = self.shapes[job]
        for quarter in range(4):
            work = self.work[job].at[quarter]
            landing = self.landings[job][stage].at[quarter]
            self.copy(job, quarter, stage).wait_recv()
            if stage < 4:
                add_blocks(8 >> stage, work, landing)
                self.copy(job, quarter, stage + 1).start()
            else:
                mine = pl.multiple_of(self.y * rows, 16)
                total = work[0, pl.ds(mine, rows)].astype(jnp.float32)
                first = quarter * width // 4
                result = self.results[job][first // 4096 if width == 4096 else first // 1024]
                result[:, pl.ds(first % result.shape[1], width // 4)] = total + landing[
                    ...
                ].astype(jnp.float32)

    def direct(self, job, quarter, step):
        rows = self.shapes[job][0]
        first, order = QUARTERS[quarter]
        inner, away = step // 2, step % 2
        if first == "x":
            dp = flip(self.z, order[inner]) * 4 + self.x
        else:
            dp = self.z * 4 + flip(self.x, order[inner])
        part = pl.multiple_of((1 - self.y if away else self.y) * rows, 16)
        return remote(
            self.work[job].at[quarter, inner, pl.ds(part, rows)],
            self.landings[job][2].at[quarter, step - 1],
            self.send_sem.at[job, quarter, 2],
            self.recv_sem.at[job, quarter, 2],
            {"dp": dp, "seq": flip(self.seq, 2) if away else self.seq},
        )

    def finish_direct(self, job, stage):
        rows, width = self.shapes[job]
        for quarter in range(4):
            work = self.work[job].at[quarter]
            landing = self.landings[job][stage].at[quarter]
            if stage < 2:
                self.copy(job, quarter, stage).wait_recv()
                add_blocks(8 >> stage, work, landing)
                if stage == 0:
                    self.copy(job, quarter, 1).start()
                else:
                    for step in range(1, 8):
                        self.direct(job, quarter, step).start()
            else:
                remote(
                    landing, landing, self.send_sem.at[job, quarter, 2],
                    self.recv_sem.at[job, quarter, 2], {"seq": flip(self.seq, 2)},
                ).wait()
                mine = pl.multiple_of(self.y * rows, 16)
                total = work[0, pl.ds(mine, rows)].astype(jnp.float32)
                for step in range(7):
                    total = total + landing[step].astype(jnp.float32)
                self.results[job][0][:, pl.ds(quarter * width // 4, width // 4)] = total

    def drain(self):
        last = len(self.shapes) - 1
        for job in range(last + 1):
            for quarter in range(4):
                for stage in range(2 if job == last else 5):
                    self.copy(job, quarter, stage).wait_send()


def attention_backward_pair(query, keys, values, share, inverse, grad, mixed, lows):
    span = keys.shape[0]
    here = query.shape[0]
    chunk = 128
    lane = lax.broadcasted_iota(jnp.int32, query.shape, 1)
    zero = jnp.zeros(query.shape, query.dtype)
    queries = jnp.concatenate(
        [jnp.where(lane < 64, query, zero), jnp.where(lane >= 64, query, zero)], axis=0
    )
    turned = grad.astype(jnp.float32).T
    product = turned * mixed.astype(jnp.float32).T
    centre = jnp.concatenate(
        [
            jnp.sum(product[:64], axis=0, keepdims=True),
            jnp.sum(product[64:], axis=0, keepdims=True),
        ],
        axis=1,
    )
    none = jnp.zeros((64, here), jnp.float32)
    sets = []
    for part in range(2):
        factor = inverse[part : part + 1]
        first = turned[:64] * factor[:, :here]
        second = turned[64:] * factor[:, here:]
        grads = jnp.concatenate(
            [jnp.concatenate([first, none], axis=1), jnp.concatenate([none, second], axis=1)],
            axis=0,
        ).astype(jnp.bfloat16)
        sets.append((grads, grads.T, centre * factor))
    grad_keys, grad_values = [], []
    for index in range(span // chunk):
        rows = pl.ds(index * chunk, chunk)
        part = share[rows]
        grads, grads_back, centre = sets[2 * index // (span // chunk)]
        grad_share = project(values[rows], grads)
        grad_score = (part.astype(jnp.float32) * (grad_share - centre)).astype(jnp.bfloat16)
        lows[rows] = grad_score
        grad_keys.append((project(grad_score, queries) * LN2).astype(jnp.bfloat16))
        grad_values.append(project(part, grads_back).astype(jnp.bfloat16))
    out = rows_product(keys[...], lows[...])
    out = jnp.concatenate([out[:64, :here], out[64:, here:]], axis=0)
    return (out.T * 0.125).astype(jnp.bfloat16), grad_keys, grad_values


def flat(vector):
    return vector[...].astype(jnp.float32).reshape(1, vector.shape[0])


def forward_kernel(
    lengths, spans, own, stored, out_grad, gain_one, bias_one, w_skip, w_query, w_key, w_value,
    hidden, query, inverses, mixed, grad_low, kept, shares, keys_out, values_out, normed_out, other,
    partner, normed, joined_sent, joined_landing, turned, w_rows, heads, keys, values,
    distance, scores, exponents, outs, tops, load_sem, send_sem, recv_sem, share_sem,
):
    seq = lax.axis_index("seq")
    core_index = lax.rem(seq, 2)
    core, far = {"seq": flip(seq, 1)}, {"seq": flip(seq, 2)}
    section = {"section": 1 - lax.axis_index("section")}
    here, width = own.shape
    span = keys.shape[0]
    half = width // 2
    pairs = width // 128
    piece = here // 2

    loads = [
        pltpu.make_async_copy(source, target, load_sem.at[index])
        for index, (source, target) in enumerate(
            (
                (w_skip, w_rows),
                (w_query, heads.at[0]),
                (w_key, heads.at[1]),
                (w_value, heads.at[2]),
                (keys, keys_out),
                (values, values_out),
                (normed, normed_out),
                (joined_landing, other),
            )
        )
    ]

    def send(index, part):
        rows = pl.ds(part * piece, piece)
        source, target, device = (
            (stored.at[rows], partner.at[rows], section),
            (normed.at[rows], normed.at[pl.ds(here + part * piece, piece)], core),
            (normed.at[rows], normed.at[pl.ds(2 * here + part * piece, piece)], far),
            (
                normed.at[pl.ds(2 * here + part * piece, piece)],
                normed.at[pl.ds(3 * here + part * piece, piece)],
                core,
            ),
            (
                joined_sent.at[pl.ds(part * half, half)],
                joined_landing.at[pl.ds(part * half, half)],
                core,
            ),
        )[index]
        return remote(source, target, send_sem.at[index, part], recv_sem.at[index, part], device)

    for index in range(4):
        loads[index].start()
    enter([core, far, section])
    send(0, 0).start()
    send(0, 1).start()

    bounds = []
    start = jnp.int32(0)
    for index in range(4):
        bounds.append((start, start + lengths[0, 0, index]))
        start = start + lengths[0, 0, index]

    def segment(places):
        return sum((places >= bounds[index][1]).astype(jnp.int32) for index in range(4))

    place = seq * here + lax.broadcasted_iota(jnp.int32, (here, 1), 0)
    inside = jnp.zeros((here, 1), jnp.int32)
    for index in range(4):
        low_end = bounds[index][0] + spans[0, 0, index, 0]
        high_end = bounds[index][0] + spans[0, 0, index, 1]
        inside += (place >= low_end).astype(jnp.int32) * (place < high_end).astype(jnp.int32)
    grad_low[...] = jnp.where(
        inside > 0, out_grad[...].astype(jnp.float32), 0.0
    ).astype(jnp.bfloat16)
    query_place = seq * here + lax.broadcasted_iota(jnp.int32, (1, here), 1)
    query_segment = segment(query_place)
    for index in range(4):
        key_place = flip(seq, index) * here + lax.broadcasted_iota(jnp.int32, (here, 1), 0)
        gap = jnp.abs(query_place - key_place).astype(jnp.float32)
        distance[pl.ds(index * here, here)] = jnp.where(
            segment(key_place) == query_segment, gap, 1e30
        )

    def joined_rows(part, source):
        turned[...] = source[...].T

        def keep(row, value):
            kept[pl.ds(part * half + row, 32)] = value

        def pass_on(row, value):
            joined_sent[pl.ds(part * half + row, 32)] = value

        split_cores(core_index, turned, keep, pass_on, 32)
        send(4, part).start()

    joined_rows(0, own)
    loads[0].wait()
    hidden[...] = project(own[...], w_rows[pl.ds(0, width)])
    gain, bias = flat(gain_one), flat(bias_one)
    for part in range(2):
        rows = pl.ds(part * piece, piece)
        send(0, part).wait_recv()
        value = hidden[rows] + project(partner[rows], w_rows[pl.ds(width, width)])
        hidden[rows] = value
        center = value - mean_rows(value)
        scale = lax.rsqrt(mean_rows(center * center) + EPS)
        normed[rows] = (center * scale * gain + bias).astype(jnp.bfloat16)
        send(2, part).start()
        send(1, part).start()
    for index in range(1, 4):
        loads[index].wait()
    scale = 0.125 * LOG2E
    query[...] = (project(normed[pl.ds(0, here)], heads[0]) * scale).astype(jnp.bfloat16)

    def both(first, count):
        rows = pl.ds(first, count)
        keys[rows] = project(normed[rows], heads[1]).astype(jnp.bfloat16)
        values[rows] = project(normed[rows], heads[2]).astype(jnp.bfloat16)

    def attend(part, pair):
        columns = pl.ds(pl.multiple_of(pair * 128, 128), 128)
        base = part * 2 * here
        value = query[:, columns]
        lane = lax.broadcasted_iota(jnp.int32, value.shape, 1)
        zero = jnp.zeros(value.shape, value.dtype)
        stacked = jnp.concatenate(
            [jnp.where(lane < 64, value, zero), jnp.where(lane >= 64, value, zero)], axis=0
        )
        head = 2 * pair + 1 + lax.div(lax.broadcasted_iota(jnp.int32, (1, 2 * here), 1), here)
        slope = LOG2E * jnp.exp2(head.astype(jnp.float32) * -0.5)
        top = jnp.full((8, 2 * here), -jnp.inf, jnp.float32)
        for index in range(4):
            rows = pl.ds(base + index * 128, 128)
            score = back_product(keys[rows, columns], stacked)
            gap = distance[rows]
            score = score - slope * jnp.concatenate([gap, gap], axis=1)
            scores[pl.ds(index * 128, 128)] = score
            top = jnp.maximum(top, jnp.max(score.reshape(16, 8, 2 * here), axis=0))
        top = jnp.max(top, axis=0, keepdims=True)
        for index in range(4):
            rows = pl.ds(index * 128, 128)
            exponents[pair, pl.ds(base + index * 128, 128)] = jnp.exp2(
                scores[rows] - top
            ).astype(jnp.bfloat16)
        rows = pl.ds(base, 2 * here)
        pltpu.make_async_copy(
            exponents.at[pair, rows], shares.at[pair, rows], share_sem
        ).start()
        back = jnp.concatenate(
            [values[rows, columns].T, jnp.ones((16, 2 * here), jnp.bfloat16)], axis=0
        )
        return project(back, exponents[pair, rows]), top

    send(1, 0).wait_recv()
    send(1, 1).wait_recv()
    both(0, 2 * here)
    joined_rows(1, partner)

    def near(pair, carry):
        out, top = attend(0, pair)
        outs[pair] = out
        tops[pair] = top
        return carry

    lax.fori_loop(0, pairs, near, 0)
    for part in range(2):
        send(2, part).wait_recv()
        send(3, part).start()
    both(2 * here, here)
    send(3, 0).wait_recv()
    send(3, 1).wait_recv()
    both(3 * here, here)
    for index in range(4, 7):
        loads[index].start()

    def away(pair, carry):
        out, top = attend(1, pair)
        first, first_top = outs[pair], tops[pair]
        best = jnp.maximum(top, first_top)
        one, two = jnp.exp2(first_top - best), jnp.exp2(top - best)
        total = 1.0 / (one * first[128:129] + two * out[128:129])
        one, two = one * total, two * total
        inverses[pair, pl.ds(0, 1)] = one
        inverses[pair, pl.ds(1, 1)] = two
        out = first[:128] * one + out[:128] * two
        out = jnp.concatenate([out[:64, :here], out[64:, here:]], axis=0)
        columns = pl.ds(pl.multiple_of(pair * 128, 128), 128)
        mixed[:, columns] = out.T.astype(jnp.bfloat16)
        return carry

    lax.fori_loop(0, pairs, away, 0)
    for part in range(2):
        send(4, part).wait_recv()
    loads[7].start()
    pltpu.make_async_copy(exponents, shares, share_sem).wait()
    for index in range(4, 8):
        loads[index].wait()
    for index in range(5):
        for part in range(2):
            send(index, part).wait_send()


def forward(lengths, spans, own, stored, out_grad, norms, weights, collective_id):
    here, width = own.shape
    span = 4 * here
    pairs = width // 128
    inside = pl.BlockSpec(memory_space=pltpu.VMEM)
    outside = pl.BlockSpec(memory_space=pl.ANY)
    scalars = pl.BlockSpec(memory_space=pltpu.SMEM)
    low_shape = lambda *shape: jax.ShapeDtypeStruct(shape, jnp.bfloat16)
    low_rows = lambda *shape: pltpu.VMEM(shape, jnp.bfloat16)
    dma = pltpu.SemaphoreType.DMA
    return pl.pallas_call(
        forward_kernel,
        in_specs=[scalars, scalars] + [inside] * 5 + [outside] * 4,
        out_specs=[inside] * 6 + [outside] * 5,
        out_shape=[
            jax.ShapeDtypeStruct((here, width), jnp.float32),
            low_shape(here, width),
            jax.ShapeDtypeStruct((pairs, 2, 2 * here), jnp.float32),
            low_shape(here, width),
            low_shape(here, width),
            low_shape(width, here),
            low_shape(pairs, span, 2 * here),
            low_shape(span, width),
            low_shape(span, width),
            low_shape(span, width),
            low_shape(width, here),
        ],
        scratch_shapes=[
            low_rows(here, width),
            low_rows(span, width),
            low_rows(width, here),
            low_rows(width, here),
            low_rows(width, here),
            low_rows(2 * width, width),
            low_rows(3, width, width),
            low_rows(span, width),
            low_rows(span, width),
            pltpu.VMEM((span, here), jnp.float32),
            pltpu.VMEM((2 * here, 2 * here), jnp.float32),
            low_rows(pairs, span, 2 * here),
            pltpu.VMEM((pairs, 144, 2 * here), jnp.float32),
            pltpu.VMEM((pairs, 1, 2 * here), jnp.float32),
            dma((8,)),
            dma((5, 2)),
            dma((5, 2)),
            dma,
        ],
        compiler_params=pltpu.CompilerParams(
            collective_id=collective_id,
            has_side_effects=True,
            vmem_limit_bytes=56 * 2**20,
        ),
    )(lengths, spans, own, stored, out_grad, *norms, *weights)


def split_cores(core, source, kept, sent, rows):
    for index in range(source.shape[0] // (2 * rows)):
        mine = pl.multiple_of(index * 2 * rows + core * rows, rows)
        away = pl.multiple_of(index * 2 * rows + (1 - core) * rows, rows)
        kept(index * rows, source[pl.ds(mine, rows)])
        sent(index * rows, source[pl.ds(away, rows)])


def backward_kernel(
    shapes, query, keys, values, shares, inverses, mixed, grad_low, hidden, w_out, w_up, w_down,
    w_query, w_key, w_value, w_skip, normed_all, joined_kept, joined_other, gain_one, gain_two, bias_two,
    output, grad_own, grad_stored, vectors, *refs,
):
    refs = list(refs)
    take = lambda n: [refs.pop(0) for _ in range(n)]
    results = [take(1), take(1), take(1), take(1), take(2), take(1)]
    lows, held, held_sem, parts, free_sem, swap_send, swap_recv = take(7)
    grad_query, query_landing, side_send, side_recv = take(4)
    columns_two, heads, load_sem, units, residuals = take(5)
    grad_normed, normed_send, normed_landing, grad_hidden, hidden_landing = take(5)
    stored_send, stored_landing, vector_landing, vector_send, vector_recv = take(5)
    turned, inverse_two, block_sem, pair_send, pair_recv, act_recv, part_sem = take(7)
    grad = grad_hidden
    halving = Halving(shapes, results, refs)
    z, x, seq = place_here()
    core_index = lax.rem(seq, 2)
    core = {"seq": flip(seq, 1)}
    far = {"seq": flip(seq, 2)}
    section = {"section": 1 - lax.axis_index("section")}
    pairs = shares.shape[0]
    here, width = query.shape
    block = 512
    blocks = w_up.shape[1] // block
    half = width // 2

    def fetch(pair):
        slot = lax.rem(pair, 2)
        return pltpu.make_async_copy(shares.at[pair], held.at[slot], held_sem.at[slot])

    def load(index):
        source, target = (
            (keys, columns_two.at[pl.ds(0, width)]),
            (values, columns_two.at[pl.ds(width, width)]),
            (w_query, heads.at[0]),
            (w_key, heads.at[1]),
            (w_value, heads.at[2]),
            (hidden, units),
            (hidden, residuals),
            (w_skip, columns_two),
            (joined_kept, held.at[0, :, pl.ds(0, here)]),
            (joined_other, held.at[0, :, pl.ds(here, here)]),
            (w_out.at[:, pl.ds(0, half)], held.at[0]),
            (w_out.at[:, pl.ds(half, half)], held.at[1]),
        )[index]
        return pltpu.make_async_copy(source, target, load_sem.at[index])

    def load_part(index):
        return pltpu.make_async_copy(
            normed_all.at[:, pl.ds(index * half, half)], held.at[index], part_sem.at[index]
        )

    def load_block(step):
        slot = lax.rem(step, 2)
        place = pl.ds(pl.multiple_of(step * block, block), block)
        there = pl.ds(pl.multiple_of(slot * block, block), block)
        return (
            pltpu.make_async_copy(
                w_up.at[:, place], columns_two.at[pl.ds(width, width), there], block_sem.at[slot, 0]
            ),
            pltpu.make_async_copy(
                w_down.at[place], columns_two.at[there], block_sem.at[slot, 1]
            ),
        )

    def side(index):
        source, target, device = (
            (parts.at[0], parts.at[1], core),
            (parts.at[2], parts.at[3], core),
            (grad_query, query_landing, core),
            (normed_send, normed_landing, far),
            (grad_hidden, hidden_landing, core),
            (stored_send, stored_landing, section),
            (grad_low, parts.at[0, :, pl.ds(0, width)], core),
            (parts.at[1, :, pl.ds(0, width)], parts.at[0, :, pl.ds(width, width)], core),
        )[index]
        return remote(source, target, side_send.at[index], side_recv.at[index], device)

    def pair_half(index, part):
        lanes = pl.ds((1 - index) * here, here)
        return remote(
            parts.at[3, :, pl.ds((2 * index + part) * here, here)],
            lows.at[pl.ds(half + part * here, here), lanes],
            pair_send.at[index],
            pair_recv.at[index],
            core,
        )

    def pair_whole(index):
        if index == 2:
            source = target = parts.at[2]
        elif index == 3:
            source = target = heads.at[1]
        else:
            source = target = lows.at[pl.ds(half, half), pl.ds((1 - index) * here, here)]
        return remote(source, target, pair_send.at[index], pair_recv.at[index], core)

    def act_place(step, base):
        rows = pl.ds(pl.multiple_of(base + lax.rem(step, 2) * here, here), here)
        return rows, pl.ds(pl.multiple_of(lax.div(step, 2) * here, here), here)

    def act_copy(step):
        rows, lanes = act_place(step, half)
        return remote(
            parts.at[2, :, pl.ds(pl.multiple_of(step * here, here), here)],
            heads.at[2, rows, lanes],
            pair_send.at[2],
            act_recv.at[step],
            core,
        )

    def up_copy(step):
        rows = pl.ds(pl.multiple_of(lax.div(step, 2) * here, here), here)
        lanes = pl.ds(pl.multiple_of(lax.rem(step, 2) * block, block), block)
        return remote(
            heads.at[0, rows, lanes],
            heads.at[1, rows, lanes],
            pair_send.at[3],
            pair_recv.at[3],
            core,
        )

    vector_steps = [
        [core],
        [{"dp": z * 4 + flip(x, mask)} for mask in (1, 2, 3)],
        [{"dp": flip(z, mask) * 4 + x} for mask in (1, 2, 3)],
        [far],
    ]
    vector_slots = (0, 1, 4, 7)

    def vector_copies(step):
        return [
            remote(
                vectors,
                vector_landing.at[slot],
                vector_send.at[slot],
                vector_recv.at[slot],
                device,
            )
            for slot, device in enumerate(vector_steps[step], vector_slots[step])
        ]

    def vector_start(step):
        for copy in vector_copies(step):
            copy.start()

    def vector_finish(step):
        copies = vector_copies(step)
        for copy in copies:
            copy.wait()
        for index in range(len(copies)):
            vectors[...] += vector_landing[vector_slots[step] + index]
        if step < 3:
            vector_start(step + 1)

    for index in (6, 10, 11):
        load(index).start()
    for copy in load_block(0):
        copy.start()
    devices = [core, far, section]
    for mask in (1, 2, 3):
        for dp in (z * 4 + flip(x, mask), flip(z, mask) * 4 + x):
            devices += [{"dp": dp}, {"dp": dp, "seq": flip(seq, 2)}]
    enter(devices)
    side(6).start()

    def share_rows(index):
        def kept(row, value):
            lows[pl.ds(row, 16), pl.ds((1 - index) * here, here)] = value

        def sent(row, value):
            lanes = pl.ds((2 * index + row // here) * here, here)
            parts[3, pl.ds(row % here, 16), lanes] = value

        split_cores(core_index, turned, kept, sent, 16)
        pair_half(index, 0).start()
        pair_half(index, 1).start()

    turned[...] = mixed[...].T
    share_rows(0)
    load(6).wait()
    for index in range(2):
        load(10 + index).wait()
        columns = pl.ds(index * half, half)
        residuals[:, columns] += project(mixed[...], held[index])

    def norm_two_rows(index, carry):
        rows = pl.ds(pl.multiple_of(index * 32, 32), 32)
        value = residuals[rows]
        center = value - mean_rows(value)
        scale = lax.rsqrt(mean_rows(center * center) + EPS)
        center = center * scale
        units[rows] = center
        inverse_two[rows] = scale
        stored_send[rows] = (center * flat(gain_two) + flat(bias_two)).astype(jnp.bfloat16)
        grad_normed[rows] = jnp.zeros_like(value)
        return carry

    lax.fori_loop(0, here // 32, norm_two_rows, 0)
    turned[...] = stored_send[...].T
    share_rows(1)
    side(6).wait_recv()

    def down_share(step):
        act_copy(step).wait_recv()
        rows, lanes = act_place(step, 0)
        rows_other, _ = act_place(step, half)
        value = project(heads[2, rows, lanes], grad_low[...]) + project(
            heads[2, rows_other, lanes], parts[0, :, pl.ds(0, width)]
        )
        for index in range(2):
            for quarter in range(4):
                halving.put_and_send(
                    0,
                    quarter,
                    2 * step + index,
                    value[index * 128 : index * 128 + 128, quarter * 256 : quarter * 256 + 256],
                )

    def one_block(step, carry):
        @pl.when(step + 1 < blocks)
        def _():
            for copy in load_block(step + 1):
                copy.start()

        for copy in load_block(step):
            copy.wait()
        there = pl.ds(pl.multiple_of(lax.rem(step, 2) * block, block), block)
        up_part = columns_two.at[pl.ds(width, width), there]
        down_part = columns_two.at[there]
        upward = project(stored_send[...], up_part[...])
        cdf = 0.5 * (1.0 + lax.erf(upward * 0.7071067811865476))
        act = (upward * cdf).astype(jnp.bfloat16)
        density = jnp.exp(upward * upward * -0.5) * 0.3989422804014327
        slope = cdf + upward * density
        grad_up = (back_product(grad_low[...], down_part[...]) * slope).astype(jnp.bfloat16)
        residuals[...] += project(act, down_part[...])
        grad_normed[...] += back_product(grad_up, up_part[...])
        up_rows = pl.ds(pl.multiple_of(lax.div(step, 2) * here, here), here)
        heads[0, up_rows, there] = grad_up
        up_copy(step).start()
        turned[pl.ds(0, block)] = act.T
        rows, lanes = act_place(step, 0)
        first = lax.rem(step, 2) * here
        sent_lanes = pl.ds(pl.multiple_of(step * here, here), here)

        def kept(row, value):
            heads[2, pl.ds(pl.multiple_of(first + row, 64), 64), lanes] = value

        def sent(row, value):
            parts[2, pl.ds(row, 64), sent_lanes] = value

        split_cores(core_index, turned.at[pl.ds(0, block)], kept, sent, 64)
        act_copy(step).start()

        @pl.when(step > 0)
        def _():
            down_share(step - 1)

        return carry

    lax.fori_loop(0, blocks, one_block, 0)
    load(0).start()
    load(1).start()

    def norm_back(ones, grads, gain, inverse):
        scaled = grads * gain
        value = scaled - mean_rows(scaled) - ones * mean_rows(scaled * ones)
        return (
            inverse * value,
            jnp.sum(grads * ones, axis=0, keepdims=True),
            jnp.sum(grads, axis=0, keepdims=True),
        )

    def norm_two_back(index, sums):
        rows = pl.ds(pl.multiple_of(index * 32, 32), 32)
        value, gain_part, bias_part = norm_back(
            units[rows], grad_normed[rows], flat(gain_two), inverse_two[rows]
        )
        output[rows] = residuals[rows].astype(jnp.bfloat16)
        value = grad_low[rows].astype(jnp.float32) + value
        residuals[rows] = value
        parts[1, rows, pl.ds(0, width)] = value.astype(jnp.bfloat16)
        return sums[0] + gain_part, sums[1] + bias_part

    nothing = jnp.zeros((1, width), jnp.float32)
    gain_sum, bias_sum = lax.fori_loop(0, here // 32, norm_two_back, (nothing, nothing))
    side(7).start()
    load(5).start()
    vectors[pl.ds(2, 1)] = gain_sum
    vectors[pl.ds(3, 1)] = bias_sum
    vectors[pl.ds(4, 4)] = jnp.zeros((4, width), jnp.float32)
    down_share(blocks - 1)
    for index in range(2):
        columns = pl.ds(index * half, half)
        part = back_product(parts[1, :, columns], held[index])
        grad_normed[...] = part if index == 0 else grad_normed[...] + part
    grad[...] = grad_normed[...].astype(jnp.bfloat16)
    fetch(0).start()
    pair_whole(1).wait_recv()
    pair_whole(3).wait_recv()
    for quarter in range(4):
        rows = pl.ds(quarter * here, here)
        halving.store(
            1,
            quarter,
            project(lows[pl.ds(0, half), pl.ds(0, here)], heads[0, rows])
            + project(lows[pl.ds(half, half), pl.ds(0, here)], heads[1, rows]),
        )
    pair_whole(3).wait_send()
    pl.semaphore_signal(free_sem.at[0], inc=1, device_id=core, device_id_type=MESH)
    pair_whole(0).wait_recv()
    side(7).wait_recv()
    for quarter in range(4):
        halving.store(
            2,
            quarter,
            project(
                lows[pl.ds(0, half), pl.ds(here, here)], parts[1, :, pl.ds(quarter * 256, 256)]
            )
            + project(
                lows[pl.ds(half, half), pl.ds(here, here)],
                parts[0, :, pl.ds(width + quarter * 256, 256)],
            ),
        )
    for index in range(3):
        pair_whole(index).wait_send()
    side(7).wait_send()
    for index in range(3, 5):
        load(index).start()
    pl.semaphore_wait(free_sem.at[0], 1)
    halving.finish(0, 0)
    load(0).wait()
    load(1).wait()

    def one_pair(pair, carry):
        @pl.when(pair + 1 < pairs)
        def _():
            fetch(pair + 1).start()

        fetch(pair).wait()
        columns = pl.ds(pl.multiple_of(pair * 128, 128), 128)
        others = pl.ds(pl.multiple_of(width + pair * 128, 128), 128)
        out, grad_keys, grad_values = attention_backward_pair(
            query[:, columns],
            columns_two.at[pl.ds(0, width), columns],
            columns_two.at[pl.ds(width, width), columns],
            held.at[lax.rem(pair, 2)],
            inverses[pair],
            grad[:, columns],
            mixed[:, columns],
            lows,
        )
        grad_query[:, columns] = out
        for index, (one, two) in enumerate(zip(grad_keys, grad_values)):
            part, rows = index * 128 // here, pl.ds(index * 128 % here, 128)
            parts[part, rows, columns] = one
            parts[part, rows, others] = two
        for step in range(2):
            for index, place in enumerate((columns, others)):
                remote(
                    parts.at[2 * step + 1, :, place],
                    heads.at[0, pl.ds((2 * step + index) * here, here), columns],
                    swap_send,
                    swap_recv,
                    core,
                ).start()
        return carry

    lax.fori_loop(0, pairs, one_pair, 0)
    side(2).start()
    load(7).start()
    load_part(0).start()
    load_part(1).start()
    swapped = remote(heads.at[0], heads.at[0], swap_send, swap_recv, core)
    swapped.wait()
    pl.semaphore_signal(free_sem.at[1], inc=1, device_id=core, device_id_type=MESH)
    for step in (1, 0):

        def add_rows(index, carry):
            rows = pl.ds(pl.multiple_of(index * 64, 64), 64)
            for index in range(2):
                columns = pl.ds(index * width, width)
                first = pl.multiple_of((2 * step + index) * here + rows.start, 64)
                parts[2 * step, rows, columns] = (
                    parts[2 * step, rows, columns].astype(jnp.float32)
                    + heads[0, pl.ds(first, 64)].astype(jnp.float32)
                ).astype(jnp.bfloat16)
            return carry

        lax.fori_loop(0, here // 64, add_rows, 0)
    load(2).start()
    for index in range(3, 5):
        load(index).wait()

    def from_parts(part, rows):
        return back_product(parts[part, :, pl.ds(0, width)], heads[1, rows]) + back_product(
            parts[part, :, pl.ds(width, width)], heads[2, rows]
        )

    def far_rows(index, carry):
        rows = pl.ds(pl.multiple_of(index * 256, 256), 256)
        normed_send[:, rows] = from_parts(2, rows).astype(jnp.bfloat16)
        return carry

    lax.fori_loop(0, width // 256, far_rows, 0)
    side(3).start()
    pl.semaphore_wait(free_sem.at[1], 1)
    side(0).start()
    side(1).start()
    halving.finish(1, 0)
    halving.finish(2, 0)
    halving.finish(0, 1)

    load(2).wait()

    def own_rows(index, carry):
        rows = pl.ds(pl.multiple_of(index * 256, 256), 256)
        grad_normed[:, rows] = from_parts(0, rows) + back_product(grad_query[...], heads[0, rows])
        return carry

    lax.fori_loop(0, width // 256, own_rows, 0)
    load_part(0).wait()
    load_part(1).wait()

    def select_rows(index, carry):
        first = pl.multiple_of(index * 128, 128)
        row = first + lax.broadcasted_iota(jnp.int32, (128, width), 0)
        lane = lax.broadcasted_iota(jnp.int32, (128, width), 1)
        source = lax.div(row, 16) * 32 + core_index * 16 + lax.rem(row, 16)
        pick = jnp.where(lane == source, 1.0, 0.0).astype(jnp.bfloat16)
        value = back_product(pick[:, :half], held[0]) + back_product(pick[:, half:], held[1])
        value = value.astype(jnp.bfloat16)
        lows[pl.ds(first, 128)] = value[:, :half]
        lows[pl.ds(pl.multiple_of(half + first, 128), 128)] = value[:, half:]
        return carry

    lax.fori_loop(0, half // 128, select_rows, 0)
    load(8).start()
    load(9).start()

    def rows_one(part):
        return lows[pl.ds(part // 2 * half, half), pl.ds(part % 2 * here, here)]

    side(2).wait_recv()
    for quarter in range(4):
        columns = pl.ds(quarter * 256, 256)
        halving.store(
            3,
            quarter,
            project(rows_one(0), grad_query[:, columns])
            + project(rows_one(1), query_landing[:, columns]),
        )
    side(0).wait_recv()
    side(1).wait_recv()
    for quarter in range(4):
        columns = pl.ds(quarter * 512, 512)
        halving.store(
            4,
            quarter,
            project(rows_one(0), parts[0, :, columns])
            + project(rows_one(1), parts[1, :, columns])
            + project(rows_one(2), parts[2, :, columns])
            + project(rows_one(3), parts[3, :, columns]),
        )
    halving.finish(0, 2)
    halving.finish(1, 1)
    halving.finish(2, 1)
    load(5).wait()
    side(3).wait_recv()

    def norm_rows(index, sums):
        rows = pl.ds(pl.multiple_of(index * 32, 32), 32)
        grads = grad_normed[rows] + normed_landing[rows].astype(jnp.float32)
        center = units[rows] - mean_rows(units[rows])
        scale = lax.rsqrt(mean_rows(center * center) + EPS)
        value, gain_part, bias_part = norm_back(center * scale, grads, flat(gain_one), scale)
        grad_hidden[rows] = (residuals[rows] + value).astype(jnp.bfloat16)
        return sums[0] + gain_part, sums[1] + bias_part

    gain_sum, bias_sum = lax.fori_loop(0, here // 32, norm_rows, (nothing, nothing))
    side(4).start()
    vectors[pl.ds(0, 1)] = gain_sum
    vectors[pl.ds(1, 1)] = bias_sum
    vector_start(0)
    load(7).wait()

    def stored_rows(index, carry):
        rows = pl.ds(pl.multiple_of(index * 256, 256), 256)
        below = pl.ds(pl.multiple_of(width + index * 256, 256), 256)
        stored_send[:, rows] = back_product(grad_hidden[...], columns_two[below]).astype(
            jnp.bfloat16
        )
        return carry

    lax.fori_loop(0, width // 256, stored_rows, 0)
    side(5).start()
    load(8).wait()
    load(9).wait()
    side(4).wait_recv()
    for quarter in range(4):
        columns = pl.ds(quarter * 256, 256)
        halving.store(
            5,
            quarter,
            project(held[0, :, pl.ds(0, here)], grad_hidden[:, columns])
            + project(held[0, :, pl.ds(here, here)], hidden_landing[:, columns]),
        )
    halving.finish(0, 3)
    halving.finish(1, 2)
    halving.finish(2, 2)
    halving.finish(3, 0)
    halving.finish(4, 0)
    vector_finish(0)

    def own_grads(index, carry):
        rows = pl.ds(pl.multiple_of(index * 256, 256), 256)
        grad_own[:, rows] = back_product(grad_hidden[...], columns_two[rows]).astype(jnp.bfloat16)
        return carry

    lax.fori_loop(0, width // 256, own_grads, 0)
    halving.finish_direct(5, 0)
    halving.finish(0, 4)
    for job in (1, 2):
        halving.finish(job, 3)
    for job in (3, 4):
        halving.finish(job, 1)
    vector_finish(1)
    halving.finish_direct(5, 1)
    for job in (1, 2):
        halving.finish(job, 4)
    for job in (3, 4):
        halving.finish(job, 2)
    vector_finish(2)
    for job in (3, 4):
        halving.finish(job, 3)
    halving.finish_direct(5, 2)
    for job in (3, 4):
        halving.finish(job, 4)
    vector_finish(3)
    side(5).wait_recv()
    grad_stored[...] = stored_landing[...]
    halving.drain()
    for index in range(7):
        side(index).wait_send()


def backward(inputs, large, small, collective_id):
    query = inputs[0]
    keys = large[0]
    here, width = query.shape
    span = keys.shape[0]
    shapes = [(width // 16, width), (width // 64, 4 * width), (width // 64, width)]
    shapes += [(width // 64, width), (width // 64, 2 * width), (width // 32, width)]
    inside = pl.BlockSpec(memory_space=pltpu.VMEM)
    outside = pl.BlockSpec(memory_space=pl.ANY)
    result_shapes = shapes[:4] + [shapes[3], shapes[3]] + shapes[5:]
    rows_shape = (here, width)
    low_rows = pltpu.VMEM(rows_shape, jnp.bfloat16)
    full_rows = pltpu.VMEM(rows_shape, jnp.float32)
    dma = pltpu.SemaphoreType.DMA
    operands = [query, *large[:3], *inputs[1:], *large[3:], *small]
    specs = [inside] + [outside] * 3 + [inside] * 3 + [outside] * (len(large) - 3)
    specs += [inside] * len(small)
    return pl.pallas_call(
        functools.partial(backward_kernel, shapes),
        in_specs=specs,
        out_specs=[inside] * (4 + len(result_shapes)),
        out_shape=[jax.ShapeDtypeStruct(rows_shape, jnp.bfloat16)] * 3
        + [jax.ShapeDtypeStruct((8, width), jnp.float32)]
        + [jax.ShapeDtypeStruct(shape, jnp.float32) for shape in result_shapes],
        scratch_shapes=[
            pltpu.VMEM((span, 2 * here), jnp.bfloat16),
            pltpu.VMEM((2, span, 2 * here), jnp.bfloat16),
            dma((2,)),
            pltpu.VMEM((4, here, 2 * width), jnp.bfloat16),
            pltpu.SemaphoreType.REGULAR((2,)),
            dma,
            dma,
            low_rows,
            low_rows,
            dma((8,)),
            dma((8,)),
            pltpu.VMEM((2 * width, width), jnp.bfloat16),
            pltpu.VMEM((3, width, width), jnp.bfloat16),
            dma((12,)),
            full_rows,
            full_rows,
            full_rows,
            low_rows,
            low_rows,
            low_rows,
            low_rows,
            low_rows,
            low_rows,
            pltpu.VMEM((8, 8, width), jnp.float32),
            dma((8,)),
            dma((8,)),
            pltpu.VMEM((width, here), jnp.bfloat16),
            pltpu.VMEM((here, 1), jnp.float32),
            dma((2, 2)),
            dma((4,)),
            dma((4,)),
            dma((8,)),
            dma((2,)),
        ]
        + Halving.scratch(shapes),
        compiler_params=pltpu.CompilerParams(
            collective_id=collective_id,
            has_side_effects=True,
            vmem_limit_bytes=62 * 2**20,
        ),
    )(*operands)


def mean_rows(value):
    return jnp.mean(value, axis=-1, keepdims=True)


def copy_kernel(*refs):
    count = (len(refs) - 1) // 3
    ways = []
    for index in range(count):
        source, target, stop = refs[index], refs[count + index], refs[2 * count + index]
        ways.append(
            (
                pltpu.make_async_copy(source, stop, refs[-1].at[0, index]),
                pltpu.make_async_copy(stop, target, refs[-1].at[1, index]),
            )
        )
    for into, _ in ways:
        into.start()
    for into, out in ways:
        into.wait()
        out.start()
    for _, out in ways:
        out.wait()


def copied(arrays):
    outside = pl.BlockSpec(memory_space=pl.ANY)
    return pl.pallas_call(
        copy_kernel,
        in_specs=[outside] * len(arrays),
        out_specs=[outside] * len(arrays),
        out_shape=[jax.ShapeDtypeStruct(array.shape, array.dtype) for array in arrays],
        scratch_shapes=[pltpu.VMEM(array.shape, array.dtype) for array in arrays]
        + [pltpu.SemaphoreType.DMA((2, len(arrays)))],
    )(*arrays)


def on_device(
    states,
    mirror,
    w_skip,
    norm1_gain,
    norm1_bias,
    w_query,
    w_key,
    w_value,
    w_out,
    norm2_gain,
    norm2_bias,
    w_up,
    w_down,
    out_grad,
    lengths,
    infill_spans,
):
    rows_here = states.shape[2]
    model_width = states.shape[3]
    seq = lax.axis_index("seq")
    (
        hidden,
        query,
        inverses,
        mixed_rows,
        grad_low,
        joined_mine,
        shares,
        keys_all,
        values_all,
        normed_all,
        joined_other,
    ) = forward(
        lengths,
        infill_spans,
        states.reshape(rows_here, model_width),
        mirror.reshape(rows_here, model_width),
        out_grad.reshape(rows_here, model_width),
        [norm1_gain, norm1_bias],
        (w_skip, w_query, w_key, w_value),
        2,
    )
    results = backward(
        [query, inverses, mixed_rows, grad_low],
        [
            keys_all,
            values_all,
            shares,
            hidden,
            w_out,
            w_up,
            w_down,
            w_query,
            w_key,
            w_value,
            w_skip,
            normed_all,
            joined_mine,
            joined_other,
        ],
        [norm1_gain, norm2_gain, norm2_bias],
        1,
    )
    sums = results[3]
    (
        output,
        grad_own,
        grad_stored,
        down_sum,
        up_sum,
        out_sum,
        query_sum,
        key_sum,
        value_sum,
        skip_sum,
    ) = copied(results[:3] + results[4:])
    shard = lax.axis_index("dp") * 4 + seq
    piece = model_width // 64
    sums = lax.dynamic_slice(sums, (0, shard * piece), (4, piece))
    return (
        output.reshape(states.shape),
        grad_own.reshape(states.shape),
        grad_stored.reshape(states.shape),
        skip_sum[None],
        sums[0][None],
        sums[1][None],
        query_sum[None],
        key_sum[None],
        value_sum[None],
        out_sum[None],
        sums[2][None],
        sums[3][None],
        up_sum[None],
        down_sum[None],
    )


def solution(mesh):
    in_specs = (
        P("section", "dp", "seq", None),
        P("section", "dp", "seq", None),
        P(),
        P(),
        P(),
        P(),
        P(),
        P(),
        P(),
        P(),
        P(),
        P(),
        P(),
        P("section", "dp", "seq", None),
        P("section", "dp", None),
        P("section", "dp", None, None),
    )
    out_specs = (
        P("section", "dp", "seq", None),
        P("section", "dp", "seq", None),
        P("section", "dp", "seq", None),
        P("section", ("dp", "seq"), None),
        P("section", ("dp", "seq")),
        P("section", ("dp", "seq")),
        P("section", ("dp", "seq"), None),
        P("section", ("dp", "seq"), None),
        P("section", ("dp", "seq"), None),
        P("section", ("dp", "seq"), None),
        P("section", ("dp", "seq")),
        P("section", ("dp", "seq")),
        P("section", ("dp", "seq"), None),
        P("section", ("dp", "seq"), None),
    )
    return jax.shard_map(
        on_device, mesh=mesh, in_specs=in_specs, out_specs=out_specs, check_vma=False
    )
```

```python
import functools

import jax
import jax.numpy as jnp
from jax.experimental import pallas as pl
from jax.experimental.pallas import tpu as pltpu
from jax import lax
from jax.sharding import PartitionSpec as P

LOG2E = 1.4426950408889634
LN2 = 0.6931471805599453


EPS = 1e-05


def project(left, right):
    return jnp.dot(left, right, preferred_element_type=jnp.float32)


def rows_product(left, right):
    return lax.dot_general(
        left, right, (((0,), (0,)), ((), ())), preferred_element_type=jnp.float32
    )


def back_product(left, right):
    return lax.dot_general(
        left, right, (((1,), (1,)), ((), ())), preferred_element_type=jnp.float32
    )


MESH = pl.DeviceIdType.MESH
NEAR, WRAP = (0, 3, 1, 2), (0, 1, 3, 2)
QUARTERS = (("x", NEAR), ("x", WRAP), ("z", NEAR), ("z", WRAP))


def flip(value, mask):
    if mask == 1:
        return value + 1 - 2 * lax.rem(value, 2)
    if mask == 2:
        return lax.rem(value + 2, 4)
    if mask == 3:
        return 3 - value
    return value


def block_place(quarter, outer, inner, x, z):
    first, order = QUARTERS[quarter]
    if first == "x":
        return flip(z, order[inner]) * 4 + flip(x, order[outer])
    return flip(z, order[outer]) * 4 + flip(x, order[inner])


def stage_partner(quarter, stage, x, z, seq):
    if stage == 4:
        return {"seq": lax.rem(seq + 2, 4)}
    first, order = QUARTERS[quarter]
    mask = order[2] if stage % 2 == 0 else order[1]
    if (first == "x") == (stage < 2):
        return {"dp": z * 4 + flip(x, mask)}
    return {"dp": flip(z, mask) * 4 + x}


def remote(source, target, send, recv, device):
    return pltpu.make_async_remote_copy(
        src_ref=source,
        dst_ref=target,
        send_sem=send,
        recv_sem=recv,
        device_id=device,
        device_id_type=MESH,
    )


def greet(devices):
    for device in devices:
        pl.semaphore_signal(
            pltpu.get_barrier_semaphore(), inc=1, device_id=device, device_id_type=MESH
        )


def enter(devices):
    pl.semaphore_wait(pltpu.get_barrier_semaphore(), len(devices))


def add_blocks(count, total, other):
    def one(index, carry):
        total[index] = (
            total[index].astype(jnp.float32) + other[index].astype(jnp.float32)
        ).astype(jnp.bfloat16)
        return carry

    lax.fori_loop(0, count, one, 0)


def place_here():
    dp, seq = lax.axis_index("dp"), lax.axis_index("seq")
    return lax.div(dp, 4), lax.rem(dp, 4), seq


def either(one, two):
    return 2 * lax.rem(lax.div(one, 2) + lax.div(two, 2), 2) + lax.rem(one + two, 2)


def relative_place(quarter, z, x, there):
    first, order = QUARTERS[quarter]

    def position(value):
        if order == NEAR:
            return 2 * value - lax.div(value, 2) - 4 * lax.div(value, 3)
        return value + lax.div(value, 2) * (1 - 2 * lax.rem(value, 2))

    z_place = position(either(z, lax.div(there, 4)))
    x_place = position(either(x, lax.rem(there, 4)))
    return x_place * 4 + z_place if first == "x" else z_place * 4 + x_place


class Halving:
    def __init__(self, shapes, results, scratch):
        self.shapes, self.results = shapes, results
        scratch = list(scratch)
        count = len(shapes)
        self.work = scratch[:count]
        self.landings = [scratch[count + 5 * job : count + 5 * job + 5] for job in range(count)]
        self.landings[-1] = self.landings[-1][:3]
        self.send_sem, self.recv_sem = scratch[-2:]
        self.z, self.x, self.seq = place_here()
        self.y = lax.div(self.seq, 2)

    @staticmethod
    def scratch(shapes):
        shapes_of = [(4, 16, 2 * rows, width // 4) for rows, width in shapes]
        for job, (rows, width) in enumerate(shapes):
            direct = job == len(shapes) - 1
            shapes_of += [(4, blocks, 2 * rows, width // 4) for blocks in (8, 4)]
            if direct:
                shapes_of.append((4, 7, rows, width // 4))
            else:
                shapes_of += [(4, blocks, 2 * rows, width // 4) for blocks in (2, 1)]
                shapes_of.append((4, rows, width // 4))
        sems = pltpu.SemaphoreType.DMA((len(shapes), 4, 5))
        return [pltpu.VMEM(shape, jnp.bfloat16) for shape in shapes_of] + [sems, sems]

    def put(self, job, quarter, there, value):
        place = relative_place(quarter, self.z, self.x, there)
        self.work[job][quarter, place] = value.astype(jnp.bfloat16)
        return place

    def put_and_send(self, job, quarter, there, value):
        place = self.put(job, quarter, there, value)

        @pl.when(place >= 8)
        def _():
            remote(
                self.work[job].at[quarter, place],
                self.landings[job][0].at[quarter, place - 8],
                self.send_sem.at[job, quarter, 0],
                self.recv_sem.at[job, quarter, 0],
                stage_partner(quarter, 0, self.x, self.z, self.seq),
            ).start()

    def store(self, job, quarter, value):
        rows = 2 * self.shapes[job][0]
        for index in range(16):
            self.put(job, quarter, index, value[index * rows : (index + 1) * rows])
        self.copy(job, quarter, 0).start()

    def copy(self, job, quarter, stage):
        rows = self.shapes[job][0]
        if stage < 4:
            size = 8 >> stage
            source = self.work[job].at[quarter, pl.ds(size, size)]
        else:
            away = pl.multiple_of((1 - self.y) * rows, 16)
            source = self.work[job].at[quarter, 0, pl.ds(away, rows)]
        return remote(
            source,
            self.landings[job][stage].at[quarter],
            self.send_sem.at[job, quarter, stage],
            self.recv_sem.at[job, quarter, stage],
            stage_partner(quarter, stage, self.x, self.z, self.seq),
        )

    def finish(self, job, stage):
        rows, width = self.shapes[job]
        for quarter in range(4):
            work = self.work[job].at[quarter]
            landing = self.landings[job][stage].at[quarter]
            self.copy(job, quarter, stage).wait_recv()
            if stage < 4:
                add_blocks(8 >> stage, work, landing)
                self.copy(job, quarter, stage + 1).start()
            else:
                mine = pl.multiple_of(self.y * rows, 16)
                total = work[0, pl.ds(mine, rows)].astype(jnp.float32)
                first = quarter * width // 4
                result = self.results[job][first // 4096 if width == 4096 else first // 1024]
                result[:, pl.ds(first % result.shape[1], width // 4)] = total + landing[
                    ...
                ].astype(jnp.float32)

    def direct(self, job, quarter, step):
        rows = self.shapes[job][0]
        first, order = QUARTERS[quarter]
        inner, away = step // 2, step % 2
        if first == "x":
            dp = flip(self.z, order[inner]) * 4 + self.x
        else:
            dp = self.z * 4 + flip(self.x, order[inner])
        part = pl.multiple_of((1 - self.y if away else self.y) * rows, 16)
        return remote(
            self.work[job].at[quarter, inner, pl.ds(part, rows)],
            self.landings[job][2].at[quarter, step - 1],
            self.send_sem.at[job, quarter, 2],
            self.recv_sem.at[job, quarter, 2],
            {"dp": dp, "seq": flip(self.seq, 2) if away else self.seq},
        )

    def finish_direct(self, job, stage):
        rows, width = self.shapes[job]
        for quarter in range(4):
            work = self.work[job].at[quarter]
            landing = self.landings[job][stage].at[quarter]
            if stage < 2:
                self.copy(job, quarter, stage).wait_recv()
                add_blocks(8 >> stage, work, landing)
                if stage == 0:
                    self.copy(job, quarter, 1).start()
                else:
                    for step in range(1, 8):
                        self.direct(job, quarter, step).start()
            else:
                remote(
                    landing, landing, self.send_sem.at[job, quarter, 2],
                    self.recv_sem.at[job, quarter, 2], {"seq": flip(self.seq, 2)},
                ).wait()
                mine = pl.multiple_of(self.y * rows, 16)
                total = work[0, pl.ds(mine, rows)].astype(jnp.float32)
                for step in range(7):
                    total = total + landing[step].astype(jnp.float32)
                self.results[job][0][:, pl.ds(quarter * width // 4, width // 4)] = total

    def drain(self):
        last = len(self.shapes) - 1
        for job in range(last + 1):
            for quarter in range(4):
                for stage in range(2 if job == last else 5):
                    self.copy(job, quarter, stage).wait_send()


def attention_backward_pair(query, keys, values, share, inverse, grad, mixed, lows):
    span = keys.shape[0]
    here = query.shape[0]
    chunk = span // 2
    lane = lax.broadcasted_iota(jnp.int32, query.shape, 1)
    zero = jnp.zeros(query.shape, query.dtype)
    queries = jnp.concatenate(
        [jnp.where(lane < 64, query, zero), jnp.where(lane >= 64, query, zero)], axis=0
    )
    turned = grad.astype(jnp.float32).T
    product = turned * mixed.astype(jnp.float32).T
    centre = jnp.concatenate(
        [
            jnp.sum(product[:64], axis=0, keepdims=True),
            jnp.sum(product[64:], axis=0, keepdims=True),
        ],
        axis=1,
    )
    none = jnp.zeros((64, here), jnp.float32)
    sets = []
    for part in range(2):
        factor = inverse[part : part + 1]
        first = turned[:64] * factor[:, :here]
        second = turned[64:] * factor[:, here:]
        grads = jnp.concatenate(
            [jnp.concatenate([first, none], axis=1), jnp.concatenate([none, second], axis=1)],
            axis=0,
        ).astype(jnp.bfloat16)
        sets.append((grads, grads.T, centre * factor))
    grad_keys, grad_values = [], []
    for index in range(span // chunk):
        rows = pl.ds(index * chunk, chunk)
        part = share[rows]
        grads, grads_back, centre = sets[index]
        grad_share = project(values[rows], grads)
        grad_score = (part.astype(jnp.float32) * (grad_share - centre)).astype(jnp.bfloat16)
        lows[rows] = grad_score
        grad_keys.append((project(grad_score, queries) * LN2).astype(jnp.bfloat16))
        grad_values.append(project(part, grads_back).astype(jnp.bfloat16))
    out = rows_product(keys[...], lows[...])
    out = jnp.concatenate([out[:64, :here], out[64:, here:]], axis=0)
    return (out.T * 0.125).astype(jnp.bfloat16), grad_keys, grad_values


def flat(vector):
    return vector[...].astype(jnp.float32).reshape(1, vector.shape[0])


def forward_kernel(
    lengths, spans, own, stored, out_grad, gain_one, bias_one, w_skip, w_query, w_key, w_value,
    hidden, query, inverses, mixed, grad_low, kept, shares, keys_out, values_out, normed_out, other,
    partner, normed, joined_sent, joined_landing, turned, w_rows, heads, keys, values,
    distance, scores, exponents, outs, tops, load_sem, send_sem, recv_sem, share_sem,
):
    seq = lax.axis_index("seq")
    core_index = lax.rem(seq, 2)
    core, far = {"seq": flip(seq, 1)}, {"seq": flip(seq, 2)}
    section = {"section": 1 - lax.axis_index("section")}
    here, width = own.shape
    span = keys.shape[0]
    half = width // 2
    pairs = width // 128
    parts = 4
    piece = here // parts

    loads = [
        pltpu.make_async_copy(source, target, load_sem.at[index])
        for index, (source, target) in enumerate(
            (
                (w_skip, w_rows),
                (w_query, heads.at[0]),
                (w_key, heads.at[1]),
                (w_value, heads.at[2]),
                (keys, keys_out),
                (values, values_out),
                (normed, normed_out),
                (joined_landing, other),
            )
        )
    ]

    def send(index, part):
        rows = pl.ds(part * piece, piece)
        source, target, device = (
            (stored.at[rows], partner.at[rows], section),
            (normed.at[rows], normed.at[pl.ds(here + part * piece, piece)], core),
            (normed.at[rows], normed.at[pl.ds(2 * here + part * piece, piece)], far),
            (
                normed.at[pl.ds(2 * here + part * piece, piece)],
                normed.at[pl.ds(3 * here + part * piece, piece)],
                core,
            ),
            (
                joined_sent.at[pl.ds(part % 2 * half, half)],
                joined_landing.at[pl.ds(part % 2 * half, half)],
                core,
            ),
        )[index]
        return remote(source, target, send_sem.at[index, part], recv_sem.at[index, part], device)

    greet([core, far, section])
    for index in range(4):
        loads[index].start()
    enter([core, far, section])
    for part in range(parts):
        send(0, part).start()

    bounds = []
    start = jnp.int32(0)
    for index in range(4):
        bounds.append((start, start + lengths[0, 0, index]))
        start = start + lengths[0, 0, index]

    def segment(places):
        return sum((places >= bounds[index][1]).astype(jnp.int32) for index in range(4))

    place = seq * here + lax.broadcasted_iota(jnp.int32, (here, 1), 0)
    inside = jnp.zeros((here, 1), jnp.int32)
    for index in range(4):
        low_end = bounds[index][0] + spans[0, 0, pl.ds(index, 1), pl.ds(0, 1)]
        high_end = bounds[index][0] + spans[0, 0, pl.ds(index, 1), pl.ds(1, 1)]
        inside += (place >= low_end).astype(jnp.int32) * (place < high_end).astype(jnp.int32)
    grad_low[...] = jnp.where(
        inside > 0, out_grad[...].astype(jnp.float32), 0.0
    ).astype(jnp.bfloat16)
    query_place = seq * here + lax.broadcasted_iota(jnp.int32, (1, here), 1)
    query_segment = segment(query_place)
    for index in range(4):
        key_place = flip(seq, index) * here + lax.broadcasted_iota(jnp.int32, (here, 1), 0)
        gap = jnp.abs(query_place - key_place).astype(jnp.float32)
        distance[pl.ds(index * here, here)] = jnp.where(
            segment(key_place) == query_segment, gap, 1e30
        )

    def joined_rows(part, source):
        turned[...] = source[...].T

        def keep(row, value):
            kept[pl.ds(part * half + row, 32)] = value

        def pass_on(row, value):
            joined_sent[pl.ds(part * half + row, 32)] = value

        split_cores(core_index, turned, keep, pass_on, 32)
        send(4, part).start()

    joined_rows(0, own)
    loads[0].wait()
    hidden[...] = project(own[...], w_rows[pl.ds(0, width)])
    gain, bias = flat(gain_one), flat(bias_one)
    for part in range(parts):
        rows = pl.ds(part * piece, piece)
        send(0, part).wait_recv()
        value = hidden[rows] + project(partner[rows], w_rows[pl.ds(width, width)])
        hidden[rows] = value
        center = value - mean_rows(value)
        scale = lax.rsqrt(mean_rows(center * center) + EPS)
        normed[rows] = (center * scale * gain + bias).astype(jnp.bfloat16)
        send(2, part).start()
        send(1, part).start()
    for index in range(1, 4):
        loads[index].wait()
    scale = 0.125 * LOG2E
    query[...] = (project(normed[pl.ds(0, here)], heads[0]) * scale).astype(jnp.bfloat16)

    def both(first, count):
        rows = pl.ds(first, count)
        keys[rows] = project(normed[rows], heads[1]).astype(jnp.bfloat16)
        values[rows] = project(normed[rows], heads[2]).astype(jnp.bfloat16)

    def attend(part, pair):
        columns = pl.ds(pl.multiple_of(pair * 128, 128), 128)
        base = part * 2 * here
        value = query[:, columns]
        lane = lax.broadcasted_iota(jnp.int32, value.shape, 1)
        zero = jnp.zeros(value.shape, value.dtype)
        stacked = jnp.concatenate(
            [jnp.where(lane < 64, value, zero), jnp.where(lane >= 64, value, zero)], axis=0
        )
        head = 2 * pair + 1 + lax.div(lax.broadcasted_iota(jnp.int32, (1, 2 * here), 1), here)
        slope = LOG2E * jnp.exp2(head.astype(jnp.float32) * -0.5)
        rows = pl.ds(base, 2 * here)
        gap = distance[rows]
        score = back_product(keys[rows, columns], stacked)
        score = score - slope * jnp.concatenate([gap, gap], axis=1)
        scores[...] = score
        top = jnp.max(score.reshape(here // 4, 8, 2 * here), axis=0)
        top = jnp.max(top, axis=0, keepdims=True)
        exponents[pair, rows] = jnp.exp2(scores[...] - top).astype(jnp.bfloat16)
        pltpu.make_async_copy(
            exponents.at[pair, rows], shares.at[pair, rows], share_sem
        ).start()
        back = jnp.concatenate(
            [values[rows, columns].T, jnp.ones((16, 2 * here), jnp.bfloat16)], axis=0
        )
        return project(back, exponents[pair, rows]), top

    for part in range(parts):
        send(1, part).wait_recv()
    both(0, 2 * here)
    joined_rows(1, partner)

    def near(pair, carry):
        out, top = attend(0, pair)
        outs[pair] = out
        tops[pair] = top
        return carry

    lax.fori_loop(0, pairs - 3, near, 0)
    for part in range(parts - 1):
        send(2, part).wait_recv()
        send(3, part).start()
    lax.fori_loop(pairs - 3, pairs, near, 0)
    send(2, parts - 1).wait_recv()
    send(3, parts - 1).start()
    both(2 * here, here)
    for part in range(parts):
        send(3, part).wait_recv()
    both(3 * here, here)
    for index in range(4, 7):
        loads[index].start()

    def away(pair, carry):
        out, top = attend(1, pair)
        first, first_top = outs[pair], tops[pair]
        best = jnp.maximum(top, first_top)
        one, two = jnp.exp2(first_top - best), jnp.exp2(top - best)
        total = 1.0 / (one * first[128:129] + two * out[128:129])
        one, two = one * total, two * total
        inverses[pair, pl.ds(0, 1)] = one
        inverses[pair, pl.ds(1, 1)] = two
        out = first[:128] * one + out[:128] * two
        out = jnp.concatenate([out[:64, :here], out[64:, here:]], axis=0)
        columns = pl.ds(pl.multiple_of(pair * 128, 128), 128)
        mixed[:, columns] = out.T.astype(jnp.bfloat16)
        return carry

    lax.fori_loop(0, pairs, away, 0)
    for part in range(2):
        send(4, part).wait_recv()
    loads[7].start()
    pltpu.make_async_copy(exponents, shares, share_sem).wait()
    for index in range(4, 8):
        loads[index].wait()
    for index in range(5):
        for part in range(parts if index < 4 else 2):
            send(index, part).wait_send()


def forward(lengths, spans, own, stored, out_grad, norms, weights, collective_id):
    here, width = own.shape
    span = 4 * here
    pairs = width // 128
    inside = pl.BlockSpec(memory_space=pltpu.VMEM)
    outside = pl.BlockSpec(memory_space=pl.ANY)
    scalars = pl.BlockSpec(memory_space=pltpu.SMEM)
    low_shape = lambda *shape: jax.ShapeDtypeStruct(shape, jnp.bfloat16)
    low_rows = lambda *shape: pltpu.VMEM(shape, jnp.bfloat16)
    dma = pltpu.SemaphoreType.DMA
    return pl.pallas_call(
        forward_kernel,
        in_specs=[scalars, inside, inside, outside, inside, inside, inside] + [outside] * 4,
        out_specs=[inside] * 6 + [outside] * 5,
        out_shape=[
            jax.ShapeDtypeStruct((here, width), jnp.float32),
            low_shape(here, width),
            jax.ShapeDtypeStruct((pairs, 2, 2 * here), jnp.float32),
            low_shape(here, width),
            low_shape(here, width),
            low_shape(width, here),
            low_shape(pairs, span, 2 * here),
            low_shape(span, width),
            low_shape(span, width),
            low_shape(span, width),
            low_shape(width, here),
        ],
        scratch_shapes=[
            low_rows(here, width),
            low_rows(span, width),
            low_rows(width, here),
            low_rows(width, here),
            low_rows(width, here),
            low_rows(2 * width, width),
            low_rows(3, width, width),
            low_rows(span, width),
            low_rows(span, width),
            pltpu.VMEM((span, here), jnp.float32),
            pltpu.VMEM((2 * here, 2 * here), jnp.float32),
            low_rows(pairs, span, 2 * here),
            pltpu.VMEM((pairs, 144, 2 * here), jnp.float32),
            pltpu.VMEM((pairs, 1, 2 * here), jnp.float32),
            dma((8,)),
            dma((5, 4)),
            dma((5, 4)),
            dma,
        ],
        compiler_params=pltpu.CompilerParams(
            collective_id=collective_id,
            has_side_effects=True,
            vmem_limit_bytes=56 * 2**20,
        ),
    )(lengths, spans, own, stored, out_grad, *norms, *weights)


def split_cores(core, source, kept, sent, rows):
    for index in range(source.shape[0] // (2 * rows)):
        mine = pl.multiple_of(index * 2 * rows + core * rows, rows)
        away = pl.multiple_of(index * 2 * rows + (1 - core) * rows, rows)
        kept(index * rows, source[pl.ds(mine, rows)])
        sent(index * rows, source[pl.ds(away, rows)])


def backward_kernel(
    shapes, query, keys, values, shares, inverses, mixed, grad_low, hidden, w_out, w_up, w_down,
    w_query, w_key, w_value, w_skip, normed_all, joined_kept, joined_other, gain_one, gain_two, bias_two,
    output, grad_own, grad_stored, vectors, *refs,
):
    refs = list(refs)
    take = lambda n: [refs.pop(0) for _ in range(n)]
    results = [take(1), take(1), take(1), take(1), take(2), take(1)]
    lows, held, held_sem, parts, free_sem, swap_send, swap_recv = take(7)
    grad_query, query_landing, side_send, side_recv = take(4)
    columns_two, heads, load_sem, units, residuals = take(5)
    grad_normed, normed_send, normed_landing, grad_hidden, hidden_landing = take(5)
    stored_send, stored_landing, vector_landing, vector_send, vector_recv = take(5)
    turned, inverse_two, block_sem, pair_send, pair_recv, act_recv, part_sem = take(7)
    grad = grad_hidden
    halving = Halving(shapes, results, refs)
    z, x, seq = place_here()
    core_index = lax.rem(seq, 2)
    core = {"seq": flip(seq, 1)}
    far = {"seq": flip(seq, 2)}
    section = {"section": 1 - lax.axis_index("section")}
    pairs = shares.shape[0]
    here, width = query.shape
    block = 512
    blocks = w_up.shape[1] // block
    half = width // 2

    def fetch(pair):
        slot = lax.rem(pair, 2)
        return pltpu.make_async_copy(shares.at[pair], held.at[slot], held_sem.at[slot])

    def load(index):
        source, target = (
            (keys, columns_two.at[pl.ds(0, width)]),
            (values, columns_two.at[pl.ds(width, width)]),
            (w_query, heads.at[0]),
            (w_key, heads.at[1]),
            (w_value, heads.at[2]),
            (hidden, units),
            (hidden, residuals),
            (w_skip, columns_two),
            (joined_kept, held.at[0, :, pl.ds(0, here)]),
            (joined_other, held.at[0, :, pl.ds(here, here)]),
            (w_out.at[:, pl.ds(0, half)], held.at[0]),
            (w_out.at[:, pl.ds(half, half)], held.at[1]),
        )[index]
        return pltpu.make_async_copy(source, target, load_sem.at[index])

    def load_part(index):
        return pltpu.make_async_copy(
            normed_all.at[:, pl.ds(index * half, half)], held.at[index], part_sem.at[index]
        )

    def load_block(step):
        slot = lax.rem(step, 2)
        place = pl.ds(pl.multiple_of(step * block, block), block)
        there = pl.ds(pl.multiple_of(slot * block, block), block)
        return (
            pltpu.make_async_copy(
                w_up.at[:, place], columns_two.at[pl.ds(width, width), there], block_sem.at[slot, 0]
            ),
            pltpu.make_async_copy(
                w_down.at[place], columns_two.at[there], block_sem.at[slot, 1]
            ),
        )

    def side(index):
        source, target, device = (
            (parts.at[0], parts.at[1], core),
            (parts.at[2], parts.at[3], core),
            (grad_query, query_landing, core),
            (normed_send, normed_landing, far),
            (grad_hidden, hidden_landing, core),
            (stored_send, stored_landing, section),
            (grad_low, parts.at[0, :, pl.ds(0, width)], core),
            (parts.at[1, :, pl.ds(0, width)], parts.at[0, :, pl.ds(width, width)], core),
        )[index]
        return remote(source, target, side_send.at[index], side_recv.at[index], device)

    def pair_half(index, part):
        lanes = pl.ds((1 - index) * here, here)
        return remote(
            parts.at[3, :, pl.ds((2 * index + part) * here, here)],
            lows.at[pl.ds(half + part * here, here), lanes],
            pair_send.at[index],
            pair_recv.at[index],
            core,
        )

    def pair_whole(index):
        if index == 2:
            source = target = parts.at[2]
        elif index == 3:
            source = target = heads.at[1]
        else:
            source = target = lows.at[pl.ds(half, half), pl.ds((1 - index) * here, here)]
        return remote(source, target, pair_send.at[index], pair_recv.at[index], core)

    def act_place(step, base):
        rows = pl.ds(pl.multiple_of(base + lax.rem(step, 2) * here, here), here)
        return rows, pl.ds(pl.multiple_of(lax.div(step, 2) * here, here), here)

    def act_copy(step):
        rows, lanes = act_place(step, half)
        return remote(
            parts.at[2, :, pl.ds(pl.multiple_of(step * here, here), here)],
            heads.at[2, rows, lanes],
            pair_send.at[2],
            act_recv.at[step],
            core,
        )

    def up_copy(step):
        rows = pl.ds(pl.multiple_of(lax.div(step, 2) * here, here), here)
        lanes = pl.ds(pl.multiple_of(lax.rem(step, 2) * block, block), block)
        return remote(
            heads.at[0, rows, lanes],
            heads.at[1, rows, lanes],
            pair_send.at[3],
            pair_recv.at[3],
            core,
        )

    vector_steps = [
        [core],
        [{"dp": z * 4 + flip(x, mask)} for mask in (1, 2, 3)],
        [{"dp": flip(z, mask) * 4 + x} for mask in (1, 2, 3)],
        [far],
    ]
    vector_slots = (0, 1, 4, 7)

    def vector_copies(step):
        return [
            remote(
                vectors,
                vector_landing.at[slot],
                vector_send.at[slot],
                vector_recv.at[slot],
                device,
            )
            for slot, device in enumerate(vector_steps[step], vector_slots[step])
        ]

    def vector_start(step):
        for copy in vector_copies(step):
            copy.start()

    def vector_finish(step):
        copies = vector_copies(step)
        for copy in copies:
            copy.wait()
        for index in range(len(copies)):
            vectors[...] += vector_landing[vector_slots[step] + index]
        if step < 3:
            vector_start(step + 1)

    devices = [core, far, section]
    for mask in (1, 2, 3):
        for dp in (z * 4 + flip(x, mask), flip(z, mask) * 4 + x):
            devices += [{"dp": dp}, {"dp": dp, "seq": flip(seq, 2)}]
    greet(devices)
    for index in (6, 10, 11):
        load(index).start()
    for copy in load_block(0):
        copy.start()

    def share_rows(index):
        def kept(row, value):
            lows[pl.ds(row, 16), pl.ds((1 - index) * here, here)] = value

        def sent(row, value):
            lanes = pl.ds((2 * index + row // here) * here, here)
            parts[3, pl.ds(row % here, 16), lanes] = value

        split_cores(core_index, turned, kept, sent, 16)

    turned[...] = mixed[...].T
    share_rows(0)
    load(6).wait()
    for index in range(2):
        load(10 + index).wait()
        columns = pl.ds(index * half, half)
        residuals[:, columns] += project(mixed[...], held[index])

    def norm_two_rows(index, carry):
        rows = pl.ds(pl.multiple_of(index * 32, 32), 32)
        value = residuals[rows]
        center = value - mean_rows(value)
        scale = lax.rsqrt(mean_rows(center * center) + EPS)
        center = center * scale
        units[rows] = center
        inverse_two[rows] = scale
        stored_send[rows] = (center * flat(gain_two) + flat(bias_two)).astype(jnp.bfloat16)
        grad_normed[rows] = jnp.zeros_like(value)
        return carry

    lax.fori_loop(0, here // 32, norm_two_rows, 0)
    turned[...] = stored_send[...].T
    share_rows(1)
    enter(devices)
    side(6).start()
    for index in range(2):
        pair_half(index, 0).start()
        pair_half(index, 1).start()

    def down_share(step):
        act_copy(step).wait_recv()
        rows, lanes = act_place(step, 0)
        rows_other, _ = act_place(step, half)
        value = project(heads[2, rows, lanes], grad_low[...]) + project(
            heads[2, rows_other, lanes], parts[0, :, pl.ds(0, width)]
        )
        for index in range(2):
            for quarter in range(4):
                halving.put_and_send(
                    0,
                    quarter,
                    2 * step + index,
                    value[index * 128 : index * 128 + 128, quarter * 256 : quarter * 256 + 256],
                )

    def one_block(step, carry):
        @pl.when(step + 1 < blocks)
        def _():
            for copy in load_block(step + 1):
                copy.start()

        for copy in load_block(step):
            copy.wait()
        there = pl.ds(pl.multiple_of(lax.rem(step, 2) * block, block), block)
        up_part = columns_two.at[pl.ds(width, width), there]
        down_part = columns_two.at[there]
        upward = project(stored_send[...], up_part[...])
        cdf = 0.5 * (1.0 + lax.erf(upward * 0.7071067811865476))
        act = (upward * cdf).astype(jnp.bfloat16)
        density = jnp.exp(upward * upward * -0.5) * 0.3989422804014327
        slope = cdf + upward * density
        grad_up = (back_product(grad_low[...], down_part[...]) * slope).astype(jnp.bfloat16)
        residuals[...] += project(act, down_part[...])
        grad_normed[...] += back_product(grad_up, up_part[...])
        up_rows = pl.ds(pl.multiple_of(lax.div(step, 2) * here, here), here)
        heads[0, up_rows, there] = grad_up
        up_copy(step).start()
        turned[pl.ds(0, block)] = act.T
        rows, lanes = act_place(step, 0)
        first = lax.rem(step, 2) * here
        sent_lanes = pl.ds(pl.multiple_of(step * here, here), here)

        def kept(row, value):
            heads[2, pl.ds(pl.multiple_of(first + row, 64), 64), lanes] = value

        def sent(row, value):
            parts[2, pl.ds(row, 64), sent_lanes] = value

        split_cores(core_index, turned.at[pl.ds(0, block)], kept, sent, 64)
        act_copy(step).start()

        @pl.when(step == 1)
        def _():
            side(6).wait_recv()

        @pl.when(step > 0)
        def _():
            down_share(step - 1)

        return carry

    lax.fori_loop(0, blocks, one_block, 0)
    load(0).start()
    load(1).start()

    def norm_back(ones, grads, gain, inverse):
        scaled = grads * gain
        value = scaled - mean_rows(scaled) - ones * mean_rows(scaled * ones)
        return (
            inverse * value,
            jnp.sum(grads * ones, axis=0, keepdims=True),
            jnp.sum(grads, axis=0, keepdims=True),
        )

    def norm_two_back(index, sums):
        rows = pl.ds(pl.multiple_of(index * 32, 32), 32)
        value, gain_part, bias_part = norm_back(
            units[rows], grad_normed[rows], flat(gain_two), inverse_two[rows]
        )
        output[rows] = residuals[rows].astype(jnp.bfloat16)
        value = grad_low[rows].astype(jnp.float32) + value
        residuals[rows] = value
        parts[1, rows, pl.ds(0, width)] = value.astype(jnp.bfloat16)
        return sums[0] + gain_part, sums[1] + bias_part

    nothing = jnp.zeros((1, width), jnp.float32)
    gain_sum, bias_sum = lax.fori_loop(0, here // 32, norm_two_back, (nothing, nothing))
    side(7).start()
    load(5).start()
    vectors[pl.ds(2, 1)] = gain_sum
    vectors[pl.ds(3, 1)] = bias_sum
    vectors[pl.ds(4, 4)] = jnp.zeros((4, width), jnp.float32)
    down_share(blocks - 1)
    for index in range(2):
        columns = pl.ds(index * half, half)
        part = back_product(parts[1, :, columns], held[index])
        grad_normed[...] = part if index == 0 else grad_normed[...] + part
    grad[...] = grad_normed[...].astype(jnp.bfloat16)
    fetch(0).start()
    pair_whole(1).wait_recv()
    pair_whole(3).wait_recv()
    for quarter in range(4):
        rows = pl.ds(quarter * here, here)
        halving.store(
            1,
            quarter,
            project(lows[pl.ds(0, half), pl.ds(0, here)], heads[0, rows])
            + project(lows[pl.ds(half, half), pl.ds(0, here)], heads[1, rows]),
        )
    pair_whole(3).wait_send()
    pl.semaphore_signal(free_sem.at[0], inc=1, device_id=core, device_id_type=MESH)
    pair_whole(0).wait_recv()
    side(7).wait_recv()
    for quarter in range(4):
        halving.store(
            2,
            quarter,
            project(
                lows[pl.ds(0, half), pl.ds(here, here)], parts[1, :, pl.ds(quarter * 256, 256)]
            )
            + project(
                lows[pl.ds(half, half), pl.ds(here, here)],
                parts[0, :, pl.ds(width + quarter * 256, 256)],
            ),
        )
    for index in range(3):
        pair_whole(index).wait_send()
    side(7).wait_send()
    for index in range(3, 5):
        load(index).start()
    pl.semaphore_wait(free_sem.at[0], 1)
    load(0).wait()
    load(1).wait()

    def one_pair(pair, carry):
        @pl.when(pair + 1 < pairs)
        def _():
            fetch(pair + 1).start()

        fetch(pair).wait()
        columns = pl.ds(pl.multiple_of(pair * 128, 128), 128)
        others = pl.ds(pl.multiple_of(width + pair * 128, 128), 128)
        out, grad_keys, grad_values = attention_backward_pair(
            query[:, columns],
            columns_two.at[pl.ds(0, width), columns],
            columns_two.at[pl.ds(width, width), columns],
            held.at[lax.rem(pair, 2)],
            inverses[pair],
            grad[:, columns],
            mixed[:, columns],
            lows,
        )
        grad_query[:, columns] = out
        for part in range(4):
            first = part % 2 * here
            parts[part, :, columns] = grad_keys[part // 2][first : first + here]
            parts[part, :, others] = grad_values[part // 2][first : first + here]
        for step in range(2):
            for index, place in enumerate((columns, others)):
                remote(
                    parts.at[2 * step + 1, :, place],
                    heads.at[0, pl.ds((2 * step + index) * here, here), columns],
                    swap_send,
                    swap_recv,
                    core,
                ).start()
        return carry

    lax.fori_loop(0, 3, one_pair, 0)
    halving.finish(0, 0)
    lax.fori_loop(3, pairs, one_pair, 0)
    side(2).start()
    load(7).start()
    load_part(0).start()
    load_part(1).start()
    swapped = remote(heads.at[0], heads.at[0], swap_send, swap_recv, core)
    swapped.wait()
    pl.semaphore_signal(free_sem.at[1], inc=1, device_id=core, device_id_type=MESH)
    for step in (1, 0):

        def add_rows(index, carry):
            rows = pl.ds(pl.multiple_of(index * 64, 64), 64)
            for index in range(2):
                columns = pl.ds(index * width, width)
                first = pl.multiple_of((2 * step + index) * here + rows.start, 64)
                parts[2 * step, rows, columns] = (
                    parts[2 * step, rows, columns].astype(jnp.float32)
                    + heads[0, pl.ds(first, 64)].astype(jnp.float32)
                ).astype(jnp.bfloat16)
            return carry

        lax.fori_loop(0, here // 64, add_rows, 0)
    load(2).start()
    for index in range(3, 5):
        load(index).wait()

    def from_parts(part, rows):
        return back_product(parts[part, :, pl.ds(0, width)], heads[1, rows]) + back_product(
            parts[part, :, pl.ds(width, width)], heads[2, rows]
        )

    def far_rows(index, carry):
        rows = pl.ds(pl.multiple_of(index * 256, 256), 256)
        normed_send[:, rows] = from_parts(2, rows).astype(jnp.bfloat16)
        return carry

    lax.fori_loop(0, width // 256, far_rows, 0)
    side(3).start()
    pl.semaphore_wait(free_sem.at[1], 1)
    side(0).start()
    side(1).start()
    halving.finish(1, 0)
    halving.finish(2, 0)
    halving.finish(0, 1)

    load(2).wait()

    def own_rows(index, carry):
        rows = pl.ds(pl.multiple_of(index * 256, 256), 256)
        grad_normed[:, rows] = from_parts(0, rows) + back_product(grad_query[...], heads[0, rows])
        return carry

    lax.fori_loop(0, width // 256, own_rows, 0)
    load_part(0).wait()
    load_part(1).wait()

    def select_rows(index, carry):
        first = pl.multiple_of(index * 128, 128)
        row = first + lax.broadcasted_iota(jnp.int32, (128, width), 0)
        lane = lax.broadcasted_iota(jnp.int32, (128, width), 1)
        source = lax.div(row, 16) * 32 + core_index * 16 + lax.rem(row, 16)
        pick = jnp.where(lane == source, 1.0, 0.0).astype(jnp.bfloat16)
        value = back_product(pick[:, :half], held[0]) + back_product(pick[:, half:], held[1])
        value = value.astype(jnp.bfloat16)
        lows[pl.ds(first, 128)] = value[:, :half]
        lows[pl.ds(pl.multiple_of(half + first, 128), 128)] = value[:, half:]
        return carry

    lax.fori_loop(0, half // 128, select_rows, 0)
    load(8).start()
    load(9).start()

    def rows_one(part):
        return lows[pl.ds(part // 2 * half, half), pl.ds(part % 2 * here, here)]

    side(2).wait_recv()
    for quarter in range(4):
        columns = pl.ds(quarter * 256, 256)
        halving.store(
            3,
            quarter,
            project(rows_one(0), grad_query[:, columns])
            + project(rows_one(1), query_landing[:, columns]),
        )
    side(0).wait_recv()
    side(1).wait_recv()
    for quarter in range(4):
        columns = pl.ds(quarter * 512, 512)
        halving.store(
            4,
            quarter,
            project(rows_one(0), parts[0, :, columns])
            + project(rows_one(1), parts[1, :, columns])
            + project(rows_one(2), parts[2, :, columns])
            + project(rows_one(3), parts[3, :, columns]),
        )
    halving.finish(0, 2)
    halving.finish(1, 1)
    halving.finish(2, 1)
    load(5).wait()
    side(3).wait_recv()

    def norm_rows(index, sums):
        rows = pl.ds(pl.multiple_of(index * 32, 32), 32)
        grads = grad_normed[rows] + normed_landing[rows].astype(jnp.float32)
        center = units[rows] - mean_rows(units[rows])
        scale = lax.rsqrt(mean_rows(center * center) + EPS)
        value, gain_part, bias_part = norm_back(center * scale, grads, flat(gain_one), scale)
        grad_hidden[rows] = (residuals[rows] + value).astype(jnp.bfloat16)
        return sums[0] + gain_part, sums[1] + bias_part

    gain_sum, bias_sum = lax.fori_loop(0, here // 32, norm_rows, (nothing, nothing))
    side(4).start()
    vectors[pl.ds(0, 1)] = gain_sum
    vectors[pl.ds(1, 1)] = bias_sum
    vector_start(0)
    load(7).wait()

    def stored_rows(index, carry):
        rows = pl.ds(pl.multiple_of(index * 256, 256), 256)
        below = pl.ds(pl.multiple_of(width + index * 256, 256), 256)
        stored_send[:, rows] = back_product(grad_hidden[...], columns_two[below]).astype(
            jnp.bfloat16
        )
        return carry

    lax.fori_loop(0, width // 256, stored_rows, 0)
    side(5).start()
    halving.finish(3, 0)
    halving.finish(4, 0)
    vector_finish(0)
    load(8).wait()
    load(9).wait()
    side(4).wait_recv()
    for quarter in range(4):
        columns = pl.ds(quarter * 256, 256)
        halving.store(
            5,
            quarter,
            project(held[0, :, pl.ds(0, here)], grad_hidden[:, columns])
            + project(held[0, :, pl.ds(here, here)], hidden_landing[:, columns]),
        )

    def own_grads(index, carry):
        rows = pl.ds(pl.multiple_of(index * 256, 256), 256)
        grad_own[:, rows] = back_product(grad_hidden[...], columns_two[rows]).astype(jnp.bfloat16)
        return carry

    lax.fori_loop(0, width // 256, own_grads, 0)
    for job, stage in ((0, 3), (1, 2), (2, 2), (3, 1), (4, 1)):
        halving.finish(job, stage)
    vector_finish(1)
    halving.finish_direct(5, 0)
    for job, stage in ((3, 2), (4, 2), (0, 4), (1, 3), (2, 3)):
        halving.finish(job, stage)
    vector_finish(2)
    halving.finish_direct(5, 1)
    for job, stage in ((3, 3), (4, 3), (1, 4), (2, 4)):
        halving.finish(job, stage)
    vector_finish(3)
    halving.finish_direct(5, 2)
    for job in (3, 4):
        halving.finish(job, 4)
    side(5).wait_recv()
    grad_stored[...] = stored_landing[...]
    halving.drain()
    for index in range(7):
        side(index).wait_send()


def backward(inputs, large, small, collective_id):
    query = inputs[0]
    keys = large[0]
    here, width = query.shape
    span = keys.shape[0]
    shapes = [(width // 16, width), (width // 64, 4 * width), (width // 64, width)]
    shapes += [(width // 64, width), (width // 64, 2 * width), (width // 32, width)]
    inside = pl.BlockSpec(memory_space=pltpu.VMEM)
    outside = pl.BlockSpec(memory_space=pl.ANY)
    result_shapes = shapes[:4] + [shapes[3], shapes[3]] + shapes[5:]
    rows_shape = (here, width)
    low_rows = pltpu.VMEM(rows_shape, jnp.bfloat16)
    full_rows = pltpu.VMEM(rows_shape, jnp.float32)
    dma = pltpu.SemaphoreType.DMA
    operands = [query, *large[:3], *inputs[1:], *large[3:], *small]
    specs = [inside] + [outside] * 3 + [inside] * 3 + [outside] * (len(large) - 3)
    specs += [inside] * len(small)
    return pl.pallas_call(
        functools.partial(backward_kernel, shapes),
        in_specs=specs,
        out_specs=[inside] * (4 + len(result_shapes)),
        out_shape=[jax.ShapeDtypeStruct(rows_shape, jnp.bfloat16)] * 3
        + [jax.ShapeDtypeStruct((8, width), jnp.float32)]
        + [jax.ShapeDtypeStruct(shape, jnp.float32) for shape in result_shapes],
        scratch_shapes=[
            pltpu.VMEM((span, 2 * here), jnp.bfloat16),
            pltpu.VMEM((2, span, 2 * here), jnp.bfloat16),
            dma((2,)),
            pltpu.VMEM((4, here, 2 * width), jnp.bfloat16),
            pltpu.SemaphoreType.REGULAR((2,)),
            dma,
            dma,
            low_rows,
            low_rows,
            dma((8,)),
            dma((8,)),
            pltpu.VMEM((2 * width, width), jnp.bfloat16),
            pltpu.VMEM((3, width, width), jnp.bfloat16),
            dma((12,)),
            full_rows,
            full_rows,
            full_rows,
            low_rows,
            low_rows,
            low_rows,
            low_rows,
            low_rows,
            low_rows,
            pltpu.VMEM((8, 8, width), jnp.float32),
            dma((8,)),
            dma((8,)),
            pltpu.VMEM((width, here), jnp.bfloat16),
            pltpu.VMEM((here, 1), jnp.float32),
            dma((2, 2)),
            dma((4,)),
            dma((4,)),
            dma((8,)),
            dma((2,)),
        ]
        + Halving.scratch(shapes),
        compiler_params=pltpu.CompilerParams(
            collective_id=collective_id,
            has_side_effects=True,
            vmem_limit_bytes=62 * 2**20,
        ),
    )(*operands)


def mean_rows(value):
    return jnp.mean(value, axis=-1, keepdims=True)


def copy_kernel(count, vectors, *refs):
    sources, targets, pieces, stops = (
        refs[:count], refs[count : 2 * count], refs[2 * count : 2 * count + 4], refs[2 * count + 4 : -1]
    )
    ways = []
    for index, (source, target, stop) in enumerate(zip(sources, targets, stops)):
        ways.append(
            (
                pltpu.make_async_copy(source, stop, refs[-1].at[0, index]),
                pltpu.make_async_copy(stop, target, refs[-1].at[1, index]),
            )
        )
    for into, _ in ways:
        into.start()
    width = vectors.shape[1]
    size = width // 64
    shard = lax.axis_index("dp") * 4 + lax.axis_index("seq")
    turned = pltpu.roll(vectors[...], lax.rem(width - shard * size, width), 1)
    for index, piece in enumerate(pieces):
        piece[...] = turned[index : index + 1, :size]
    for into, out in ways:
        into.wait()
        out.start()
    for _, out in ways:
        out.wait()


def copied(vectors, arrays):
    outside = pl.BlockSpec(memory_space=pl.ANY)
    inside = pl.BlockSpec(memory_space=pltpu.VMEM)
    piece = jax.ShapeDtypeStruct((1, vectors.shape[1] // 64), jnp.float32)
    return pl.pallas_call(
        functools.partial(copy_kernel, len(arrays)),
        in_specs=[inside] + [outside] * len(arrays),
        out_specs=[outside] * len(arrays) + [inside] * 4,
        out_shape=[jax.ShapeDtypeStruct(array.shape, array.dtype) for array in arrays]
        + [piece] * 4,
        scratch_shapes=[pltpu.VMEM(array.shape, array.dtype) for array in arrays]
        + [pltpu.SemaphoreType.DMA((2, len(arrays)))],
    )(vectors, *arrays)


def on_device(
    states,
    mirror,
    w_skip,
    norm1_gain,
    norm1_bias,
    w_query,
    w_key,
    w_value,
    w_out,
    norm2_gain,
    norm2_bias,
    w_up,
    w_down,
    out_grad,
    lengths,
    infill_spans,
):
    rows_here = states.shape[2]
    model_width = states.shape[3]
    seq = lax.axis_index("seq")
    (
        hidden,
        query,
        inverses,
        mixed_rows,
        grad_low,
        joined_mine,
        shares,
        keys_all,
        values_all,
        normed_all,
        joined_other,
    ) = forward(
        lengths,
        infill_spans,
        states.reshape(rows_here, model_width),
        mirror.reshape(rows_here, model_width),
        out_grad.reshape(rows_here, model_width),
        [norm1_gain, norm1_bias],
        (w_skip, w_query, w_key, w_value),
        2,
    )
    results = backward(
        [query, inverses, mixed_rows, grad_low],
        [
            keys_all,
            values_all,
            shares,
            hidden,
            w_out,
            w_up,
            w_down,
            w_query,
            w_key,
            w_value,
            w_skip,
            normed_all,
            joined_mine,
            joined_other,
        ],
        [norm1_gain, norm2_gain, norm2_bias],
        1,
    )
    (
        output,
        grad_own,
        grad_stored,
        down_sum,
        up_sum,
        out_sum,
        query_sum,
        key_sum,
        value_sum,
        skip_sum,
        gain_one_sum,
        bias_one_sum,
        gain_two_sum,
        bias_two_sum,
    ) = copied(results[3], results[:3] + results[4:])
    return (
        output.reshape(states.shape),
        grad_own.reshape(states.shape),
        grad_stored.reshape(states.shape),
        skip_sum[None],
        gain_one_sum,
        bias_one_sum,
        query_sum[None],
        key_sum[None],
        value_sum[None],
        out_sum[None],
        gain_two_sum,
        bias_two_sum,
        up_sum[None],
        down_sum[None],
    )


def solution(mesh):
    in_specs = (
        P("section", "dp", "seq", None),
        P("section", "dp", "seq", None),
        P(),
        P(),
        P(),
        P(),
        P(),
        P(),
        P(),
        P(),
        P(),
        P(),
        P(),
        P("section", "dp", "seq", None),
        P("section", "dp", None),
        P("section", "dp", None, None),
    )
    out_specs = (
        P("section", "dp", "seq", None),
        P("section", "dp", "seq", None),
        P("section", "dp", "seq", None),
        P("section", ("dp", "seq"), None),
        P("section", ("dp", "seq")),
        P("section", ("dp", "seq")),
        P("section", ("dp", "seq"), None),
        P("section", ("dp", "seq"), None),
        P("section", ("dp", "seq"), None),
        P("section", ("dp", "seq"), None),
        P("section", ("dp", "seq")),
        P("section", ("dp", "seq")),
        P("section", ("dp", "seq"), None),
        P("section", ("dp", "seq"), None),
    )
    return jax.shard_map(
        on_device, mesh=mesh, in_specs=in_specs, out_specs=out_specs, check_vma=False
    )
```

```python
import functools

import jax
import jax.numpy as jnp
from jax.experimental import pallas as pl
from jax.experimental.pallas import tpu as pltpu
from jax import lax
from jax.sharding import PartitionSpec as P

LOG2E = 1.4426950408889634
LN2 = 0.6931471805599453


EPS = 1e-05


def project(left, right):
    return jnp.dot(left, right, preferred_element_type=jnp.float32)


def rows_product(left, right):
    return lax.dot_general(
        left, right, (((0,), (0,)), ((), ())), preferred_element_type=jnp.float32
    )


def back_product(left, right):
    return lax.dot_general(
        left, right, (((1,), (1,)), ((), ())), preferred_element_type=jnp.float32
    )


MESH = pl.DeviceIdType.MESH
NEAR, WRAP = (0, 3, 1, 2), (0, 1, 3, 2)
QUARTERS = (("x", NEAR), ("x", WRAP), ("z", NEAR), ("z", WRAP))


def flip(value, mask):
    if mask == 1:
        return value + 1 - 2 * lax.rem(value, 2)
    if mask == 2:
        return lax.rem(value + 2, 4)
    if mask == 3:
        return 3 - value
    return value


def block_place(quarter, outer, inner, x, z):
    first, order = QUARTERS[quarter]
    if first == "x":
        return flip(z, order[inner]) * 4 + flip(x, order[outer])
    return flip(z, order[outer]) * 4 + flip(x, order[inner])


def stage_partner(quarter, stage, x, z, seq):
    if stage == 4:
        return {"seq": lax.rem(seq + 2, 4)}
    first, order = QUARTERS[quarter]
    mask = order[2] if stage % 2 == 0 else order[1]
    if (first == "x") == (stage < 2):
        return {"dp": z * 4 + flip(x, mask)}
    return {"dp": flip(z, mask) * 4 + x}


def remote(source, target, send, recv, device):
    return pltpu.make_async_remote_copy(
        src_ref=source,
        dst_ref=target,
        send_sem=send,
        recv_sem=recv,
        device_id=device,
        device_id_type=MESH,
    )


def greet(devices):
    for device in devices:
        pl.semaphore_signal(
            pltpu.get_barrier_semaphore(), inc=1, device_id=device, device_id_type=MESH
        )


def enter(devices):
    pl.semaphore_wait(pltpu.get_barrier_semaphore(), len(devices))


def add_blocks(count, total, other):
    def one(index, carry):
        total[index] = (
            total[index].astype(jnp.float32) + other[index].astype(jnp.float32)
        ).astype(jnp.bfloat16)
        return carry

    lax.fori_loop(0, count, one, 0)


def place_here():
    dp, seq = lax.axis_index("dp"), lax.axis_index("seq")
    return lax.div(dp, 4), lax.rem(dp, 4), seq


def either(one, two):
    return 2 * lax.rem(lax.div(one, 2) + lax.div(two, 2), 2) + lax.rem(one + two, 2)


def relative_place(quarter, z, x, there):
    first, order = QUARTERS[quarter]

    def position(value):
        if order == NEAR:
            return 2 * value - lax.div(value, 2) - 4 * lax.div(value, 3)
        return value + lax.div(value, 2) * (1 - 2 * lax.rem(value, 2))

    z_place = position(either(z, lax.div(there, 4)))
    x_place = position(either(x, lax.rem(there, 4)))
    return x_place * 4 + z_place if first == "x" else z_place * 4 + x_place


class Halving:
    def __init__(self, shapes, results, scratch):
        self.shapes, self.results = shapes, results
        scratch = list(scratch)
        count = len(shapes)
        self.work = scratch[:count]
        self.landings = [scratch[count + 5 * job : count + 5 * job + 5] for job in range(count)]
        self.landings[-1] = self.landings[-1][:3]
        self.send_sem, self.recv_sem = scratch[-2:]
        self.z, self.x, self.seq = place_here()
        self.y = lax.div(self.seq, 2)

    @staticmethod
    def scratch(shapes):
        shapes_of = [(4, 16, 2 * rows, width // 4) for rows, width in shapes]
        for job, (rows, width) in enumerate(shapes):
            direct = job == len(shapes) - 1
            shapes_of += [(4, blocks, 2 * rows, width // 4) for blocks in (8, 4)]
            if direct:
                shapes_of.append((4, 7, rows, width // 4))
            else:
                shapes_of += [(4, blocks, 2 * rows, width // 4) for blocks in (2, 1)]
                shapes_of.append((4, rows, width // 4))
        sems = pltpu.SemaphoreType.DMA((len(shapes), 4, 5))
        return [pltpu.VMEM(shape, jnp.bfloat16) for shape in shapes_of] + [sems, sems]

    def put(self, job, quarter, there, value):
        place = relative_place(quarter, self.z, self.x, there)
        self.work[job][quarter, place] = value.astype(jnp.bfloat16)
        return place

    def put_and_send(self, job, quarter, there, value):
        place = self.put(job, quarter, there, value)

        @pl.when(place >= 8)
        def _():
            remote(
                self.work[job].at[quarter, place],
                self.landings[job][0].at[quarter, place - 8],
                self.send_sem.at[job, quarter, 0],
                self.recv_sem.at[job, quarter, 0],
                stage_partner(quarter, 0, self.x, self.z, self.seq),
            ).start()

    def store(self, job, quarter, value):
        rows = 2 * self.shapes[job][0]
        for index in range(16):
            self.put(job, quarter, index, value[index * rows : (index + 1) * rows])
        self.copy(job, quarter, 0).start()

    def copy(self, job, quarter, stage):
        rows = self.shapes[job][0]
        if stage < 4:
            size = 8 >> stage
            source = self.work[job].at[quarter, pl.ds(size, size)]
        else:
            away = pl.multiple_of((1 - self.y) * rows, 16)
            source = self.work[job].at[quarter, 0, pl.ds(away, rows)]
        return remote(
            source,
            self.landings[job][stage].at[quarter],
            self.send_sem.at[job, quarter, stage],
            self.recv_sem.at[job, quarter, stage],
            stage_partner(quarter, stage, self.x, self.z, self.seq),
        )

    def finish(self, job, stage):
        rows, width = self.shapes[job]
        for quarter in range(4):
            work = self.work[job].at[quarter]
            landing = self.landings[job][stage].at[quarter]
            self.copy(job, quarter, stage).wait_recv()
            if stage < 4:
                add_blocks(8 >> stage, work, landing)
                self.copy(job, quarter, stage + 1).start()
            else:
                mine = pl.multiple_of(self.y * rows, 16)
                total = work[0, pl.ds(mine, rows)].astype(jnp.float32)
                first = quarter * width // 4
                result = self.results[job][first // 4096 if width == 4096 else first // 1024]
                result[:, pl.ds(first % result.shape[1], width // 4)] = total + landing[
                    ...
                ].astype(jnp.float32)

    def direct(self, job, quarter, step):
        rows = self.shapes[job][0]
        first, order = QUARTERS[quarter]
        inner, away = step // 2, step % 2
        if first == "x":
            dp = flip(self.z, order[inner]) * 4 + self.x
        else:
            dp = self.z * 4 + flip(self.x, order[inner])
        part = pl.multiple_of((1 - self.y if away else self.y) * rows, 16)
        return remote(
            self.work[job].at[quarter, inner, pl.ds(part, rows)],
            self.landings[job][2].at[quarter, step - 1],
            self.send_sem.at[job, quarter, 2],
            self.recv_sem.at[job, quarter, 2],
            {"dp": dp, "seq": flip(self.seq, 2) if away else self.seq},
        )

    def finish_direct(self, job, stage):
        rows, width = self.shapes[job]
        for quarter in range(4):
            work = self.work[job].at[quarter]
            landing = self.landings[job][stage].at[quarter]
            if stage < 2:
                self.copy(job, quarter, stage).wait_recv()
                add_blocks(8 >> stage, work, landing)
                if stage == 0:
                    self.copy(job, quarter, 1).start()
                else:
                    for step in range(1, 8):
                        self.direct(job, quarter, step).start()
            else:
                remote(
                    landing, landing, self.send_sem.at[job, quarter, 2],
                    self.recv_sem.at[job, quarter, 2], {"seq": flip(self.seq, 2)},
                ).wait()
                mine = pl.multiple_of(self.y * rows, 16)
                total = work[0, pl.ds(mine, rows)].astype(jnp.float32)
                for step in range(7):
                    total = total + landing[step].astype(jnp.float32)
                self.results[job][0][:, pl.ds(quarter * width // 4, width // 4)] = total

    def drain(self):
        last = len(self.shapes) - 1
        for job in range(last + 1):
            for quarter in range(4):
                for stage in range(2 if job == last else 5):
                    self.copy(job, quarter, stage).wait_send()


def attention_backward_pair(query, keys, values, share, inverse, grad, mixed, lows):
    span = keys.shape[0]
    here = query.shape[0]
    chunk = span // 2
    lane = lax.broadcasted_iota(jnp.int32, query.shape, 1)
    zero = jnp.zeros(query.shape, query.dtype)
    queries = jnp.concatenate(
        [jnp.where(lane < 64, query, zero), jnp.where(lane >= 64, query, zero)], axis=0
    )
    turned = grad.astype(jnp.float32).T
    product = turned * mixed.astype(jnp.float32).T
    centre = jnp.concatenate(
        [
            jnp.sum(product[:64], axis=0, keepdims=True),
            jnp.sum(product[64:], axis=0, keepdims=True),
        ],
        axis=1,
    )
    none = jnp.zeros((64, here), jnp.float32)
    sets = []
    for part in range(2):
        factor = inverse[part : part + 1]
        first = turned[:64] * factor[:, :here]
        second = turned[64:] * factor[:, here:]
        grads = jnp.concatenate(
            [jnp.concatenate([first, none], axis=1), jnp.concatenate([none, second], axis=1)],
            axis=0,
        ).astype(jnp.bfloat16)
        sets.append((grads, grads.T, centre * factor))
    grad_keys, grad_values = [], []
    for index in range(span // chunk):
        rows = pl.ds(index * chunk, chunk)
        part = share[rows]
        grads, grads_back, centre = sets[index]
        grad_share = project(values[rows], grads)
        grad_score = (part.astype(jnp.float32) * (grad_share - centre)).astype(jnp.bfloat16)
        lows[rows] = grad_score
        grad_keys.append((project(grad_score, queries) * LN2).astype(jnp.bfloat16))
        grad_values.append(project(part, grads_back).astype(jnp.bfloat16))
    out = rows_product(keys[...], lows[...])
    out = jnp.concatenate([out[:64, :here], out[64:, here:]], axis=0)
    return (out.T * 0.125).astype(jnp.bfloat16), grad_keys, grad_values


def flat(vector):
    return vector[...].astype(jnp.float32).reshape(1, vector.shape[0])


def forward_kernel(
    lengths, spans, own, stored, out_grad, gain_one, bias_one, w_skip, w_query, w_key, w_value,
    hidden, query, inverses, mixed, grad_low, kept, shares, keys_out, values_out, normed_out, other,
    partner, normed, joined_sent, joined_landing, turned, w_rows, heads, keys, values,
    distance, scores, exponents, outs, tops, load_sem, send_sem, recv_sem, share_sem,
):
    seq = lax.axis_index("seq")
    core_index = lax.rem(seq, 2)
    core, far = {"seq": flip(seq, 1)}, {"seq": flip(seq, 2)}
    section = {"section": 1 - lax.axis_index("section")}
    here, width = own.shape
    span = keys.shape[0]
    half = width // 2
    pairs = width // 128
    parts = 2
    piece = here // parts

    loads = [
        pltpu.make_async_copy(source, target, load_sem.at[index])
        for index, (source, target) in enumerate(
            (
                (w_skip, w_rows),
                (w_query, heads.at[0]),
                (w_key, heads.at[1]),
                (w_value, heads.at[2]),
                (keys, keys_out),
                (values, values_out),
                (normed, normed_out),
                (joined_landing, other),
            )
        )
    ]

    def send(index, part):
        rows = pl.ds(part * piece, piece)
        source, target, device = (
            (stored.at[rows], partner.at[rows], section),
            (normed.at[rows], normed.at[pl.ds(here + part * piece, piece)], core),
            (normed.at[rows], normed.at[pl.ds(2 * here + part * piece, piece)], far),
            (
                normed.at[pl.ds(2 * here + part * piece, piece)],
                normed.at[pl.ds(3 * here + part * piece, piece)],
                core,
            ),
            (
                joined_sent.at[pl.ds(part % 2 * half, half)],
                joined_landing.at[pl.ds(part % 2 * half, half)],
                core,
            ),
        )[index]
        return remote(source, target, send_sem.at[index, part], recv_sem.at[index, part], device)

    greet([core, far, section])
    for index in range(4):
        loads[index].start()
    enter([core, far, section])
    for part in range(parts):
        send(0, part).start()

    bounds = []
    start = jnp.int32(0)
    for index in range(4):
        bounds.append((start, start + lengths[0, 0, index]))
        start = start + lengths[0, 0, index]

    def segment(places):
        return sum((places >= bounds[index][1]).astype(jnp.int32) for index in range(4))

    place = seq * here + lax.broadcasted_iota(jnp.int32, (here, 1), 0)
    inside = jnp.zeros((here, 1), jnp.int32)
    for index in range(4):
        low_end = bounds[index][0] + spans[2 * index]
        high_end = bounds[index][0] + spans[2 * index + 1]
        inside += (place >= low_end).astype(jnp.int32) * (place < high_end).astype(jnp.int32)
    grad_low[...] = jnp.where(
        inside > 0, out_grad[...].astype(jnp.float32), 0.0
    ).astype(jnp.bfloat16)
    query_place = seq * here + lax.broadcasted_iota(jnp.int32, (1, here), 1)
    query_segment = segment(query_place)
    for index in range(4):
        key_place = flip(seq, index) * here + lax.broadcasted_iota(jnp.int32, (here, 1), 0)
        gap = jnp.abs(query_place - key_place).astype(jnp.float32)
        distance[pl.ds(index * here, here)] = jnp.where(
            segment(key_place) == query_segment, gap, 1e30
        )

    def joined_rows(part, source):
        turned[...] = source[...].T

        def keep(row, value):
            kept[pl.ds(part * half + row, 32)] = value

        def pass_on(row, value):
            joined_sent[pl.ds(part * half + row, 32)] = value

        split_cores(core_index, turned, keep, pass_on, 32)
        send(4, part).start()

    joined_rows(0, own)
    loads[0].wait()
    hidden[...] = project(own[...], w_rows[pl.ds(0, width)])
    gain, bias = flat(gain_one), flat(bias_one)
    for part in range(parts):
        rows = pl.ds(part * piece, piece)
        send(0, part).wait_recv()
        value = hidden[rows] + project(partner[rows], w_rows[pl.ds(width, width)])
        hidden[rows] = value
        center = value - mean_rows(value)
        scale = lax.rsqrt(mean_rows(center * center) + EPS)
        normed[rows] = (center * scale * gain + bias).astype(jnp.bfloat16)
        send(2, part).start()
        send(1, part).start()
    for index in range(1, 4):
        loads[index].wait()
    scale = 0.125 * LOG2E
    query[...] = (project(normed[pl.ds(0, here)], heads[0]) * scale).astype(jnp.bfloat16)

    def both(first, count):
        rows = pl.ds(first, count)
        keys[rows] = project(normed[rows], heads[1]).astype(jnp.bfloat16)
        values[rows] = project(normed[rows], heads[2]).astype(jnp.bfloat16)

    def attend(part, pair):
        columns = pl.ds(pl.multiple_of(pair * 128, 128), 128)
        base = part * 2 * here
        value = query[:, columns]
        lane = lax.broadcasted_iota(jnp.int32, value.shape, 1)
        zero = jnp.zeros(value.shape, value.dtype)
        stacked = jnp.concatenate(
            [jnp.where(lane < 64, value, zero), jnp.where(lane >= 64, value, zero)], axis=0
        )
        head = 2 * pair + 1 + lax.div(lax.broadcasted_iota(jnp.int32, (1, 2 * here), 1), here)
        slope = LOG2E * jnp.exp2(head.astype(jnp.float32) * -0.5)
        rows = pl.ds(base, 2 * here)
        gap = distance[rows]
        score = back_product(keys[rows, columns], stacked)
        score = score - slope * jnp.concatenate([gap, gap], axis=1)
        scores[...] = score
        top = jnp.max(score.reshape(here // 4, 8, 2 * here), axis=0)
        top = jnp.max(top, axis=0, keepdims=True)
        exponents[pair, rows] = jnp.exp2(scores[...] - top).astype(jnp.bfloat16)
        pltpu.make_async_copy(
            exponents.at[pair, rows], shares.at[pair, rows], share_sem
        ).start()
        back = jnp.concatenate(
            [values[rows, columns].T, jnp.ones((16, 2 * here), jnp.bfloat16)], axis=0
        )
        return project(back, exponents[pair, rows]), top

    for part in range(parts):
        send(1, part).wait_recv()
    both(0, 2 * here)
    joined_rows(1, partner)

    def near(pair, carry):
        out, top = attend(0, pair)
        outs[pair] = out
        tops[pair] = top
        return carry

    lax.fori_loop(0, pairs - 3, near, 0)
    for part in range(parts - 1):
        send(2, part).wait_recv()
        send(3, part).start()
    lax.fori_loop(pairs - 3, pairs, near, 0)
    send(2, parts - 1).wait_recv()
    send(3, parts - 1).start()
    both(2 * here, here)
    for part in range(parts):
        send(3, part).wait_recv()
    both(3 * here, here)
    for index in range(4, 7):
        loads[index].start()

    def away(pair, carry):
        out, top = attend(1, pair)
        first, first_top = outs[pair], tops[pair]
        best = jnp.maximum(top, first_top)
        one, two = jnp.exp2(first_top - best), jnp.exp2(top - best)
        total = 1.0 / (one * first[128:129] + two * out[128:129])
        one, two = one * total, two * total
        inverses[pair, pl.ds(0, 1)] = one
        inverses[pair, pl.ds(1, 1)] = two
        out = first[:128] * one + out[:128] * two
        out = jnp.concatenate([out[:64, :here], out[64:, here:]], axis=0)
        columns = pl.ds(pl.multiple_of(pair * 128, 128), 128)
        mixed[:, columns] = out.T.astype(jnp.bfloat16)
        return carry

    lax.fori_loop(0, pairs, away, 0)
    for part in range(2):
        send(4, part).wait_recv()
    loads[7].start()
    pltpu.make_async_copy(exponents, shares, share_sem).wait()
    for index in range(4, 8):
        loads[index].wait()
    for index in range(5):
        for part in range(parts if index < 4 else 2):
            send(index, part).wait_send()


def forward(lengths, spans, own, stored, out_grad, norms, weights, collective_id):
    here, width = own.shape
    span = 4 * here
    pairs = width // 128
    inside = pl.BlockSpec(memory_space=pltpu.VMEM)
    outside = pl.BlockSpec(memory_space=pl.ANY)
    scalars = pl.BlockSpec(memory_space=pltpu.SMEM)
    low_shape = lambda *shape: jax.ShapeDtypeStruct(shape, jnp.bfloat16)
    low_rows = lambda *shape: pltpu.VMEM(shape, jnp.bfloat16)
    dma = pltpu.SemaphoreType.DMA
    return pl.pallas_call(
        forward_kernel,
        in_specs=[scalars, scalars, inside, outside, inside, inside, inside] + [outside] * 4,
        out_specs=[inside] * 6 + [outside] * 5,
        out_shape=[
            jax.ShapeDtypeStruct((here, width), jnp.float32),
            low_shape(here, width),
            jax.ShapeDtypeStruct((pairs, 2, 2 * here), jnp.float32),
            low_shape(here, width),
            low_shape(here, width),
            low_shape(width, here),
            low_shape(pairs, span, 2 * here),
            low_shape(span, width),
            low_shape(span, width),
            low_shape(span, width),
            low_shape(width, here),
        ],
        scratch_shapes=[
            low_rows(here, width),
            low_rows(span, width),
            low_rows(width, here),
            low_rows(width, here),
            low_rows(width, here),
            low_rows(2 * width, width),
            low_rows(3, width, width),
            low_rows(span, width),
            low_rows(span, width),
            pltpu.VMEM((span, here), jnp.float32),
            pltpu.VMEM((2 * here, 2 * here), jnp.float32),
            low_rows(pairs, span, 2 * here),
            pltpu.VMEM((pairs, 144, 2 * here), jnp.float32),
            pltpu.VMEM((pairs, 1, 2 * here), jnp.float32),
            dma((8,)),
            dma((5, 4)),
            dma((5, 4)),
            dma,
        ],
        compiler_params=pltpu.CompilerParams(
            collective_id=collective_id,
            has_side_effects=True,
            vmem_limit_bytes=56 * 2**20,
        ),
    )(lengths, spans, own, stored, out_grad, *norms, *weights)


def split_cores(core, source, kept, sent, rows):
    for index in range(source.shape[0] // (2 * rows)):
        mine = pl.multiple_of(index * 2 * rows + core * rows, rows)
        away = pl.multiple_of(index * 2 * rows + (1 - core) * rows, rows)
        kept(index * rows, source[pl.ds(mine, rows)])
        sent(index * rows, source[pl.ds(away, rows)])


def backward_kernel(
    shapes, query, keys, values, shares, inverses, mixed, grad_low, hidden, w_out, w_up, w_down,
    w_query, w_key, w_value, w_skip, normed_all, joined_kept, joined_other, gain_one, gain_two, bias_two,
    output, grad_own, grad_stored, vectors, *refs,
):
    refs = list(refs)
    take = lambda n: [refs.pop(0) for _ in range(n)]
    results = [take(1), take(1), take(1), take(1), take(2), take(1)]
    lows, held, held_sem, parts, free_sem, swap_send, swap_recv = take(7)
    grad_query, query_landing, side_send, side_recv = take(4)
    columns_two, heads, load_sem, units, residuals = take(5)
    grad_normed, normed_send, normed_landing, grad_hidden, hidden_landing = take(5)
    stored_send, stored_landing, vector_landing, vector_send, vector_recv = take(5)
    turned, inverse_two, block_sem, pair_send, pair_recv, act_recv, part_sem = take(7)
    grad = grad_hidden
    halving = Halving(shapes, results, refs)
    z, x, seq = place_here()
    core_index = lax.rem(seq, 2)
    core = {"seq": flip(seq, 1)}
    far = {"seq": flip(seq, 2)}
    section = {"section": 1 - lax.axis_index("section")}
    pairs = shares.shape[0]
    here, width = query.shape
    block = 512
    blocks = w_up.shape[1] // block
    half = width // 2

    def fetch(pair):
        slot = lax.rem(pair, 2)
        return pltpu.make_async_copy(shares.at[pair], held.at[slot], held_sem.at[slot])

    def load(index):
        source, target = (
            (keys, columns_two.at[pl.ds(0, width)]),
            (values, columns_two.at[pl.ds(width, width)]),
            (w_query, heads.at[0]),
            (w_key, heads.at[1]),
            (w_value, heads.at[2]),
            (hidden, units),
            (hidden, residuals),
            (w_skip, columns_two),
            (joined_kept, held.at[0, :, pl.ds(0, here)]),
            (joined_other, held.at[0, :, pl.ds(here, here)]),
            (w_out.at[:, pl.ds(0, half)], held.at[0]),
            (w_out.at[:, pl.ds(half, half)], held.at[1]),
        )[index]
        return pltpu.make_async_copy(source, target, load_sem.at[index])

    def load_part(index):
        return pltpu.make_async_copy(
            normed_all.at[:, pl.ds(index * half, half)], held.at[index], part_sem.at[index]
        )

    def load_block(step):
        slot = lax.rem(step, 2)
        place = pl.ds(pl.multiple_of(step * block, block), block)
        there = pl.ds(pl.multiple_of(slot * block, block), block)
        return (
            pltpu.make_async_copy(
                w_up.at[:, place], columns_two.at[pl.ds(width, width), there], block_sem.at[slot, 0]
            ),
            pltpu.make_async_copy(
                w_down.at[place], columns_two.at[there], block_sem.at[slot, 1]
            ),
        )

    def side(index):
        source, target, device = (
            (parts.at[0], parts.at[1], core),
            (parts.at[2], parts.at[3], core),
            (grad_query, query_landing, core),
            (normed_send, normed_landing, far),
            (grad_hidden, hidden_landing, core),
            (stored_send, stored_landing, section),
            (grad_low, parts.at[0, :, pl.ds(0, width)], core),
            (parts.at[1, :, pl.ds(0, width)], parts.at[0, :, pl.ds(width, width)], core),
        )[index]
        return remote(source, target, side_send.at[index], side_recv.at[index], device)

    def pair_half(index, part):
        lanes = pl.ds((1 - index) * here, here)
        return remote(
            parts.at[3, :, pl.ds((2 * index + part) * here, here)],
            lows.at[pl.ds(half + part * here, here), lanes],
            pair_send.at[index],
            pair_recv.at[index],
            core,
        )

    def pair_whole(index):
        if index == 2:
            source = target = parts.at[2]
        elif index == 3:
            source = target = heads.at[1]
        else:
            source = target = lows.at[pl.ds(half, half), pl.ds((1 - index) * here, here)]
        return remote(source, target, pair_send.at[index], pair_recv.at[index], core)

    def act_place(step, base):
        rows = pl.ds(pl.multiple_of(base + lax.rem(step, 2) * here, here), here)
        return rows, pl.ds(pl.multiple_of(lax.div(step, 2) * here, here), here)

    def act_copy(step):
        rows, lanes = act_place(step, half)
        return remote(
            parts.at[2, :, pl.ds(pl.multiple_of(step * here, here), here)],
            heads.at[2, rows, lanes],
            pair_send.at[2],
            act_recv.at[step],
            core,
        )

    def up_copy(step):
        rows = pl.ds(pl.multiple_of(lax.div(step, 2) * here, here), here)
        lanes = pl.ds(pl.multiple_of(lax.rem(step, 2) * block, block), block)
        return remote(
            heads.at[0, rows, lanes],
            heads.at[1, rows, lanes],
            pair_send.at[3],
            pair_recv.at[3],
            core,
        )

    vector_steps = [
        [core],
        [{"dp": z * 4 + flip(x, mask)} for mask in (1, 2, 3)],
        [{"dp": flip(z, mask) * 4 + x} for mask in (1, 2, 3)],
        [far],
    ]
    vector_slots = (0, 1, 4, 7)

    def vector_copies(step):
        return [
            remote(
                vectors,
                vector_landing.at[slot],
                vector_send.at[slot],
                vector_recv.at[slot],
                device,
            )
            for slot, device in enumerate(vector_steps[step], vector_slots[step])
        ]

    def vector_start(step):
        for copy in vector_copies(step):
            copy.start()

    def vector_finish(step):
        copies = vector_copies(step)
        for copy in copies:
            copy.wait()
        for index in range(len(copies)):
            vectors[...] += vector_landing[vector_slots[step] + index]
        if step < 3:
            vector_start(step + 1)

    devices = [core, far, section]
    for mask in (1, 2, 3):
        for dp in (z * 4 + flip(x, mask), flip(z, mask) * 4 + x):
            devices += [{"dp": dp}, {"dp": dp, "seq": flip(seq, 2)}]
    greet(devices)
    for index in (6, 10, 11):
        load(index).start()
    for copy in load_block(0):
        copy.start()

    def share_rows(index):
        def kept(row, value):
            lows[pl.ds(row, 16), pl.ds((1 - index) * here, here)] = value

        def sent(row, value):
            lanes = pl.ds((2 * index + row // here) * here, here)
            parts[3, pl.ds(row % here, 16), lanes] = value

        split_cores(core_index, turned, kept, sent, 16)

    turned[...] = mixed[...].T
    share_rows(0)
    load(6).wait()
    for index in range(2):
        load(10 + index).wait()
        columns = pl.ds(index * half, half)
        residuals[:, columns] += project(mixed[...], held[index])

    def norm_two_rows(index, carry):
        rows = pl.ds(pl.multiple_of(index * 32, 32), 32)
        value = residuals[rows]
        center = value - mean_rows(value)
        scale = lax.rsqrt(mean_rows(center * center) + EPS)
        center = center * scale
        units[rows] = center
        inverse_two[rows] = scale
        stored_send[rows] = (center * flat(gain_two) + flat(bias_two)).astype(jnp.bfloat16)
        grad_normed[rows] = jnp.zeros_like(value)
        return carry

    lax.fori_loop(0, here // 32, norm_two_rows, 0)
    turned[...] = stored_send[...].T
    share_rows(1)
    enter(devices)
    side(6).start()
    for index in range(2):
        pair_half(index, 0).start()
        pair_half(index, 1).start()

    def down_share(step):
        act_copy(step).wait_recv()
        rows, lanes = act_place(step, 0)
        rows_other, _ = act_place(step, half)
        value = project(heads[2, rows, lanes], grad_low[...]) + project(
            heads[2, rows_other, lanes], parts[0, :, pl.ds(0, width)]
        )
        for index in range(2):
            for quarter in range(4):
                halving.put_and_send(
                    0,
                    quarter,
                    2 * step + index,
                    value[index * 128 : index * 128 + 128, quarter * 256 : quarter * 256 + 256],
                )

    def one_block(step, carry):
        @pl.when(step + 1 < blocks)
        def _():
            for copy in load_block(step + 1):
                copy.start()

        for copy in load_block(step):
            copy.wait()
        there = pl.ds(pl.multiple_of(lax.rem(step, 2) * block, block), block)
        up_part = columns_two.at[pl.ds(width, width), there]
        down_part = columns_two.at[there]
        upward = project(stored_send[...], up_part[...])
        cdf = 0.5 * (1.0 + lax.erf(upward * 0.7071067811865476))
        act = (upward * cdf).astype(jnp.bfloat16)
        density = jnp.exp(upward * upward * -0.5) * 0.3989422804014327
        slope = cdf + upward * density
        grad_up = (back_product(grad_low[...], down_part[...]) * slope).astype(jnp.bfloat16)
        residuals[...] += project(act, down_part[...])
        grad_normed[...] += back_product(grad_up, up_part[...])
        up_rows = pl.ds(pl.multiple_of(lax.div(step, 2) * here, here), here)
        heads[0, up_rows, there] = grad_up
        up_copy(step).start()
        turned[pl.ds(0, block)] = act.T
        rows, lanes = act_place(step, 0)
        first = lax.rem(step, 2) * here
        sent_lanes = pl.ds(pl.multiple_of(step * here, here), here)

        def kept(row, value):
            heads[2, pl.ds(pl.multiple_of(first + row, 64), 64), lanes] = value

        def sent(row, value):
            parts[2, pl.ds(row, 64), sent_lanes] = value

        split_cores(core_index, turned.at[pl.ds(0, block)], kept, sent, 64)
        act_copy(step).start()

        @pl.when(step == 1)
        def _():
            side(6).wait_recv()

        @pl.when(step > 0)
        def _():
            down_share(step - 1)

        return carry

    lax.fori_loop(0, blocks, one_block, 0)
    load(0).start()
    load(1).start()

    def norm_back(ones, grads, gain, inverse):
        scaled = grads * gain
        value = scaled - mean_rows(scaled) - ones * mean_rows(scaled * ones)
        return (
            inverse * value,
            jnp.sum(grads * ones, axis=0, keepdims=True),
            jnp.sum(grads, axis=0, keepdims=True),
        )

    def norm_two_back(index, sums):
        rows = pl.ds(pl.multiple_of(index * 32, 32), 32)
        value, gain_part, bias_part = norm_back(
            units[rows], grad_normed[rows], flat(gain_two), inverse_two[rows]
        )
        output[rows] = residuals[rows].astype(jnp.bfloat16)
        value = grad_low[rows].astype(jnp.float32) + value
        residuals[rows] = value
        parts[1, rows, pl.ds(0, width)] = value.astype(jnp.bfloat16)
        return sums[0] + gain_part, sums[1] + bias_part

    nothing = jnp.zeros((1, width), jnp.float32)
    gain_sum, bias_sum = lax.fori_loop(0, here // 32, norm_two_back, (nothing, nothing))
    side(7).start()
    load(5).start()
    vectors[pl.ds(2, 1)] = gain_sum
    vectors[pl.ds(3, 1)] = bias_sum
    vectors[pl.ds(4, 4)] = jnp.zeros((4, width), jnp.float32)
    down_share(blocks - 1)
    for index in range(2):
        columns = pl.ds(index * half, half)
        part = back_product(parts[1, :, columns], held[index])
        grad_normed[...] = part if index == 0 else grad_normed[...] + part
    grad[...] = grad_normed[...].astype(jnp.bfloat16)
    fetch(0).start()
    pair_whole(1).wait_recv()
    pair_whole(3).wait_recv()
    for quarter in range(4):
        rows = pl.ds(quarter * here, here)
        halving.store(
            1,
            quarter,
            project(lows[pl.ds(0, half), pl.ds(0, here)], heads[0, rows])
            + project(lows[pl.ds(half, half), pl.ds(0, here)], heads[1, rows]),
        )
    pair_whole(3).wait_send()
    pl.semaphore_signal(free_sem.at[0], inc=1, device_id=core, device_id_type=MESH)
    pair_whole(0).wait_recv()
    side(7).wait_recv()
    for quarter in range(4):
        halving.store(
            2,
            quarter,
            project(
                lows[pl.ds(0, half), pl.ds(here, here)], parts[1, :, pl.ds(quarter * 256, 256)]
            )
            + project(
                lows[pl.ds(half, half), pl.ds(here, here)],
                parts[0, :, pl.ds(width + quarter * 256, 256)],
            ),
        )
    for index in range(3):
        pair_whole(index).wait_send()
    side(7).wait_send()
    for index in range(3, 5):
        load(index).start()
    pl.semaphore_wait(free_sem.at[0], 1)
    load(0).wait()
    load(1).wait()

    def one_pair(pair, carry):
        @pl.when(pair + 1 < pairs)
        def _():
            fetch(pair + 1).start()

        fetch(pair).wait()
        columns = pl.ds(pl.multiple_of(pair * 128, 128), 128)
        others = pl.ds(pl.multiple_of(width + pair * 128, 128), 128)
        out, grad_keys, grad_values = attention_backward_pair(
            query[:, columns],
            columns_two.at[pl.ds(0, width), columns],
            columns_two.at[pl.ds(width, width), columns],
            held.at[lax.rem(pair, 2)],
            inverses[pair],
            grad[:, columns],
            mixed[:, columns],
            lows,
        )
        grad_query[:, columns] = out
        for part in range(4):
            first = part % 2 * here
            parts[part, :, columns] = grad_keys[part // 2][first : first + here]
            parts[part, :, others] = grad_values[part // 2][first : first + here]
        for step in range(2):
            for index, place in enumerate((columns, others)):
                remote(
                    parts.at[2 * step + 1, :, place],
                    heads.at[0, pl.ds((2 * step + index) * here, here), columns],
                    swap_send,
                    swap_recv,
                    core,
                ).start()
        return carry

    lax.fori_loop(0, 3, one_pair, 0)
    halving.finish(0, 0)
    lax.fori_loop(3, pairs, one_pair, 0)
    side(2).start()
    load(7).start()
    load_part(0).start()
    load_part(1).start()
    swapped = remote(heads.at[0], heads.at[0], swap_send, swap_recv, core)
    swapped.wait()
    pl.semaphore_signal(free_sem.at[1], inc=1, device_id=core, device_id_type=MESH)
    for step in (1, 0):

        def add_rows(index, carry):
            rows = pl.ds(pl.multiple_of(index * 64, 64), 64)
            for index in range(2):
                columns = pl.ds(index * width, width)
                first = pl.multiple_of((2 * step + index) * here + rows.start, 64)
                parts[2 * step, rows, columns] = (
                    parts[2 * step, rows, columns].astype(jnp.float32)
                    + heads[0, pl.ds(first, 64)].astype(jnp.float32)
                ).astype(jnp.bfloat16)
            return carry

        lax.fori_loop(0, here // 64, add_rows, 0)
    load(2).start()
    for index in range(3, 5):
        load(index).wait()

    def from_parts(part, rows):
        return back_product(parts[part, :, pl.ds(0, width)], heads[1, rows]) + back_product(
            parts[part, :, pl.ds(width, width)], heads[2, rows]
        )

    def far_rows(index, carry):
        rows = pl.ds(pl.multiple_of(index * 256, 256), 256)
        normed_send[:, rows] = from_parts(2, rows).astype(jnp.bfloat16)
        return carry

    lax.fori_loop(0, width // 256, far_rows, 0)
    side(3).start()
    pl.semaphore_wait(free_sem.at[1], 1)
    side(0).start()
    side(1).start()
    halving.finish(1, 0)
    halving.finish(2, 0)
    halving.finish(0, 1)

    load(2).wait()

    def own_rows(index, carry):
        rows = pl.ds(pl.multiple_of(index * 256, 256), 256)
        grad_normed[:, rows] = from_parts(0, rows) + back_product(grad_query[...], heads[0, rows])
        return carry

    lax.fori_loop(0, width // 256, own_rows, 0)
    load_part(0).wait()
    load_part(1).wait()

    def select_rows(index, carry):
        first = pl.multiple_of(index * 256, 256)
        row = first + lax.broadcasted_iota(jnp.int32, (256, width), 0)
        lane = lax.broadcasted_iota(jnp.int32, (256, width), 1)
        source = lax.div(row, 16) * 32 + core_index * 16 + lax.rem(row, 16)
        pick = jnp.where(lane == source, 1.0, 0.0).astype(jnp.bfloat16)
        value = back_product(pick[:, :half], held[0]) + back_product(pick[:, half:], held[1])
        value = value.astype(jnp.bfloat16)
        lows[pl.ds(first, 256)] = value[:, :half]
        lows[pl.ds(pl.multiple_of(half + first, 256), 256)] = value[:, half:]
        return carry

    lax.fori_loop(0, half // 256, select_rows, 0)
    load(8).start()
    load(9).start()

    def rows_one(part):
        return lows[pl.ds(part // 2 * half, half), pl.ds(part % 2 * here, here)]

    side(2).wait_recv()
    for quarter in range(4):
        columns = pl.ds(quarter * 256, 256)
        halving.store(
            3,
            quarter,
            project(rows_one(0), grad_query[:, columns])
            + project(rows_one(1), query_landing[:, columns]),
        )
    side(0).wait_recv()
    side(1).wait_recv()
    for quarter in range(4):
        columns = pl.ds(quarter * 512, 512)
        halving.store(
            4,
            quarter,
            project(rows_one(0), parts[0, :, columns])
            + project(rows_one(1), parts[1, :, columns])
            + project(rows_one(2), parts[2, :, columns])
            + project(rows_one(3), parts[3, :, columns]),
        )
    halving.finish(0, 2)
    halving.finish(1, 1)
    halving.finish(2, 1)
    load(5).wait()
    side(3).wait_recv()

    def norm_rows(index, sums):
        rows = pl.ds(pl.multiple_of(index * 32, 32), 32)
        grads = grad_normed[rows] + normed_landing[rows].astype(jnp.float32)
        center = units[rows] - mean_rows(units[rows])
        scale = lax.rsqrt(mean_rows(center * center) + EPS)
        value, gain_part, bias_part = norm_back(center * scale, grads, flat(gain_one), scale)
        grad_hidden[rows] = (residuals[rows] + value).astype(jnp.bfloat16)
        return sums[0] + gain_part, sums[1] + bias_part

    gain_sum, bias_sum = lax.fori_loop(0, here // 32, norm_rows, (nothing, nothing))
    side(4).start()
    vectors[pl.ds(0, 1)] = gain_sum
    vectors[pl.ds(1, 1)] = bias_sum
    vector_start(0)
    load(7).wait()

    def stored_rows(index, carry):
        rows = pl.ds(pl.multiple_of(index * 256, 256), 256)
        below = pl.ds(pl.multiple_of(width + index * 256, 256), 256)
        stored_send[:, rows] = back_product(grad_hidden[...], columns_two[below]).astype(
            jnp.bfloat16
        )
        return carry

    lax.fori_loop(0, width // 256, stored_rows, 0)
    side(5).start()
    halving.finish(3, 0)
    halving.finish(4, 0)
    vector_finish(0)
    load(8).wait()
    load(9).wait()
    side(4).wait_recv()
    for quarter in range(4):
        columns = pl.ds(quarter * 256, 256)
        halving.store(
            5,
            quarter,
            project(held[0, :, pl.ds(0, here)], grad_hidden[:, columns])
            + project(held[0, :, pl.ds(here, here)], hidden_landing[:, columns]),
        )

    def own_grads(index, carry):
        rows = pl.ds(pl.multiple_of(index * 256, 256), 256)
        grad_own[:, rows] = back_product(grad_hidden[...], columns_two[rows]).astype(jnp.bfloat16)
        return carry

    lax.fori_loop(0, width // 256, own_grads, 0)
    for job, stage in ((0, 3), (1, 2), (2, 2), (3, 1), (4, 1)):
        halving.finish(job, stage)
    vector_finish(1)
    halving.finish_direct(5, 0)
    for job, stage in ((3, 2), (4, 2), (0, 4), (1, 3), (2, 3)):
        halving.finish(job, stage)
    vector_finish(2)
    halving.finish_direct(5, 1)
    for job, stage in ((3, 3), (4, 3), (1, 4), (2, 4)):
        halving.finish(job, stage)
    vector_finish(3)
    halving.finish_direct(5, 2)
    for job in (3, 4):
        halving.finish(job, 4)
    side(5).wait_recv()
    grad_stored[...] = stored_landing[...]
    halving.drain()
    for index in range(7):
        side(index).wait_send()


def backward(inputs, large, small, collective_id):
    query = inputs[0]
    keys = large[0]
    here, width = query.shape
    span = keys.shape[0]
    shapes = [(width // 16, width), (width // 64, 4 * width), (width // 64, width)]
    shapes += [(width // 64, width), (width // 64, 2 * width), (width // 32, width)]
    inside = pl.BlockSpec(memory_space=pltpu.VMEM)
    outside = pl.BlockSpec(memory_space=pl.ANY)
    result_shapes = shapes[:4] + [shapes[3], shapes[3]] + shapes[5:]
    rows_shape = (here, width)
    low_rows = pltpu.VMEM(rows_shape, jnp.bfloat16)
    full_rows = pltpu.VMEM(rows_shape, jnp.float32)
    dma = pltpu.SemaphoreType.DMA
    operands = [query, *large[:3], *inputs[1:], *large[3:], *small]
    specs = [inside] + [outside] * 3 + [inside] * 3 + [outside] * (len(large) - 3)
    specs += [inside] * len(small)
    return pl.pallas_call(
        functools.partial(backward_kernel, shapes),
        in_specs=specs,
        out_specs=[inside] * (4 + len(result_shapes)),
        out_shape=[jax.ShapeDtypeStruct(rows_shape, jnp.bfloat16)] * 3
        + [jax.ShapeDtypeStruct((8, width), jnp.float32)]
        + [jax.ShapeDtypeStruct(shape, jnp.float32) for shape in result_shapes],
        scratch_shapes=[
            pltpu.VMEM((span, 2 * here), jnp.bfloat16),
            pltpu.VMEM((2, span, 2 * here), jnp.bfloat16),
            dma((2,)),
            pltpu.VMEM((4, here, 2 * width), jnp.bfloat16),
            pltpu.SemaphoreType.REGULAR((2,)),
            dma,
            dma,
            low_rows,
            low_rows,
            dma((8,)),
            dma((8,)),
            pltpu.VMEM((2 * width, width), jnp.bfloat16),
            pltpu.VMEM((3, width, width), jnp.bfloat16),
            dma((12,)),
            full_rows,
            full_rows,
            full_rows,
            low_rows,
            low_rows,
            low_rows,
            low_rows,
            low_rows,
            low_rows,
            pltpu.VMEM((8, 8, width), jnp.float32),
            dma((8,)),
            dma((8,)),
            pltpu.VMEM((width, here), jnp.bfloat16),
            pltpu.VMEM((here, 1), jnp.float32),
            dma((2, 2)),
            dma((4,)),
            dma((4,)),
            dma((8,)),
            dma((2,)),
        ]
        + Halving.scratch(shapes),
        compiler_params=pltpu.CompilerParams(
            collective_id=collective_id,
            has_side_effects=True,
            vmem_limit_bytes=62 * 2**20,
        ),
    )(*operands)


def mean_rows(value):
    return jnp.mean(value, axis=-1, keepdims=True)


def copy_kernel(count, vectors, *refs):
    sources, targets = refs[:count], refs[count : 2 * count]
    pieces, stops = refs[2 * count : 2 * count + 4], refs[2 * count + 4 : -2]
    held, sems = refs[-2:]
    fetch = pltpu.make_async_copy(vectors, held, sems.at[0, count])
    fetch.start()
    ways = []
    for index, (source, target, stop) in enumerate(zip(sources, targets, stops)):
        ways.append(
            (
                pltpu.make_async_copy(source, stop, sems.at[0, index]),
                pltpu.make_async_copy(stop, target, sems.at[1, index]),
            )
        )
    for into, _ in ways:
        into.start()
    for into, out in ways:
        into.wait()
        out.start()
    fetch.wait()
    width = vectors.shape[1]
    size = width // 64
    shard = lax.axis_index("dp") * 4 + lax.axis_index("seq")
    turned = pltpu.roll(held[...], lax.rem(width - shard * size, width), 1)
    for index, piece in enumerate(pieces):
        piece[...] = turned[index : index + 1, :size]
    for _, out in ways:
        out.wait()


def copied(vectors, arrays):
    outside = pl.BlockSpec(memory_space=pl.ANY)
    inside = pl.BlockSpec(memory_space=pltpu.VMEM)
    piece = jax.ShapeDtypeStruct((1, vectors.shape[1] // 64), jnp.float32)
    return pl.pallas_call(
        functools.partial(copy_kernel, len(arrays)),
        in_specs=[outside] * (1 + len(arrays)),
        out_specs=[outside] * len(arrays) + [inside] * 4,
        out_shape=[jax.ShapeDtypeStruct(array.shape, array.dtype) for array in arrays]
        + [piece] * 4,
        scratch_shapes=[pltpu.VMEM(array.shape, array.dtype) for array in arrays]
        + [
            pltpu.VMEM(vectors.shape, vectors.dtype),
            pltpu.SemaphoreType.DMA((2, len(arrays) + 1)),
        ],
    )(vectors, *arrays)


def on_device(
    states,
    mirror,
    w_skip,
    norm1_gain,
    norm1_bias,
    w_query,
    w_key,
    w_value,
    w_out,
    norm2_gain,
    norm2_bias,
    w_up,
    w_down,
    out_grad,
    lengths,
    infill_spans,
):
    rows_here = states.shape[2]
    model_width = states.shape[3]
    seq = lax.axis_index("seq")
    (
        hidden,
        query,
        inverses,
        mixed_rows,
        grad_low,
        joined_mine,
        shares,
        keys_all,
        values_all,
        normed_all,
        joined_other,
    ) = forward(
        lengths,
        infill_spans.reshape(-1),
        states.reshape(rows_here, model_width),
        mirror.reshape(rows_here, model_width),
        out_grad.reshape(rows_here, model_width),
        [norm1_gain, norm1_bias],
        (w_skip, w_query, w_key, w_value),
        2,
    )
    results = backward(
        [query, inverses, mixed_rows, grad_low],
        [
            keys_all,
            values_all,
            shares,
            hidden,
            w_out,
            w_up,
            w_down,
            w_query,
            w_key,
            w_value,
            w_skip,
            normed_all,
            joined_mine,
            joined_other,
        ],
        [norm1_gain, norm2_gain, norm2_bias],
        1,
    )
    (
        output,
        grad_own,
        grad_stored,
        down_sum,
        up_sum,
        out_sum,
        query_sum,
        key_sum,
        value_sum,
        skip_sum,
        gain_one_sum,
        bias_one_sum,
        gain_two_sum,
        bias_two_sum,
    ) = copied(results[3], results[:3] + results[4:])
    return (
        output.reshape(states.shape),
        grad_own.reshape(states.shape),
        grad_stored.reshape(states.shape),
        skip_sum[None],
        gain_one_sum,
        bias_one_sum,
        query_sum[None],
        key_sum[None],
        value_sum[None],
        out_sum[None],
        gain_two_sum,
        bias_two_sum,
        up_sum[None],
        down_sum[None],
    )


def solution(mesh):
    in_specs = (
        P("section", "dp", "seq", None),
        P("section", "dp", "seq", None),
        P(),
        P(),
        P(),
        P(),
        P(),
        P(),
        P(),
        P(),
        P(),
        P(),
        P(),
        P("section", "dp", "seq", None),
        P("section", "dp", None),
        P("section", "dp", None, None),
    )
    out_specs = (
        P("section", "dp", "seq", None),
        P("section", "dp", "seq", None),
        P("section", "dp", "seq", None),
        P("section", ("dp", "seq"), None),
        P("section", ("dp", "seq")),
        P("section", ("dp", "seq")),
        P("section", ("dp", "seq"), None),
        P("section", ("dp", "seq"), None),
        P("section", ("dp", "seq"), None),
        P("section", ("dp", "seq"), None),
        P("section", ("dp", "seq")),
        P("section", ("dp", "seq")),
        P("section", ("dp", "seq"), None),
        P("section", ("dp", "seq"), None),
    )
    return jax.shard_map(
        on_device, mesh=mesh, in_specs=in_specs, out_specs=out_specs, check_vma=False
    )
```

```python
import functools

import jax
import jax.numpy as jnp
from jax.experimental import pallas as pl
from jax.experimental.pallas import tpu as pltpu
from jax import lax
from jax.sharding import PartitionSpec as P

LOG2E = 1.4426950408889634
LN2 = 0.6931471805599453


EPS = 1e-05


def project(left, right):
    return jnp.dot(left, right, preferred_element_type=jnp.float32)


def rows_product(left, right):
    return lax.dot_general(
        left, right, (((0,), (0,)), ((), ())), preferred_element_type=jnp.float32
    )


def back_product(left, right):
    return lax.dot_general(
        left, right, (((1,), (1,)), ((), ())), preferred_element_type=jnp.float32
    )


MESH = pl.DeviceIdType.MESH
NEAR, WRAP = (0, 3, 1, 2), (0, 1, 3, 2)
QUARTERS = (("x", NEAR), ("x", WRAP), ("z", NEAR), ("z", WRAP))


def flip(value, mask):
    if mask == 1:
        return value + 1 - 2 * lax.rem(value, 2)
    if mask == 2:
        return lax.rem(value + 2, 4)
    if mask == 3:
        return 3 - value
    return value


def block_place(quarter, outer, inner, x, z):
    first, order = QUARTERS[quarter]
    if first == "x":
        return flip(z, order[inner]) * 4 + flip(x, order[outer])
    return flip(z, order[outer]) * 4 + flip(x, order[inner])


def stage_partner(quarter, stage, x, z, seq):
    if stage == 4:
        return {"seq": lax.rem(seq + 2, 4)}
    first, order = QUARTERS[quarter]
    mask = order[2] if stage % 2 == 0 else order[1]
    if (first == "x") == (stage < 2):
        return {"dp": z * 4 + flip(x, mask)}
    return {"dp": flip(z, mask) * 4 + x}


def remote(source, target, send, recv, device):
    return pltpu.make_async_remote_copy(
        src_ref=source,
        dst_ref=target,
        send_sem=send,
        recv_sem=recv,
        device_id=device,
        device_id_type=MESH,
    )


def greet(devices):
    for device in devices:
        pl.semaphore_signal(
            pltpu.get_barrier_semaphore(), inc=1, device_id=device, device_id_type=MESH
        )


def enter(devices):
    pl.semaphore_wait(pltpu.get_barrier_semaphore(), len(devices))


def add_blocks(count, total, other):
    def one(index, carry):
        total[index] = (
            total[index].astype(jnp.float32) + other[index].astype(jnp.float32)
        ).astype(jnp.bfloat16)
        return carry

    lax.fori_loop(0, count, one, 0)


def place_here():
    dp, seq = lax.axis_index("dp"), lax.axis_index("seq")
    return lax.div(dp, 4), lax.rem(dp, 4), seq


def either(one, two):
    return 2 * lax.rem(lax.div(one, 2) + lax.div(two, 2), 2) + lax.rem(one + two, 2)


def relative_place(quarter, z, x, there):
    first, order = QUARTERS[quarter]

    def position(value):
        if order == NEAR:
            return 2 * value - lax.div(value, 2) - 4 * lax.div(value, 3)
        return value + lax.div(value, 2) * (1 - 2 * lax.rem(value, 2))

    z_place = position(either(z, lax.div(there, 4)))
    x_place = position(either(x, lax.rem(there, 4)))
    return x_place * 4 + z_place if first == "x" else z_place * 4 + x_place


class Halving:
    def __init__(self, shapes, results, scratch):
        self.shapes, self.results = shapes, results
        scratch = list(scratch)
        count = len(shapes)
        self.work = scratch[:count]
        first = [count + 5 * job for job in range(count - 1)] + [6 * count - 7]
        self.landings = [
            scratch[start : start + (5 if job < count - 2 else 3)] for job, start in enumerate(first)
        ]
        self.send_sem, self.recv_sem = scratch[-2:]
        self.z, self.x, self.seq = place_here()
        self.y = lax.div(self.seq, 2)

    @staticmethod
    def scratch(shapes):
        shapes_of = [(4, 16, 2 * rows, width // 4) for rows, width in shapes]
        for job, (rows, width) in enumerate(shapes):
            direct = job >= len(shapes) - 2
            shapes_of += [(4, blocks, 2 * rows, width // 4) for blocks in (8, 4)]
            if direct:
                shapes_of.append((4, 7, rows, width // 4))
            else:
                shapes_of += [(4, blocks, 2 * rows, width // 4) for blocks in (2, 1)]
                shapes_of.append((4, rows, width // 4))
        sems = pltpu.SemaphoreType.DMA((len(shapes), 4, 5))
        return [pltpu.VMEM(shape, jnp.bfloat16) for shape in shapes_of] + [sems, sems]

    def put(self, job, quarter, there, value):
        place = relative_place(quarter, self.z, self.x, there)
        self.work[job][quarter, place] = value.astype(jnp.bfloat16)
        return place

    def put_and_send(self, job, quarter, there, value):
        place = self.put(job, quarter, there, value)

        @pl.when(place >= 8)
        def _():
            remote(
                self.work[job].at[quarter, place],
                self.landings[job][0].at[quarter, place - 8],
                self.send_sem.at[job, quarter, 0],
                self.recv_sem.at[job, quarter, 0],
                stage_partner(quarter, 0, self.x, self.z, self.seq),
            ).start()

    def store(self, job, quarter, value):
        rows = 2 * self.shapes[job][0]
        for index in range(16):
            self.put(job, quarter, index, value[index * rows : (index + 1) * rows])
        self.copy(job, quarter, 0).start()

    def copy(self, job, quarter, stage):
        rows = self.shapes[job][0]
        if stage < 4:
            size = 8 >> stage
            source = self.work[job].at[quarter, pl.ds(size, size)]
        else:
            away = pl.multiple_of((1 - self.y) * rows, 16)
            source = self.work[job].at[quarter, 0, pl.ds(away, rows)]
        return remote(
            source,
            self.landings[job][stage].at[quarter],
            self.send_sem.at[job, quarter, stage],
            self.recv_sem.at[job, quarter, stage],
            stage_partner(quarter, stage, self.x, self.z, self.seq),
        )

    def finish(self, job, stage):
        rows, width = self.shapes[job]
        for quarter in range(4):
            work = self.work[job].at[quarter]
            landing = self.landings[job][stage].at[quarter]
            self.copy(job, quarter, stage).wait_recv()
            if stage < 4:
                add_blocks(8 >> stage, work, landing)
                self.copy(job, quarter, stage + 1).start()
            else:
                mine = pl.multiple_of(self.y * rows, 16)
                total = work[0, pl.ds(mine, rows)].astype(jnp.float32)
                first = quarter * width // 4
                result = self.results[job][first // 4096 if width == 4096 else first // 1024]
                result[:, pl.ds(first % result.shape[1], width // 4)] = total + landing[
                    ...
                ].astype(jnp.float32)

    def direct(self, job, quarter, step):
        rows = self.shapes[job][0]
        first, order = QUARTERS[quarter]
        inner, away = step // 2, step % 2
        if first == "x":
            dp = flip(self.z, order[inner]) * 4 + self.x
        else:
            dp = self.z * 4 + flip(self.x, order[inner])
        part = pl.multiple_of((1 - self.y if away else self.y) * rows, 16)
        return remote(
            self.work[job].at[quarter, inner, pl.ds(part, rows)],
            self.landings[job][2].at[quarter, step - 1],
            self.send_sem.at[job, quarter, 2],
            self.recv_sem.at[job, quarter, 2],
            {"dp": dp, "seq": flip(self.seq, 2) if away else self.seq},
        )

    def finish_direct(self, job, stage):
        rows, width = self.shapes[job]
        for quarter in range(4):
            work = self.work[job].at[quarter]
            landing = self.landings[job][stage].at[quarter]
            if stage < 2:
                self.copy(job, quarter, stage).wait_recv()
                add_blocks(8 >> stage, work, landing)
                if stage == 0:
                    self.copy(job, quarter, 1).start()
                else:
                    for step in range(1, 8):
                        self.direct(job, quarter, step).start()
            else:
                remote(
                    landing, landing, self.send_sem.at[job, quarter, 2],
                    self.recv_sem.at[job, quarter, 2], {"seq": flip(self.seq, 2)},
                ).wait()
                mine = pl.multiple_of(self.y * rows, 16)
                total = work[0, pl.ds(mine, rows)].astype(jnp.float32)
                for step in range(7):
                    total = total + landing[step].astype(jnp.float32)
                start = quarter * width // 4
                self.results[job][start // 1024][:, pl.ds(start % 1024, width // 4)] = total

    def drain(self):
        last = len(self.shapes) - 1
        for job in range(last + 1):
            for quarter in range(4):
                for stage in range(2 if job >= last - 1 else 5):
                    self.copy(job, quarter, stage).wait_send()


def attention_backward_pair(query, keys, values, share, inverse, grad, mixed, lows):
    span = keys.shape[0]
    here = query.shape[0]
    chunk = span // 2
    lane = lax.broadcasted_iota(jnp.int32, query.shape, 1)
    zero = jnp.zeros(query.shape, query.dtype)
    queries = jnp.concatenate(
        [jnp.where(lane < 64, query, zero), jnp.where(lane >= 64, query, zero)], axis=0
    )
    turned = grad.astype(jnp.float32).T
    product = turned * mixed.astype(jnp.float32).T
    centre = jnp.concatenate(
        [
            jnp.sum(product[:64], axis=0, keepdims=True),
            jnp.sum(product[64:], axis=0, keepdims=True),
        ],
        axis=1,
    )
    none = jnp.zeros((64, here), jnp.float32)
    sets = []
    for part in range(2):
        factor = inverse[part : part + 1]
        first = turned[:64] * factor[:, :here]
        second = turned[64:] * factor[:, here:]
        grads = jnp.concatenate(
            [jnp.concatenate([first, none], axis=1), jnp.concatenate([none, second], axis=1)],
            axis=0,
        ).astype(jnp.bfloat16)
        sets.append((grads, grads.T, centre * factor))
    grad_keys, grad_values = [], []
    for index in range(span // chunk):
        rows = pl.ds(index * chunk, chunk)
        part = share[rows]
        grads, grads_back, centre = sets[index]
        grad_share = project(values[rows], grads)
        grad_score = (part.astype(jnp.float32) * (grad_share - centre)).astype(jnp.bfloat16)
        lows[rows] = grad_score
        grad_keys.append((project(grad_score, queries) * LN2).astype(jnp.bfloat16))
        grad_values.append(project(part, grads_back).astype(jnp.bfloat16))
    out = rows_product(keys[...], lows[...])
    out = jnp.concatenate([out[:64, :here], out[64:, here:]], axis=0)
    return (out.T * 0.125).astype(jnp.bfloat16), grad_keys, grad_values


def flat(vector):
    return vector[...].astype(jnp.float32).reshape(1, vector.shape[0])


def forward_kernel(
    lengths, spans, own, stored, out_grad, gain_one, bias_one, w_skip, w_query, w_key, w_value,
    hidden, query, inverses, mixed, grad_low, kept, shares, keys_out, values_out, normed_out, other,
    partner, normed, joined_sent, joined_landing, turned, w_rows, heads, keys, values,
    distance, scores, exponents, outs, tops, load_sem, send_sem, recv_sem, share_sem,
):
    seq = lax.axis_index("seq")
    core_index = lax.rem(seq, 2)
    core, far = {"seq": flip(seq, 1)}, {"seq": flip(seq, 2)}
    section = {"section": 1 - lax.axis_index("section")}
    here, width = own.shape
    span = keys.shape[0]
    half = width // 2
    pairs = width // 128
    parts = 2
    piece = here // parts

    loads = [
        pltpu.make_async_copy(source, target, load_sem.at[index])
        for index, (source, target) in enumerate(
            (
                (w_skip, w_rows),
                (w_query, heads.at[0]),
                (w_key, heads.at[1]),
                (w_value, heads.at[2]),
                (keys, keys_out),
                (values, values_out),
                (normed, normed_out),
                (joined_landing, other),
            )
        )
    ]

    def send(index, part):
        rows = pl.ds(part * piece, piece)
        source, target, device = (
            (stored.at[rows], partner.at[rows], section),
            (normed.at[rows], normed.at[pl.ds(here + part * piece, piece)], core),
            (normed.at[rows], normed.at[pl.ds(2 * here + part * piece, piece)], far),
            (
                normed.at[pl.ds(2 * here + part * piece, piece)],
                normed.at[pl.ds(3 * here + part * piece, piece)],
                core,
            ),
            (
                joined_sent.at[pl.ds(part % 2 * half, half)],
                joined_landing.at[pl.ds(part % 2 * half, half)],
                core,
            ),
        )[index]
        return remote(source, target, send_sem.at[index, part], recv_sem.at[index, part], device)

    greet([core, far, section])
    for index in range(4):
        loads[index].start()
    enter([core, far, section])
    for part in range(parts):
        send(0, part).start()

    bounds = []
    start = jnp.int32(0)
    for index in range(4):
        bounds.append((start, start + lengths[0, 0, index]))
        start = start + lengths[0, 0, index]

    def segment(places):
        return sum((places >= bounds[index][1]).astype(jnp.int32) for index in range(4))

    place = seq * here + lax.broadcasted_iota(jnp.int32, (here, 1), 0)
    inside = jnp.zeros((here, 1), jnp.int32)
    for index in range(4):
        low_end = bounds[index][0] + spans[0, 0, 0, index]
        high_end = bounds[index][0] + spans[0, 0, 1, index]
        inside += (place >= low_end).astype(jnp.int32) * (place < high_end).astype(jnp.int32)
    grad_low[...] = jnp.where(
        inside > 0, out_grad[...].astype(jnp.float32), 0.0
    ).astype(jnp.bfloat16)
    query_place = seq * here + lax.broadcasted_iota(jnp.int32, (1, here), 1)
    query_segment = segment(query_place)
    for index in range(4):
        key_place = flip(seq, index) * here + lax.broadcasted_iota(jnp.int32, (here, 1), 0)
        gap = jnp.abs(query_place - key_place).astype(jnp.float32)
        distance[pl.ds(index * here, here)] = jnp.where(
            segment(key_place) == query_segment, gap, 1e30
        )

    def joined_rows(part, source):
        turned[...] = source[...].T

        def keep(row, value):
            kept[pl.ds(part * half + row, 32)] = value

        def pass_on(row, value):
            joined_sent[pl.ds(part * half + row, 32)] = value

        split_cores(core_index, turned, keep, pass_on, 32)
        send(4, part).start()

    joined_rows(0, own)
    loads[0].wait()
    hidden[...] = project(own[...], w_rows[pl.ds(0, width)])
    gain, bias = flat(gain_one), flat(bias_one)
    for part in range(parts):
        rows = pl.ds(part * piece, piece)
        send(0, part).wait_recv()
        value = hidden[rows] + project(partner[rows], w_rows[pl.ds(width, width)])
        hidden[rows] = value
        center = value - mean_rows(value)
        scale = lax.rsqrt(mean_rows(center * center) + EPS)
        normed[rows] = (center * scale * gain + bias).astype(jnp.bfloat16)
        send(2, part).start()
        send(1, part).start()
    for index in range(1, 4):
        loads[index].wait()
    scale = 0.125 * LOG2E
    query[...] = (project(normed[pl.ds(0, here)], heads[0]) * scale).astype(jnp.bfloat16)

    def both(first, count):
        rows = pl.ds(first, count)
        keys[rows] = project(normed[rows], heads[1]).astype(jnp.bfloat16)
        values[rows] = project(normed[rows], heads[2]).astype(jnp.bfloat16)

    def attend(part, pair):
        columns = pl.ds(pl.multiple_of(pair * 128, 128), 128)
        base = part * 2 * here
        value = query[:, columns]
        lane = lax.broadcasted_iota(jnp.int32, value.shape, 1)
        zero = jnp.zeros(value.shape, value.dtype)
        stacked = jnp.concatenate(
            [jnp.where(lane < 64, value, zero), jnp.where(lane >= 64, value, zero)], axis=0
        )
        head = 2 * pair + 1 + lax.div(lax.broadcasted_iota(jnp.int32, (1, 2 * here), 1), here)
        slope = LOG2E * jnp.exp2(head.astype(jnp.float32) * -0.5)
        rows = pl.ds(base, 2 * here)
        gap = distance[rows]
        score = back_product(keys[rows, columns], stacked)
        score = score - slope * jnp.concatenate([gap, gap], axis=1)
        scores[...] = score
        top = jnp.max(score.reshape(here // 4, 8, 2 * here), axis=0)
        top = jnp.max(top, axis=0, keepdims=True)
        exponents[pair, rows] = jnp.exp2(scores[...] - top).astype(jnp.bfloat16)
        pltpu.make_async_copy(
            exponents.at[pair, rows], shares.at[pair, rows], share_sem
        ).start()
        back = jnp.concatenate(
            [values[rows, columns].T, jnp.ones((16, 2 * here), jnp.bfloat16)], axis=0
        )
        return project(back, exponents[pair, rows]), top

    for part in range(parts):
        send(1, part).wait_recv()
    both(0, 2 * here)
    joined_rows(1, partner)

    def near(pair, carry):
        out, top = attend(0, pair)
        outs[pair] = out
        tops[pair] = top
        return carry

    lax.fori_loop(0, pairs - 3, near, 0)
    for part in range(parts - 1):
        send(2, part).wait_recv()
        send(3, part).start()
    lax.fori_loop(pairs - 3, pairs, near, 0)
    send(2, parts - 1).wait_recv()
    send(3, parts - 1).start()
    both(2 * here, here)
    for part in range(parts):
        send(3, part).wait_recv()
    both(3 * here, here)
    for index in range(4, 7):
        loads[index].start()

    def away(pair, carry):
        out, top = attend(1, pair)
        first, first_top = outs[pair], tops[pair]
        best = jnp.maximum(top, first_top)
        one, two = jnp.exp2(first_top - best), jnp.exp2(top - best)
        total = 1.0 / (one * first[128:129] + two * out[128:129])
        one, two = one * total, two * total
        inverses[pair, pl.ds(0, 1)] = one
        inverses[pair, pl.ds(1, 1)] = two
        out = first[:128] * one + out[:128] * two
        out = jnp.concatenate([out[:64, :here], out[64:, here:]], axis=0)
        columns = pl.ds(pl.multiple_of(pair * 128, 128), 128)
        mixed[:, columns] = out.T.astype(jnp.bfloat16)
        return carry

    lax.fori_loop(0, pairs, away, 0)
    for part in range(2):
        send(4, part).wait_recv()
    loads[7].start()
    pltpu.make_async_copy(exponents, shares, share_sem).wait()
    for index in range(4, 8):
        loads[index].wait()
    for index in range(5):
        for part in range(parts if index < 4 else 2):
            send(index, part).wait_send()


def forward(lengths, spans, own, stored, out_grad, norms, weights, collective_id):
    here, width = own.shape
    span = 4 * here
    pairs = width // 128
    inside = pl.BlockSpec(memory_space=pltpu.VMEM)
    outside = pl.BlockSpec(memory_space=pl.ANY)
    scalars = pl.BlockSpec(memory_space=pltpu.SMEM)
    low_shape = lambda *shape: jax.ShapeDtypeStruct(shape, jnp.bfloat16)
    low_rows = lambda *shape: pltpu.VMEM(shape, jnp.bfloat16)
    dma = pltpu.SemaphoreType.DMA
    return pl.pallas_call(
        forward_kernel,
        in_specs=[scalars, scalars, inside, outside, inside, inside, inside] + [outside] * 4,
        out_specs=[inside] * 6 + [outside] * 5,
        out_shape=[
            jax.ShapeDtypeStruct((here, width), jnp.float32),
            low_shape(here, width),
            jax.ShapeDtypeStruct((pairs, 2, 2 * here), jnp.float32),
            low_shape(here, width),
            low_shape(here, width),
            low_shape(width, here),
            low_shape(pairs, span, 2 * here),
            low_shape(span, width),
            low_shape(span, width),
            low_shape(span, width),
            low_shape(width, here),
        ],
        scratch_shapes=[
            low_rows(here, width),
            low_rows(span, width),
            low_rows(width, here),
            low_rows(width, here),
            low_rows(width, here),
            low_rows(2 * width, width),
            low_rows(3, width, width),
            low_rows(span, width),
            low_rows(span, width),
            pltpu.VMEM((span, here), jnp.float32),
            pltpu.VMEM((2 * here, 2 * here), jnp.float32),
            low_rows(pairs, span, 2 * here),
            pltpu.VMEM((pairs, 144, 2 * here), jnp.float32),
            pltpu.VMEM((pairs, 1, 2 * here), jnp.float32),
            dma((8,)),
            dma((5, 4)),
            dma((5, 4)),
            dma,
        ],
        compiler_params=pltpu.CompilerParams(
            collective_id=collective_id,
            has_side_effects=True,
            vmem_limit_bytes=56 * 2**20,
        ),
    )(lengths, spans, own, stored, out_grad, *norms, *weights)


def split_cores(core, source, kept, sent, rows):
    for index in range(source.shape[0] // (2 * rows)):
        mine = pl.multiple_of(index * 2 * rows + core * rows, rows)
        away = pl.multiple_of(index * 2 * rows + (1 - core) * rows, rows)
        kept(index * rows, source[pl.ds(mine, rows)])
        sent(index * rows, source[pl.ds(away, rows)])


def backward_kernel(
    shapes, query, keys, values, shares, inverses, mixed, grad_low, hidden, w_out, w_up, w_down,
    w_query, w_key, w_value, w_skip, normed_all, joined_kept, joined_other, gain_one, gain_two, bias_two,
    output, grad_own, grad_stored, vectors, *refs,
):
    refs = list(refs)
    take = lambda n: [refs.pop(0) for _ in range(n)]
    results = [take(1), take(1), take(1), take(1), take(2), take(1)]
    lows, held, held_sem, parts, free_sem, swap_send, swap_recv = take(7)
    grad_query, query_landing, side_send, side_recv = take(4)
    columns_two, heads, load_sem, units, residuals = take(5)
    grad_normed, normed_send, normed_landing, grad_hidden, hidden_landing = take(5)
    stored_send, stored_landing, vector_landing, vector_send, vector_recv = take(5)
    turned, inverse_two, block_sem, pair_send, pair_recv, act_recv, part_sem = take(7)
    grad = grad_hidden
    halving = Halving(shapes, results, refs)
    z, x, seq = place_here()
    core_index = lax.rem(seq, 2)
    core = {"seq": flip(seq, 1)}
    far = {"seq": flip(seq, 2)}
    section = {"section": 1 - lax.axis_index("section")}
    pairs = shares.shape[0]
    here, width = query.shape
    block = 512
    blocks = w_up.shape[1] // block
    half = width // 2

    def fetch(pair):
        slot = lax.rem(pair, 2)
        return pltpu.make_async_copy(shares.at[pair], held.at[slot], held_sem.at[slot])

    def load(index):
        source, target = (
            (keys, columns_two.at[pl.ds(0, width)]),
            (values, columns_two.at[pl.ds(width, width)]),
            (w_query, heads.at[0]),
            (w_key, heads.at[1]),
            (w_value, heads.at[2]),
            (hidden, units),
            (hidden, residuals),
            (w_skip, columns_two),
            (joined_kept, held.at[0, :, pl.ds(0, here)]),
            (joined_other, held.at[0, :, pl.ds(here, here)]),
            (w_out.at[:, pl.ds(0, half)], held.at[0]),
            (w_out.at[:, pl.ds(half, half)], held.at[1]),
        )[index]
        return pltpu.make_async_copy(source, target, load_sem.at[index])

    def load_part(index):
        return pltpu.make_async_copy(
            normed_all.at[:, pl.ds(index * half, half)], held.at[index], part_sem.at[index]
        )

    def load_block(step):
        slot = lax.rem(step, 2)
        place = pl.ds(pl.multiple_of(step * block, block), block)
        there = pl.ds(pl.multiple_of(slot * block, block), block)
        return (
            pltpu.make_async_copy(
                w_up.at[:, place], columns_two.at[pl.ds(width, width), there], block_sem.at[slot, 0]
            ),
            pltpu.make_async_copy(
                w_down.at[place], columns_two.at[there], block_sem.at[slot, 1]
            ),
        )

    def side(index):
        source, target, device = (
            (parts.at[0], parts.at[1], core),
            (parts.at[2], parts.at[3], core),
            (grad_query, query_landing, core),
            (normed_send, normed_landing, far),
            (grad_hidden, hidden_landing, core),
            (stored_send, stored_landing, section),
            (grad_low, parts.at[0, :, pl.ds(0, width)], core),
            (parts.at[1, :, pl.ds(0, width)], parts.at[0, :, pl.ds(width, width)], core),
        )[index]
        return remote(source, target, side_send.at[index], side_recv.at[index], device)

    def pair_half(index, part):
        lanes = pl.ds((1 - index) * here, here)
        return remote(
            parts.at[3, :, pl.ds((2 * index + part) * here, here)],
            lows.at[pl.ds(half + part * here, here), lanes],
            pair_send.at[index],
            pair_recv.at[index],
            core,
        )

    def pair_whole(index):
        if index == 2:
            source = target = parts.at[2]
        elif index == 3:
            source = target = heads.at[1]
        else:
            source = target = lows.at[pl.ds(half, half), pl.ds((1 - index) * here, here)]
        return remote(source, target, pair_send.at[index], pair_recv.at[index], core)

    def act_place(step, base):
        rows = pl.ds(pl.multiple_of(base + lax.rem(step, 2) * here, here), here)
        return rows, pl.ds(pl.multiple_of(lax.div(step, 2) * here, here), here)

    def act_copy(step):
        rows, lanes = act_place(step, half)
        return remote(
            parts.at[2, :, pl.ds(pl.multiple_of(step * here, here), here)],
            heads.at[2, rows, lanes],
            pair_send.at[2],
            act_recv.at[step],
            core,
        )

    def up_copy(step):
        rows = pl.ds(pl.multiple_of(lax.div(step, 2) * here, here), here)
        lanes = pl.ds(pl.multiple_of(lax.rem(step, 2) * block, block), block)
        return remote(
            heads.at[0, rows, lanes],
            heads.at[1, rows, lanes],
            pair_send.at[3],
            pair_recv.at[3],
            core,
        )

    vector_steps = [
        [core],
        [{"dp": z * 4 + flip(x, mask)} for mask in (1, 2, 3)],
        [{"dp": flip(z, mask) * 4 + x} for mask in (1, 2, 3)],
        [far],
    ]
    vector_slots = (0, 1, 4, 7)

    def vector_copies(step):
        return [
            remote(
                vectors,
                vector_landing.at[slot],
                vector_send.at[slot],
                vector_recv.at[slot],
                device,
            )
            for slot, device in enumerate(vector_steps[step], vector_slots[step])
        ]

    def vector_start(step):
        for copy in vector_copies(step):
            copy.start()

    def vector_finish(step):
        copies = vector_copies(step)
        for copy in copies:
            copy.wait()
        for index in range(len(copies)):
            vectors[...] += vector_landing[vector_slots[step] + index]
        if step < 3:
            vector_start(step + 1)

    devices = [core, far, section]
    for mask in (1, 2, 3):
        for dp in (z * 4 + flip(x, mask), flip(z, mask) * 4 + x):
            devices += [{"dp": dp}, {"dp": dp, "seq": flip(seq, 2)}]
    greet(devices)
    for index in (6, 10, 11):
        load(index).start()
    for copy in load_block(0):
        copy.start()

    def share_rows(index):
        def kept(row, value):
            lows[pl.ds(row, 16), pl.ds((1 - index) * here, here)] = value

        def sent(row, value):
            lanes = pl.ds((2 * index + row // here) * here, here)
            parts[3, pl.ds(row % here, 16), lanes] = value

        split_cores(core_index, turned, kept, sent, 16)

    turned[...] = mixed[...].T
    share_rows(0)
    load(6).wait()
    for index in range(2):
        load(10 + index).wait()
        columns = pl.ds(index * half, half)
        residuals[:, columns] += project(mixed[...], held[index])

    def norm_two_rows(index, carry):
        rows = pl.ds(pl.multiple_of(index * 32, 32), 32)
        value = residuals[rows]
        center = value - mean_rows(value)
        scale = lax.rsqrt(mean_rows(center * center) + EPS)
        center = center * scale
        units[rows] = center
        inverse_two[rows] = scale
        stored_send[rows] = (center * flat(gain_two) + flat(bias_two)).astype(jnp.bfloat16)
        grad_normed[rows] = jnp.zeros_like(value)
        return carry

    lax.fori_loop(0, here // 32, norm_two_rows, 0)
    turned[...] = stored_send[...].T
    share_rows(1)
    enter(devices)
    side(6).start()
    for index in range(2):
        pair_half(index, 0).start()
        pair_half(index, 1).start()

    def down_share(step):
        act_copy(step).wait_recv()
        rows, lanes = act_place(step, 0)
        rows_other, _ = act_place(step, half)
        value = project(heads[2, rows, lanes], grad_low[...]) + project(
            heads[2, rows_other, lanes], parts[0, :, pl.ds(0, width)]
        )
        for index in range(2):
            for quarter in range(4):
                halving.put_and_send(
                    0,
                    quarter,
                    2 * step + index,
                    value[index * 128 : index * 128 + 128, quarter * 256 : quarter * 256 + 256],
                )

    def one_block(step, carry):
        @pl.when(step + 1 < blocks)
        def _():
            for copy in load_block(step + 1):
                copy.start()

        for copy in load_block(step):
            copy.wait()
        there = pl.ds(pl.multiple_of(lax.rem(step, 2) * block, block), block)
        up_part = columns_two.at[pl.ds(width, width), there]
        down_part = columns_two.at[there]
        upward = project(stored_send[...], up_part[...])
        cdf = 0.5 * (1.0 + lax.erf(upward * 0.7071067811865476))
        act = (upward * cdf).astype(jnp.bfloat16)
        density = jnp.exp(upward * upward * -0.5) * 0.3989422804014327
        slope = cdf + upward * density
        grad_up = (back_product(grad_low[...], down_part[...]) * slope).astype(jnp.bfloat16)
        residuals[...] += project(act, down_part[...])
        grad_normed[...] += back_product(grad_up, up_part[...])
        up_rows = pl.ds(pl.multiple_of(lax.div(step, 2) * here, here), here)
        heads[0, up_rows, there] = grad_up
        up_copy(step).start()
        turned[pl.ds(0, block)] = act.T
        rows, lanes = act_place(step, 0)
        first = lax.rem(step, 2) * here
        sent_lanes = pl.ds(pl.multiple_of(step * here, here), here)

        def kept(row, value):
            heads[2, pl.ds(pl.multiple_of(first + row, 64), 64), lanes] = value

        def sent(row, value):
            parts[2, pl.ds(row, 64), sent_lanes] = value

        split_cores(core_index, turned.at[pl.ds(0, block)], kept, sent, 64)
        act_copy(step).start()

        @pl.when(step == 1)
        def _():
            side(6).wait_recv()

        @pl.when(step > 0)
        def _():
            down_share(step - 1)

        return carry

    lax.fori_loop(0, blocks, one_block, 0)
    load(0).start()
    load(1).start()

    def norm_back(ones, grads, gain, inverse):
        scaled = grads * gain
        value = scaled - mean_rows(scaled) - ones * mean_rows(scaled * ones)
        return (
            inverse * value,
            jnp.sum(grads * ones, axis=0, keepdims=True),
            jnp.sum(grads, axis=0, keepdims=True),
        )

    def norm_two_back(index, sums):
        rows = pl.ds(pl.multiple_of(index * 32, 32), 32)
        value, gain_part, bias_part = norm_back(
            units[rows], grad_normed[rows], flat(gain_two), inverse_two[rows]
        )
        output[rows] = residuals[rows].astype(jnp.bfloat16)
        value = grad_low[rows].astype(jnp.float32) + value
        residuals[rows] = value
        parts[1, rows, pl.ds(0, width)] = value.astype(jnp.bfloat16)
        return sums[0] + gain_part, sums[1] + bias_part

    nothing = jnp.zeros((1, width), jnp.float32)
    gain_sum, bias_sum = lax.fori_loop(0, here // 32, norm_two_back, (nothing, nothing))
    side(7).start()
    load(5).start()
    vectors[pl.ds(2, 1)] = gain_sum
    vectors[pl.ds(3, 1)] = bias_sum
    vectors[pl.ds(4, 4)] = jnp.zeros((4, width), jnp.float32)
    down_share(blocks - 1)
    for index in range(2):
        columns = pl.ds(index * half, half)
        part = back_product(parts[1, :, columns], held[index])
        grad_normed[...] = part if index == 0 else grad_normed[...] + part
    grad[...] = grad_normed[...].astype(jnp.bfloat16)
    fetch(0).start()
    pair_whole(1).wait_recv()
    pair_whole(3).wait_recv()
    for quarter in range(4):
        rows = pl.ds(quarter * here, here)
        halving.store(
            1,
            quarter,
            project(lows[pl.ds(0, half), pl.ds(0, here)], heads[0, rows])
            + project(lows[pl.ds(half, half), pl.ds(0, here)], heads[1, rows]),
        )
    pair_whole(3).wait_send()
    pl.semaphore_signal(free_sem.at[0], inc=1, device_id=core, device_id_type=MESH)
    pair_whole(0).wait_recv()
    side(7).wait_recv()
    for quarter in range(4):
        halving.store(
            2,
            quarter,
            project(
                lows[pl.ds(0, half), pl.ds(here, here)], parts[1, :, pl.ds(quarter * 256, 256)]
            )
            + project(
                lows[pl.ds(half, half), pl.ds(here, here)],
                parts[0, :, pl.ds(width + quarter * 256, 256)],
            ),
        )
    for index in range(3):
        pair_whole(index).wait_send()
    side(7).wait_send()
    for index in range(3, 5):
        load(index).start()
    pl.semaphore_wait(free_sem.at[0], 1)
    load(0).wait()
    load(1).wait()

    def one_pair(pair, carry):
        @pl.when(pair + 1 < pairs)
        def _():
            fetch(pair + 1).start()

        fetch(pair).wait()
        columns = pl.ds(pl.multiple_of(pair * 128, 128), 128)
        others = pl.ds(pl.multiple_of(width + pair * 128, 128), 128)
        out, grad_keys, grad_values = attention_backward_pair(
            query[:, columns],
            columns_two.at[pl.ds(0, width), columns],
            columns_two.at[pl.ds(width, width), columns],
            held.at[lax.rem(pair, 2)],
            inverses[pair],
            grad[:, columns],
            mixed[:, columns],
            lows,
        )
        grad_query[:, columns] = out
        for part in range(4):
            first = part % 2 * here
            parts[part, :, columns] = grad_keys[part // 2][first : first + here]
            parts[part, :, others] = grad_values[part // 2][first : first + here]
        for step in range(2):
            for index, place in enumerate((columns, others)):
                remote(
                    parts.at[2 * step + 1, :, place],
                    heads.at[0, pl.ds((2 * step + index) * here, here), columns],
                    swap_send,
                    swap_recv,
                    core,
                ).start()
        return carry

    lax.fori_loop(0, 3, one_pair, 0)
    halving.finish(0, 0)
    lax.fori_loop(3, pairs, one_pair, 0)
    side(2).start()
    load(7).start()
    load_part(0).start()
    load_part(1).start()
    swapped = remote(heads.at[0], heads.at[0], swap_send, swap_recv, core)
    swapped.wait()
    pl.semaphore_signal(free_sem.at[1], inc=1, device_id=core, device_id_type=MESH)
    for step in (1, 0):

        def add_rows(index, carry):
            rows = pl.ds(pl.multiple_of(index * 64, 64), 64)
            for index in range(2):
                columns = pl.ds(index * width, width)
                first = pl.multiple_of((2 * step + index) * here + rows.start, 64)
                parts[2 * step, rows, columns] = (
                    parts[2 * step, rows, columns].astype(jnp.float32)
                    + heads[0, pl.ds(first, 64)].astype(jnp.float32)
                ).astype(jnp.bfloat16)
            return carry

        lax.fori_loop(0, here // 64, add_rows, 0)
    load(2).start()
    for index in range(3, 5):
        load(index).wait()

    def from_parts(part, rows):
        return back_product(parts[part, :, pl.ds(0, width)], heads[1, rows]) + back_product(
            parts[part, :, pl.ds(width, width)], heads[2, rows]
        )

    def far_rows(index, carry):
        rows = pl.ds(pl.multiple_of(index * 256, 256), 256)
        normed_send[:, rows] = from_parts(2, rows).astype(jnp.bfloat16)
        return carry

    lax.fori_loop(0, width // 256, far_rows, 0)
    side(3).start()
    pl.semaphore_wait(free_sem.at[1], 1)
    side(0).start()
    side(1).start()
    halving.finish(1, 0)
    halving.finish(2, 0)
    halving.finish(0, 1)

    load(2).wait()

    def own_rows(index, carry):
        rows = pl.ds(pl.multiple_of(index * 256, 256), 256)
        grad_normed[:, rows] = from_parts(0, rows) + back_product(grad_query[...], heads[0, rows])
        return carry

    lax.fori_loop(0, width // 256, own_rows, 0)
    load_part(0).wait()
    load_part(1).wait()

    def select_rows(index, carry):
        first = pl.multiple_of(index * 256, 256)
        row = first + lax.broadcasted_iota(jnp.int32, (256, width), 0)
        lane = lax.broadcasted_iota(jnp.int32, (256, width), 1)
        source = lax.div(row, 16) * 32 + core_index * 16 + lax.rem(row, 16)
        pick = jnp.where(lane == source, 1.0, 0.0).astype(jnp.bfloat16)
        value = back_product(pick[:, :half], held[0]) + back_product(pick[:, half:], held[1])
        value = value.astype(jnp.bfloat16)
        lows[pl.ds(first, 256)] = value[:, :half]
        lows[pl.ds(pl.multiple_of(half + first, 256), 256)] = value[:, half:]
        return carry

    lax.fori_loop(0, half // 256, select_rows, 0)
    load(8).start()
    load(9).start()

    def rows_one(part):
        return lows[pl.ds(part // 2 * half, half), pl.ds(part % 2 * here, here)]

    side(2).wait_recv()
    for quarter in range(4):
        columns = pl.ds(quarter * 256, 256)
        halving.store(
            3,
            quarter,
            project(rows_one(0), grad_query[:, columns])
            + project(rows_one(1), query_landing[:, columns]),
        )
    side(0).wait_recv()
    side(1).wait_recv()
    for quarter in range(4):
        columns = pl.ds(quarter * 512, 512)
        halving.store(
            4,
            quarter,
            project(rows_one(0), parts[0, :, columns])
            + project(rows_one(1), parts[1, :, columns])
            + project(rows_one(2), parts[2, :, columns])
            + project(rows_one(3), parts[3, :, columns]),
        )
    halving.finish(0, 2)
    halving.finish(1, 1)
    halving.finish(2, 1)
    load(5).wait()
    side(3).wait_recv()

    def norm_rows(index, sums):
        rows = pl.ds(pl.multiple_of(index * 32, 32), 32)
        grads = grad_normed[rows] + normed_landing[rows].astype(jnp.float32)
        center = units[rows] - mean_rows(units[rows])
        scale = lax.rsqrt(mean_rows(center * center) + EPS)
        value, gain_part, bias_part = norm_back(center * scale, grads, flat(gain_one), scale)
        grad_hidden[rows] = (residuals[rows] + value).astype(jnp.bfloat16)
        return sums[0] + gain_part, sums[1] + bias_part

    gain_sum, bias_sum = lax.fori_loop(0, here // 32, norm_rows, (nothing, nothing))
    side(4).start()
    vectors[pl.ds(0, 1)] = gain_sum
    vectors[pl.ds(1, 1)] = bias_sum
    vector_start(0)
    load(7).wait()

    def stored_rows(index, carry):
        rows = pl.ds(pl.multiple_of(index * 256, 256), 256)
        below = pl.ds(pl.multiple_of(width + index * 256, 256), 256)
        stored_send[:, rows] = back_product(grad_hidden[...], columns_two[below]).astype(
            jnp.bfloat16
        )
        return carry

    lax.fori_loop(0, width // 256, stored_rows, 0)
    side(5).start()
    halving.finish(3, 0)
    halving.finish_direct(4, 0)
    vector_finish(0)
    load(8).wait()
    load(9).wait()
    side(4).wait_recv()
    for quarter in range(4):
        columns = pl.ds(quarter * 256, 256)
        halving.store(
            5,
            quarter,
            project(held[0, :, pl.ds(0, here)], grad_hidden[:, columns])
            + project(held[0, :, pl.ds(here, here)], hidden_landing[:, columns]),
        )

    def own_grads(index, carry):
        rows = pl.ds(pl.multiple_of(index * 256, 256), 256)
        grad_own[:, rows] = back_product(grad_hidden[...], columns_two[rows]).astype(jnp.bfloat16)
        return carry

    lax.fori_loop(0, width // 256, own_grads, 0)
    for job, stage in ((0, 3), (1, 2), (2, 2), (3, 1)):
        halving.finish(job, stage)
    halving.finish_direct(4, 1)
    vector_finish(1)
    halving.finish_direct(5, 0)
    for job, stage in ((3, 2), (0, 4), (1, 3), (2, 3)):
        halving.finish(job, stage)
    vector_finish(2)
    halving.finish_direct(5, 1)
    for job, stage in ((3, 3), (1, 4), (2, 4)):
        halving.finish(job, stage)
    halving.finish_direct(4, 2)
    vector_finish(3)
    halving.finish_direct(5, 2)
    halving.finish(3, 4)
    side(5).wait_recv()
    grad_stored[...] = stored_landing[...]
    halving.drain()
    for index in range(7):
        side(index).wait_send()


def backward(inputs, large, small, collective_id):
    query = inputs[0]
    keys = large[0]
    here, width = query.shape
    span = keys.shape[0]
    shapes = [(width // 16, width), (width // 64, 4 * width), (width // 64, width)]
    shapes += [(width // 64, width), (width // 64, 2 * width), (width // 32, width)]
    inside = pl.BlockSpec(memory_space=pltpu.VMEM)
    outside = pl.BlockSpec(memory_space=pl.ANY)
    result_shapes = shapes[:4] + [shapes[3], shapes[3]] + shapes[5:]
    rows_shape = (here, width)
    low_rows = pltpu.VMEM(rows_shape, jnp.bfloat16)
    full_rows = pltpu.VMEM(rows_shape, jnp.float32)
    dma = pltpu.SemaphoreType.DMA
    operands = [query, *large[:3], *inputs[1:], *large[3:], *small]
    specs = [inside] + [outside] * 3 + [inside] * 3 + [outside] * (len(large) - 3)
    specs += [inside] * len(small)
    return pl.pallas_call(
        functools.partial(backward_kernel, shapes),
        in_specs=specs,
        out_specs=[inside] * (4 + len(result_shapes)),
        out_shape=[jax.ShapeDtypeStruct(rows_shape, jnp.bfloat16)] * 3
        + [jax.ShapeDtypeStruct((8, width), jnp.float32)]
        + [jax.ShapeDtypeStruct(shape, jnp.float32) for shape in result_shapes],
        scratch_shapes=[
            pltpu.VMEM((span, 2 * here), jnp.bfloat16),
            pltpu.VMEM((2, span, 2 * here), jnp.bfloat16),
            dma((2,)),
            pltpu.VMEM((4, here, 2 * width), jnp.bfloat16),
            pltpu.SemaphoreType.REGULAR((2,)),
            dma,
            dma,
            low_rows,
            low_rows,
            dma((8,)),
            dma((8,)),
            pltpu.VMEM((2 * width, width), jnp.bfloat16),
            pltpu.VMEM((3, width, width), jnp.bfloat16),
            dma((12,)),
            full_rows,
            full_rows,
            full_rows,
            low_rows,
            low_rows,
            low_rows,
            low_rows,
            low_rows,
            low_rows,
            pltpu.VMEM((8, 8, width), jnp.float32),
            dma((8,)),
            dma((8,)),
            pltpu.VMEM((width, here), jnp.bfloat16),
            pltpu.VMEM((here, 1), jnp.float32),
            dma((2, 2)),
            dma((4,)),
            dma((4,)),
            dma((8,)),
            dma((2,)),
        ]
        + Halving.scratch(shapes),
        compiler_params=pltpu.CompilerParams(
            collective_id=collective_id,
            has_side_effects=True,
            vmem_limit_bytes=62 * 2**20,
        ),
    )(*operands)


def mean_rows(value):
    return jnp.mean(value, axis=-1, keepdims=True)


def copy_kernel(count, vectors, *refs):
    sources, targets = refs[:count], refs[count : 2 * count]
    pieces, stops = refs[2 * count : 2 * count + 4], refs[2 * count + 4 : -2]
    held, sems = refs[-2:]
    fetch = pltpu.make_async_copy(vectors, held, sems.at[0, count])
    fetch.start()
    ways = []
    for index, (source, target, stop) in enumerate(zip(sources, targets, stops)):
        ways.append(
            (
                pltpu.make_async_copy(source, stop, sems.at[0, index]),
                pltpu.make_async_copy(stop, target, sems.at[1, index]),
            )
        )
    for into, _ in ways:
        into.start()
    for into, out in ways:
        into.wait()
        out.start()
    fetch.wait()
    width = vectors.shape[1]
    size = width // 64
    shard = lax.axis_index("dp") * 4 + lax.axis_index("seq")
    turned = pltpu.roll(held[...], lax.rem(width - shard * size, width), 1)
    for index, piece in enumerate(pieces):
        piece[...] = turned[index : index + 1, :size]
    for _, out in ways:
        out.wait()


def copied(vectors, arrays):
    outside = pl.BlockSpec(memory_space=pl.ANY)
    inside = pl.BlockSpec(memory_space=pltpu.VMEM)
    piece = jax.ShapeDtypeStruct((1, vectors.shape[1] // 64), jnp.float32)
    return pl.pallas_call(
        functools.partial(copy_kernel, len(arrays)),
        in_specs=[outside] * (1 + len(arrays)),
        out_specs=[outside] * len(arrays) + [inside] * 4,
        out_shape=[jax.ShapeDtypeStruct(array.shape, array.dtype) for array in arrays]
        + [piece] * 4,
        scratch_shapes=[pltpu.VMEM(array.shape, array.dtype) for array in arrays]
        + [
            pltpu.VMEM(vectors.shape, vectors.dtype),
            pltpu.SemaphoreType.DMA((2, len(arrays) + 1)),
        ],
    )(vectors, *arrays)


def on_device(
    states,
    mirror,
    w_skip,
    norm1_gain,
    norm1_bias,
    w_query,
    w_key,
    w_value,
    w_out,
    norm2_gain,
    norm2_bias,
    w_up,
    w_down,
    out_grad,
    lengths,
    infill_spans,
):
    rows_here = states.shape[2]
    model_width = states.shape[3]
    seq = lax.axis_index("seq")
    (
        hidden,
        query,
        inverses,
        mixed_rows,
        grad_low,
        joined_mine,
        shares,
        keys_all,
        values_all,
        normed_all,
        joined_other,
    ) = forward(
        lengths,
        infill_spans.swapaxes(2, 3),
        states.reshape(rows_here, model_width),
        mirror.reshape(rows_here, model_width),
        out_grad.reshape(rows_here, model_width),
        [norm1_gain, norm1_bias],
        (w_skip, w_query, w_key, w_value),
        2,
    )
    results = backward(
        [query, inverses, mixed_rows, grad_low],
        [
            keys_all,
            values_all,
            shares,
            hidden,
            w_out,
            w_up,
            w_down,
            w_query,
            w_key,
            w_value,
            w_skip,
            normed_all,
            joined_mine,
            joined_other,
        ],
        [norm1_gain, norm2_gain, norm2_bias],
        1,
    )
    (
        output,
        grad_own,
        grad_stored,
        down_sum,
        up_sum,
        out_sum,
        query_sum,
        key_sum,
        value_sum,
        skip_sum,
        gain_one_sum,
        bias_one_sum,
        gain_two_sum,
        bias_two_sum,
    ) = copied(results[3], results[:3] + results[4:])
    return (
        output.reshape(states.shape),
        grad_own.reshape(states.shape),
        grad_stored.reshape(states.shape),
        skip_sum[None],
        gain_one_sum,
        bias_one_sum,
        query_sum[None],
        key_sum[None],
        value_sum[None],
        out_sum[None],
        gain_two_sum,
        bias_two_sum,
        up_sum[None],
        down_sum[None],
    )


def solution(mesh):
    in_specs = (
        P("section", "dp", "seq", None),
        P("section", "dp", "seq", None),
        P(),
        P(),
        P(),
        P(),
        P(),
        P(),
        P(),
        P(),
        P(),
        P(),
        P(),
        P("section", "dp", "seq", None),
        P("section", "dp", None),
        P("section", "dp", None, None),
    )
    out_specs = (
        P("section", "dp", "seq", None),
        P("section", "dp", "seq", None),
        P("section", "dp", "seq", None),
        P("section", ("dp", "seq"), None),
        P("section", ("dp", "seq")),
        P("section", ("dp", "seq")),
        P("section", ("dp", "seq"), None),
        P("section", ("dp", "seq"), None),
        P("section", ("dp", "seq"), None),
        P("section", ("dp", "seq"), None),
        P("section", ("dp", "seq")),
        P("section", ("dp", "seq")),
        P("section", ("dp", "seq"), None),
        P("section", ("dp", "seq"), None),
    )
    return jax.shard_map(
        on_device, mesh=mesh, in_specs=in_specs, out_specs=out_specs, check_vma=False
    )
```
